32 devices in a mesh: dp: 4 (over x, core), tensor: 8 (over z, y).
Axes of the slice: x: 2, y: 2, z: 4, core: 2. Of those that a mesh axis runs over, the one named last changes fastest.
Arguments:
- tokens: bfloat16 [16384, 1152], P(('dp', 'tensor')), may hold values from -6 to 6
- labels: int32 [64], P('dp'), may hold values from 0 to 999
- timesteps: int32 [64], P('dp'), may hold values from 0 to 999
- image_counts: int32 [4], P('dp'), may hold values from 4 to 16, as said below
- class_table: bfloat16 [1000, 1152], P(None, 'tensor'), may hold values from -6 to 6
- ada_weight: bfloat16 [1152, 6, 1152], P('tensor'), may hold values from -0.1875 to 0.1875
- ada_bias: bfloat16 [6, 1152], replicated, may hold values from -3 to 3
- qkv_weight: bfloat16 [1152, 3, 1152], P(None, None, 'tensor'), may hold values from -0.1875 to 0.1875
- qkv_bias: bfloat16 [3, 1152], P(None, 'tensor'), may hold values from -3 to 3
- qk_scale: bfloat16 [2, 72], replicated, may hold values from 0.25 to 1.75
- out_weight: bfloat16 [1152, 1152], P('tensor'), may hold values from -3 to 3
- gate_up_weight: bfloat16 [1152, 2, 3072], P(None, None, 'tensor'), may hold values from -0.1875 to 0.1875
- down_weight: bfloat16 [3072, 1152], P('tensor'), may hold values from -0.109375 to 0.109375
- out_grad: bfloat16 [16384, 1152], P(('dp', 'tensor')), may hold values from -6 to 6
Outputs:
- out: bfloat16 [16384, 1152], P(('dp', 'tensor'))
- tokens_grad: float32 [16384, 1152], P(('dp', 'tensor'))
- cond_grad: float32 [64, 1152], P('dp', 'tensor')
- class_table_grad: float32 [1000, 1152], P(None, 'tensor')
- ada_weight_grad: float32 [1152, 6, 1152], P('tensor')
- ada_bias_grad: float32 [6, 1152], replicated
- qkv_weight_grad: float32 [1152, 3, 1152], P(None, None, 'tensor')
- qkv_bias_grad: float32 [3, 1152], P(None, 'tensor')
- qk_scale_grad: float32 [2, 72], replicated
- out_weight_grad: float32 [1152, 1152], P('tensor')
- gate_up_grad: float32 [1152, 2, 3072], P(None, None, 'tensor')
- down_grad: float32 [3072, 1152], P('tensor')
The draws below stay inside these ranges and needn't reach their ends.
Inputs may be any that keep to these rules, and one draw needn't show every extreme that they name: `image_counts`: each entry is 16, 8 or 16 // 4 (never under 1); at least one group holds 16 images.
All inputs are finite; a program needn't handle non-finite values.
Results may differ from the reference program's by a relative error of at most 0.023.
Values may be sent and summed in bfloat16 or wider, within the bound.
A program may use at most 256 MiB of HBM per device.

```python
import math
import jax
import jax.numpy as jnp
from jax import lax

D = 1152
HEADS = 16
HD = 72
FF = 3072
NCLS = 1000
TSTEPS = 1000
GRID = 16
IMG_DEV = 16
PATCH = 256
GROUPS = 4
IMAGES = 64
ROWS = 16384
N_DP = 4


def draw_image_counts(key, part):
    key = jax.random.fold_in(key, 7)
    level_key, full_key = jax.random.split(key)
    levels = jax.random.randint(level_key, (GROUPS,), 0, 3)
    counts = jnp.where(levels == 0, IMG_DEV, jnp.where(levels == 1, IMG_DEV // 2, max(1, IMG_DEV // 4)))
    chosen = jax.random.randint(full_key, (), 0, GROUPS)
    counts = jnp.where(jnp.arange(GROUPS) == chosen, IMG_DEV, counts)
    return counts.astype(jnp.int32)


def plant(values, own_key, smallest, largest):
    longest = values.shape.index(max(values.shape))
    spots = []
    for shift in (0, 1):
        where = [jax.random.randint(jax.random.fold_in(own_key, axis), (), 0, length) for axis, length in enumerate(values.shape)]
        where[longest] = (where[longest] + shift) % values.shape[longest]
        spots.append(tuple(where))
    return values.at[spots[0]].set(smallest).at[spots[1]].set(largest)


def level_of(own_key, dims, cuts, low, high):
    def one(axis_at, blocks):
        heights = jax.random.uniform(jax.random.fold_in(jax.random.fold_in(own_key, 6), axis_at), (blocks,), jnp.float32, low / len(cuts), high / len(cuts))
        return jnp.repeat(jnp.exp(heights), dims[axis_at] // blocks).reshape((-1,) + (1,) * (len(dims) - axis_at - 1))

    loudness = one(*cuts[0])
    for cut in cuts[1:]:
        loudness = loudness * one(*cut)
    return loudness


def noise(key, extent, spread, most, pieces=(), held_as=jnp.bfloat16):
    level = level_of(key, extent, pieces, -0.22, 0.18) if pieces else 1.0
    entries = jax.random.normal(key, extent, jnp.float32) * spread * level
    return jnp.minimum(jnp.maximum(entries, -most), most).astype(held_as)


def setup_inputs(seed: int = 0) -> dict:
    arg_keys = jax.random.split(jax.random.key(seed), 15)
    tokens = noise(arg_keys[0], (ROWS, D), 1.0, 6.0, ((0, 32),))
    labels = plant(jax.random.randint(arg_keys[1], (IMAGES,), 0, NCLS), jax.random.fold_in(arg_keys[1], 1), 0, NCLS - 1).astype(jnp.int32)
    timesteps = plant(jax.random.randint(arg_keys[2], (IMAGES,), 0, TSTEPS), jax.random.fold_in(arg_keys[2], 1), 0, TSTEPS - 1).astype(jnp.int32)
    image_counts = draw_image_counts(jax.random.fold_in(arg_keys[14], 71), 0)
    class_table = noise(arg_keys[4], (NCLS, D), 1.0, 6.0, ((1, 8),))
    ada_weight = noise(arg_keys[5], (D, 6, D), D ** -0.5, 0.1875, ((0, 8),))
    ada_bias = noise(arg_keys[6], (6, D), 0.5, 3.0)
    qkv_weight = noise(arg_keys[7], (D, 3, D), D ** -0.5, 0.1875, ((2, 8),))
    qkv_bias = noise(arg_keys[8], (3, D), 0.5, 3.0, ((1, 8),))
    qk_scale = jnp.clip(1.0 + 0.15 * jax.random.normal(arg_keys[9], (2, HD), jnp.float32), 0.25, 1.75).astype(jnp.bfloat16)
    out_weight = noise(arg_keys[10], (D, D), (D // PATCH) ** -0.5, 3.0, ((0, 8),))
    gate_up_weight = noise(arg_keys[11], (D, 2, FF), D ** -0.5, 0.1875, ((2, 8),))
    down_weight = noise(arg_keys[12], (FF, D), FF ** -0.5, 0.109375, ((0, 8),))
    out_grad = noise(arg_keys[13], (ROWS, D), 1.0, 6.0, ((0, 32),))
    return dict(tokens=tokens, labels=labels, timesteps=timesteps, image_counts=image_counts, class_table=class_table, ada_weight=ada_weight, ada_bias=ada_bias, qkv_weight=qkv_weight, qkv_bias=qkv_bias, qk_scale=qk_scale, out_weight=out_weight, gate_up_weight=gate_up_weight, down_weight=down_weight, out_grad=out_grad)


@jax.custom_vjp
def low(v):
    return lax.optimization_barrier(v.astype(jnp.bfloat16)).astype(jnp.float32)

@jax.custom_vjp
def low_back(v):
    return v

def low_keep(v):
    return (low(v), None)

def low_pass(kept, grad):
    return (grad,)

def back_keep(v):
    return (v, None)

def back_low(kept, grad):
    return (low(grad),)
low.defvjp(low_keep, low_pass)
low_back.defvjp(back_keep, back_low)
HIGH = lax.Precision.HIGHEST
epsilon = 1e-06

def root_norm(v):
    return v * lax.rsqrt(lax.optimization_barrier(jnp.mean(v * v, axis=-1, keepdims=True)) + epsilon)

def rope_tables(count):
    pairs = HD // 4
    theta = jnp.exp(-math.log(100.0) * jnp.arange(pairs, dtype=jnp.float32) / pairs)
    place = jnp.arange(count) % PATCH
    row_angle = (place // GRID).astype(jnp.float32)[:, None] * theta
    col_angle = (place % GRID).astype(jnp.float32)[:, None] * theta
    return ((jnp.cos(row_angle), jnp.sin(row_angle)), (jnp.cos(col_angle), jnp.sin(col_angle)))

def rotate_part(segment, cosine, sine):
    half_len = segment.shape[-1] // 2
    first, second = (segment[..., :half_len], segment[..., half_len:])
    cosine = cosine[:, None, :]
    sine = sine[:, None, :]
    return jnp.concatenate([first * cosine - second * sine, second * cosine + first * sine], axis=-1)

def rotate(vectors, tables):
    half_len = vectors.shape[-1] // 2
    return jnp.concatenate([rotate_part(vectors[..., :half_len], tables[0][0], tables[0][1]), rotate_part(vectors[..., half_len:], tables[1][0], tables[1][1])], axis=-1)

def time_embedding(steps):
    columns = jnp.arange(D)
    half_width = D // 2
    frequency = jnp.exp(-math.log(10000.0) * (columns % half_width).astype(jnp.float32) / half_width)
    angles = steps.astype(jnp.float32)[:, None] * frequency[None, :]
    return jnp.where(columns[None, :] < half_width, jnp.cos(angles), jnp.sin(angles))

def reference(tokens, labels, timesteps, image_counts, class_table, ada_weight, ada_bias, qkv_weight, qkv_bias, qk_scale, out_weight, gate_up_weight, down_weight, out_grad):
    count_rows = IMG_DEV * PATCH
    tables = rope_tables(count_rows)
    factor = HD ** (-0.5)
    local_image = jnp.arange(IMAGES) % IMG_DEV
    kept_images = (local_image < jnp.repeat(image_counts, IMG_DEV)).astype(jnp.float32)
    time_embed = time_embedding(timesteps)

    def embed(table):
        return jnp.take(table, labels, axis=0) + time_embed

    def forward(tokens_f, condition, ada_w, ada_b, qkv_w, qkv_b, gains, out_w, gate_up_w, down_w):
        cond_act = low(jax.nn.silu(condition))
        modulation = low_back(jnp.einsum('id,dkc->ikc', cond_act, ada_w, precision=HIGH) + ada_b)

        def one_group(items):
            group_tokens, group_mod, group_kept = items
            parts = [group_mod[:, index][:, None, :] for index in range(6)]
            shift_one, scale_one, gate_one, shift_two, scale_two, gate_two = parts
            kept = group_kept[:, None, None]
            first_in = low(root_norm(group_tokens) * (1.0 + scale_one) + shift_one).reshape(count_rows, D)
            qkv = low_back(jnp.einsum('nd,dkc->nkc', first_in, qkv_w, precision=HIGH) + qkv_b)
            head_view = qkv.reshape(count_rows, 3, HEADS, HD)
            queries = low(rotate(root_norm(head_view[:, 0]) * gains[0], tables))
            keys_rot = low(rotate(root_norm(head_view[:, 1]) * gains[1], tables))
            values = low(head_view[:, 2])
            block_shape = (IMG_DEV, PATCH, HEADS, HD)
            scores = low_back(jnp.einsum('iqhe,ikhe->ihqk', queries.reshape(block_shape), keys_rot.reshape(block_shape), precision=HIGH) * factor)
            probability = low(jax.nn.softmax(scores, axis=-1))
            mixed = jnp.einsum('ihqk,ikhe->iqhe', probability, values.reshape(block_shape), precision=HIGH)
            mixed_heads = low(low_back(mixed.reshape(count_rows, D)))
            attention = low_back(jnp.dot(mixed_heads, out_w, precision=HIGH)).reshape(IMG_DEV, PATCH, D)
            after_attn = group_tokens + kept * gate_one * attention
            second_in = low(root_norm(after_attn) * (1.0 + scale_two) + shift_two).reshape(count_rows, D)
            gate_up = low_back(jnp.einsum('nd,dkf->nkf', second_in, gate_up_w, precision=HIGH))
            hidden = low(jax.nn.silu(gate_up[:, 0]) * gate_up[:, 1])
            feed = low_back(jnp.dot(hidden, down_w, precision=HIGH)).reshape(IMG_DEV, PATCH, D)
            return after_attn + kept * gate_two * feed
        items = (tokens_f.reshape(N_DP, IMG_DEV, PATCH, D), modulation.reshape(N_DP, IMG_DEV, 6, D), kept_images.reshape(N_DP, IMG_DEV))
        result = lax.map(jax.checkpoint(one_group), items)
        return result.reshape(ROWS, D)
    table_f = class_table.astype(jnp.float32)
    condition, embed_back = jax.vjp(embed, table_f)
    floats = [a.astype(jnp.float32) for a in (tokens, ada_weight, ada_bias, qkv_weight, qkv_bias, qk_scale, out_weight, gate_up_weight, down_weight)]
    result, backward = jax.vjp(forward, floats[0], condition, *floats[1:])
    grads = backward(out_grad.astype(jnp.float32))
    table_grad, = embed_back(grads[1])
    return (result.astype(jnp.bfloat16), grads[0], grads[1], table_grad, grads[2], grads[3], grads[4], grads[5], grads[6], grads[7], grads[8], grads[9])
```

```python
import math

import jax
import jax.numpy as jnp
import numpy as np
from jax import lax
from jax.experimental import pallas as pl
from jax.experimental.pallas import tpu as pltpu
from jax.sharding import PartitionSpec as P

HD = 72
GRID = 16
PATCH = 256
HIGH = lax.Precision.HIGHEST
MESH = pl.DeviceIdType.MESH
epsilon = 1e-06

HEAD = 80
HALF = 40
SHARD_FF = 192
A_ROWS = 4 * HEAD
B_ROWS = 2 * SHARD_FF
C_ROWS = SHARD_FF
ROWS_ALL = A_ROWS + B_ROWS + C_ROWS
D = 1152

G_STAGE, G_LONE = 128, 48
R_STAGE, R_LONE = 64, 16
G_STAGES = ROWS_ALL // G_STAGE
R_STAGES = ROWS_ALL // R_STAGE
PAY = 16


def place():
    d = lax.axis_index("dp")
    t = lax.axis_index("tensor")
    return d // 2, d % 2, t // 2, t % 2


def at(x, c, z, y):
    return (x * 2 + c, z * 2 + y)


def greet(targets):
    barrier = pltpu.get_barrier_semaphore()
    for o in targets:
        pl.semaphore_signal(barrier, inc=1, device_id=o, device_id_type=MESH)
    pl.semaphore_wait(barrier, len(targets))


def rows_at(first, size):
    return pl.ds(pl.multiple_of(first, 16), size)


def nt(a, b):
    return lax.dot_general(a, b, (((1,), (1,)), ((), ())), preferred_element_type=jnp.float32)


def tn(a, b):
    return lax.dot_general(a, b, (((0,), (0,)), ((), ())), preferred_element_type=jnp.float32)


def nn(a, b):
    return lax.dot_general(a, b, (((1,), (0,)), ((), ())), preferred_element_type=jnp.float32)


def low(v):
    return v.astype(jnp.bfloat16)


def wide(v):
    return v.astype(jnp.float32)


def turn(v, cos, sin):
    a, b = v[:HALF], v[HALF:]
    return jnp.concatenate([a * cos - b * sin, b * cos + a * sin], axis=0)


def remote(src, dst, ss, rs, to):
    return pltpu.make_async_remote_copy(
        src_ref=src, dst_ref=dst, send_sem=ss, recv_sem=rs, device_id=to, device_id_type=MESH)


CHUNK = 64
FACTOR = HD ** (-0.5)


def forward_kernel(
    own, mod_in, cond_in, tokens, out_grad, ada, keep, gains, table,
    full, cond_out, mod_out, fi_out, si_out, fg_out, att_out, qkv_out, norm_out, stat_out, mixed_out, gu_out, hid_out,
    mod_all, mod, fi, si, fg, att, att_send, att_recv, wa, ow, mixed, qkv, norm, stat, wb, gu, hid,
    send, recv, ms, mr, cs, cr, es, er, ls, qs, hs, ws, save,
):
    x, c, z, y = place()
    t = z * 2 + y
    d = x * 2 + c
    peers = [lax.rem(t + k, 8) for k in range(1, 8)]
    groups = [lax.rem(d + k, 4) for k in range(1, 4)]
    greet([(d, p) for p in peers] + [(g, t) for g in groups])
    y_side, x_side, core = at(x, c, z, 1 - y), at(1 - x, c, z, y), at(x, 1 - c, z, y)
    up, down = at(x, c, z + 1, y), at(x, c, z - 1, y)
    small = []
    for k, p in enumerate(peers):
        small.append(remote(mod_in.at[p], mod_all.at[t], ms.at[k], mr.at[t], (d, p)))
    for k, g in enumerate(groups):
        small.append(remote(cond_in, cond_out.at[d], cs.at[k], cr.at[d], (g, t)))
    for cp in small:
        cp.start()
    kept = [
        pltpu.make_async_copy(own, full.at[t], ls.at[0]),
        pltpu.make_async_copy(mod_in.at[t], mod_all.at[t], ls.at[1]),
        pltpu.make_async_copy(cond_in, cond_out.at[d], ls.at[2]),
    ]
    for cp in kept:
        cp.start()

    def plane(g):
        return rows_at(g * G_STAGE + x * G_LONE, G_STAGE - G_LONE)

    def lone(g, side):
        return rows_at(g * G_STAGE + side * (G_STAGE - G_LONE), G_LONE)

    def copy(g, kind, src, slot, rows, path, to):
        return remote(src.at[rows], full.at[slot, rows], send.at[g, kind], recv.at[g, slot, path], to)

    def arrived(g, slot, rows, path):
        copy(g, 0, own, slot, rows, path, x_side).wait_recv()

    def issue(g):
        copy(g, 2, own, t, plane(g), 0, y_side).start()
        pl.when(z < 3)(lambda: copy(g, 0, own, t, plane(g), 0, up).start())
        pl.when(z > 0)(lambda: copy(g, 1, own, t, plane(g), 0, down).start())

    def along_z(g, j):
        def below():
            slot = (z - j) * 2 + y
            arrived(g, slot, plane(g), 0)
            pl.when(z < 3)(lambda: copy(g, 1 + 2 * j, full.at[slot], slot, plane(g), 0, up).start())
            copy(g, 8 + j, full.at[slot], slot, plane(g), 0, y_side).start()
            copy(g, 11 + j, full.at[slot], slot, lone(g, x), 1, x_side).start()

        def above():
            slot = (z + j) * 2 + y
            arrived(g, slot, plane(g), 0)
            pl.when(z > 0)(lambda: copy(g, 2 + 2 * j, full.at[slot], slot, plane(g), 0, down).start())
            copy(g, 14 + j, full.at[slot], slot, plane(g), 0, y_side).start()
            copy(g, 17 + j, full.at[slot], slot, lone(g, x), 1, x_side).start()

        pl.when(z >= j)(below)
        pl.when(z + j <= 3)(above)

    def along_y(g, zz):
        slot = zz * 2 + 1 - y
        arrived(g, slot, plane(g), 0)
        copy(g, 21 + zz, full.at[slot], slot, lone(g, x), 1, x_side).start()

    def service(i):
        def on(g, act):
            pl.when(jnp.logical_and(g >= 0, g < G_STAGES))(lambda: act(g))

        on(i, issue)
        for j in (1, 2, 3):
            on(i - j, lambda g: along_z(g, j))
        on(i - 1, lambda g: along_y(g, z))
        for j in (1, 2, 3):
            @pl.when(z >= j)
            def _():
                on(i - j - 1, lambda g: along_y(g, z - j))

            @pl.when(z + j <= 3)
            def _():
                on(i - j - 1, lambda g: along_y(g, z + j))

    def lone_in(first, last):
        @pl.loop(first, last)
        def _(g):
            for k in range(1, 8):
                arrived(g, lax.rem(t + k, 8), lone(g, 1 - x), 1)

    def mod_row(image, k):
        return mod[pl.ds(image * 8 + k, 1), :]

    def by_rows(act):
        for image in range(2):
            @pl.loop(0, PATCH // CHUNK)
            def _(i):
                act(image, rows_at(image * PATCH + i * CHUNK, CHUNK))

    service(0)

    for k, p in enumerate(peers):
        remote(mod_in.at[p], mod_all.at[p], ms.at[0], mr.at[p], (d, p)).wait_recv()
    kept[1].wait()
    total = ada[...]
    for s in range(8):
        total = total + wide(mod_all[s])
    mod[...] = total * keep[...]

    def first_rows(image, rows):
        v = wide(tokens[rows, :])
        n = v * lax.rsqrt(jnp.mean(v * v, axis=-1, keepdims=True) + epsilon)
        fi[0, rows, :] = low(n * (1.0 + mod_row(image, 1)) + mod_row(image, 0))

    by_rows(first_rows)
    share_fi = remote(fi.at[0], fi.at[1], es.at[0], er.at[0], core)
    share_fi.start()
    service(1)

    def feed_rows(image, rows):
        fg[0, rows, :] = low(wide(out_grad[rows, :]) * mod_row(image, 5))

    by_rows(feed_rows)
    share_fg = remote(fg.at[0], fg.at[1], es.at[1], er.at[1], core)
    share_fg.start()

    @pl.loop(2, 7)
    def _(i):
        service(i)

    kept[0].wait()
    lone_in(0, 3)
    share_fi.wait_recv()
    share_fg.wait_recv()
    saves = [
        pltpu.make_async_copy(fi, fi_out, save.at[0]),
        pltpu.make_async_copy(fg, fg_out, save.at[1]),
        pltpu.make_async_copy(mod, mod_out, save.at[2]),
    ]
    for cp in saves:
        cp.start()

    def load_a(s):
        return pltpu.make_async_copy(full.at[s, pl.ds(0, 3 * HEAD)], wa.at[lax.rem(s, 2)], ws.at[lax.rem(s, 2)])

    load_o = pltpu.make_async_copy(full.at[:, pl.ds(3 * HEAD, HEAD)], ow, ls.at[3])
    load_o.start()
    load_a(0).start()

    def save_head(s):
        b = lax.rem(s, 2)
        return [
            pltpu.make_async_copy(qkv.at[b], qkv_out.at[s], qs.at[b, 0]),
            pltpu.make_async_copy(norm.at[b], norm_out.at[s], qs.at[b, 1]),
            pltpu.make_async_copy(stat.at[b], stat_out.at[s], qs.at[b, 2]),
        ]

    @pl.loop(0, 8)
    def _(s):
        b = lax.rem(s, 2)
        load_a(s).wait()
        pl.when(s < 7)(lambda: load_a(s + 1).start())

        @pl.when(s > 1)
        def _():
            for cp in save_head(s - 2):
                cp.wait()

        bias_row = wide(mod_all[s, 6:7, :512])
        bias_row = jnp.where(c == 0, bias_row[:, :256], bias_row[:, 256:])
        bias = jnp.transpose(jnp.broadcast_to(bias_row, (128, 256)))[: 3 * HEAD, :1]
        cos, sin = table[:HALF, :], table[HALF:, :]
        for h in range(2):
            raw = nt(wa[b], fi[h]) + bias
            turned = []
            for i in range(2):
                v = raw[i * HEAD : (i + 1) * HEAD]
                inv = lax.rsqrt(jnp.sum(v * v, axis=0, keepdims=True) * (1.0 / HD) + epsilon)
                n = v * inv
                norm[b, h, i * HEAD : (i + 1) * HEAD, :] = low(n)
                stat[b, h, i : i + 1, :] = inv
                turned.append(low(turn(n * gains[i * HEAD : (i + 1) * HEAD, :1], cos, sin)))
            q, k = turned
            v = low(raw[2 * HEAD :])
            qkv[b, h, :HEAD, :] = q
            qkv[b, h, HEAD : 2 * HEAD, :] = k
            qkv[b, h, 2 * HEAD :, :] = v
            for image in range(2):
                cut = slice(image * PATCH, (image + 1) * PATCH)
                e = jnp.exp(tn(k[:, cut], q[:, cut]) * FACTOR)
                row_sum = jnp.sum(e, axis=0, keepdims=True)
                stat[b, h, 2:3, cut] = jnp.log(row_sum)
                p = low(e * (1.0 / row_sum))
                mixed[h, pl.ds(pl.multiple_of(s * HEAD, 16), HEAD), cut] = low(nn(v[:, cut], p))
        for cp in save_head(s):
            cp.start()

        @pl.when(lax.rem(s, 4) == 3)
        def _():
            service(7 + s // 4)

    for s in (6, 7):
        for cp in save_head(s):
            cp.wait()
    load_o.wait()
    saves.append(pltpu.make_async_copy(mixed, mixed_out, save.at[3]))
    saves[-1].start()

    for image in range(2):
        cut = slice(image * PATCH, (image + 1) * PATCH)
        att_send[cut, :] = low(tn(mixed[1, :, cut], ow[...].reshape(8 * HEAD, D)))
    share_att = remote(att_send, att_recv, es.at[2], er.at[2], core)
    share_att.start()
    for image in range(2):
        cut = slice(image * PATCH, (image + 1) * PATCH)
        att[cut, :] = tn(mixed[0, :, cut], ow[...].reshape(8 * HEAD, D))
    share_att.wait_recv()

    def second_rows(image, rows):
        a = att[rows, :] + wide(att_recv[rows, :])
        att[rows, :] = a
        v = wide(tokens[rows, :]) + mod_row(image, 2) * a
        n = v * lax.rsqrt(jnp.mean(v * v, axis=-1, keepdims=True) + epsilon)
        si[0, rows, :] = low(n * (1.0 + mod_row(image, 4)) + mod_row(image, 3))

    by_rows(second_rows)
    share_si = remote(si.at[0], si.at[1], es.at[3], er.at[3], core)
    share_si.start()
    service(9)
    lone_in(3, 6)
    share_si.wait_recv()
    saves += [
        pltpu.make_async_copy(att, att_out, save.at[4]),
        pltpu.make_async_copy(si, si_out, save.at[5]),
    ]
    saves[-2].start()
    saves[-1].start()

    def load_b(s):
        return pltpu.make_async_copy(full.at[s, pl.ds(A_ROWS, B_ROWS)], wb.at[lax.rem(s, 2)], ws.at[2 + lax.rem(s, 2)])

    def save_shard(s):
        b = lax.rem(s, 2)
        return [
            pltpu.make_async_copy(gu.at[b], gu_out.at[s], hs.at[b, 0]),
            pltpu.make_async_copy(hid.at[b], hid_out.at[s], hs.at[b, 1]),
        ]

    load_b(0).start()

    @pl.loop(0, 8)
    def _(s):
        b = lax.rem(s, 2)
        load_b(s).wait()
        pl.when(s < 7)(lambda: load_b(s + 1).start())

        @pl.when(s > 1)
        def _():
            for cp in save_shard(s - 2):
                cp.wait()

        for h in range(2):
            both = nt(wb[b], si[h])
            g, u = both[:SHARD_FF], both[SHARD_FF:]
            gu[b, h] = low(both)
            hid[b, h] = low(g * (1.0 / (1.0 + jnp.exp(-g))) * u)
        for cp in save_shard(s):
            cp.start()

        pl.when(s == 3)(lambda: service(10))

    lone_in(6, 7)
    for s in (6, 7):
        for cp in save_shard(s):
            cp.wait()

    @pl.loop(0, G_STAGES)
    def _(g):
        def sent(kind, rows):
            copy(g, kind, own, t, rows, 0, x_side).wait_send()

        sent(2, plane(g))
        pl.when(z < 3)(lambda: sent(0, plane(g)))
        pl.when(z > 0)(lambda: sent(1, plane(g)))
        for k in range(4):
            sent(21 + k, lone(g, x))
        for j in (1, 2, 3):
            @pl.when(z >= j)
            def _():
                pl.when(z < 3)(lambda: sent(1 + 2 * j, plane(g)))
                sent(8 + j, plane(g))
                sent(11 + j, lone(g, x))

            @pl.when(z + j <= 3)
            def _():
                pl.when(z > 0)(lambda: sent(2 + 2 * j, plane(g)))
                sent(14 + j, plane(g))
                sent(17 + j, lone(g, x))

    for cp in small + [share_fi, share_fg, share_att, share_si]:
        cp.wait_send()
    for g in groups:
        remote(cond_in, cond_out.at[g], cs.at[0], cr.at[g], (g, t)).wait_recv()
    kept[2].wait()
    for cp in saves:
        cp.wait()


def forward(own, mod_in, cond_in, tokens, out_grad, ada, keep, gains, table):
    dma = pltpu.SemaphoreType.DMA
    vm = pltpu.VMEM
    bf, f32 = jnp.bfloat16, jnp.float32
    anywhere = pl.BlockSpec(memory_space=pl.ANY)
    inside = pl.BlockSpec(memory_space=pltpu.VMEM)
    R = tokens.shape[0]
    outs = [
        ((8, ROWS_ALL, D), bf), ((4,) + cond_in.shape, f32), ((16, D), f32),
        ((2, R, D), bf), ((2, R, D), bf), ((2, R, D), bf), ((R, D), f32),
        ((8, 2, 3 * HEAD, R), bf), ((8, 2, 2 * HEAD, R), bf), ((8, 2, 8, R), f32), ((2, 8 * HEAD, R), bf),
        ((8, 2, B_ROWS, R), bf), ((8, 2, SHARD_FF, R), bf),
    ]
    return pl.pallas_call(
        forward_kernel,
        out_shape=tuple(jax.ShapeDtypeStruct(s, e) for s, e in outs),
        in_specs=[anywhere] * 3 + [inside] * 6,
        out_specs=(anywhere,) * len(outs),
        scratch_shapes=[
            vm((8, 16, D), bf), vm((16, D), f32),
            vm((2, R, D), bf), vm((2, R, D), bf), vm((2, R, D), bf), vm((R, D), f32), vm((R, D), bf), vm((R, D), bf),
            vm((2, 3 * HEAD, D), bf), vm((8, HEAD, D), bf), vm((2, 8 * HEAD, R), bf),
            vm((2, 2, 3 * HEAD, R), bf), vm((2, 2, 2 * HEAD, R), bf), vm((2, 2, 8, R), f32),
            vm((2, B_ROWS, D), bf), vm((2, 2, B_ROWS, R), bf), vm((2, 2, SHARD_FF, R), bf),
            dma((G_STAGES, 25)), dma((G_STAGES, 8, 2)), dma((7,)), dma((8,)), dma((3,)), dma((4,)),
            dma((4,)), dma((4,)), dma((4,)), dma((2, 3)), dma((2, 2)), dma((4,)), dma((6,)),
        ],
        compiler_params=pltpu.CompilerParams(
            collective_id=0, has_side_effects=True, vmem_limit_bytes=60 * 2**20),
        name="forward",
    )(own, mod_in, cond_in, tokens, out_grad, ada, keep, gains, table)


def reduce_kernel(part_in, pay, out, pay_all, part, xin, yin, zin, fin, xs, xr, ys, yr, zs, zr, fs, fr, ps, pr, ls):
    x, c, z, y = place()
    t = z * 2 + y
    me = (x * 2 + c) * 8 + t
    targets = [lax.rem(me + k, 32) for k in range(1, 32)]
    greet([(o // 8, o % 8) for o in targets])
    load = pltpu.make_async_copy(part_in, part, ls.at[0])
    load.start()
    keep = pltpu.make_async_copy(pay, pay_all.at[me], ls.at[1])
    keep.start()

    def pay_copy(k):
        o = lax.rem(me + k, 32)
        return pltpu.make_async_remote_copy(
            src_ref=pay, dst_ref=pay_all.at[me], send_sem=ps.at[k], recv_sem=pr.at[k],
            device_id=(o // 8, o % 8), device_id_type=MESH)

    @pl.loop(1, 32)
    def _(k):
        pay_copy(k).start()

    y_side, x_side, core = at(x, c, z, 1 - y), at(1 - x, c, z, y), at(x, 1 - c, z, y)
    up, down = at(x, c, z + 1, y), at(x, c, z - 1, y)
    keep.wait()
    load.wait()

    def lone(g, side):
        return g * R_STAGE + side * (R_STAGE - R_LONE)

    def plane(g):
        return g * R_STAGE + x * R_LONE

    PL = R_STAGE - R_LONE
    MID = R_STAGE - 2 * R_LONE

    def xcopy(g, side):
        yy = 1 - y if side == 0 else y
        return remote(
            part.at[:, yy, rows_at(lone(g, 1 - x), R_LONE)], xin.at[:, yy, rows_at(g * R_LONE, R_LONE)],
            xs.at[g, side], xr.at[g, side], x_side)

    def ycopy(g):
        return remote(
            part.at[:, 1 - y, rows_at(plane(g), PL)], yin.at[:, rows_at(g * PL, PL)],
            ys.at[g], yr.at[g], y_side)

    def zcopy(g, to_z, way):
        return remote(
            part.at[to_z, y, rows_at(plane(g), PL)], zin.at[way, to_z, rows_at(g * PL, PL)],
            zs.at[g, way, to_z], zr.at[g, way, to_z], up if way == 0 else down)

    def fcopy(g, what):
        if what == 0:
            rows = rows_at(lone(g, x), R_LONE)
            return remote(out.at[c, rows], out.at[c, rows], fs.at[g, 0], fr.at[g, 0], x_side)
        rows = rows_at(g * R_STAGE + R_LONE, MID)
        return remote(part.at[z, y, rows], fin.at[rows], fs.at[g, 1], fr.at[g, 1], x_side)

    def add(zz, yy, first, rows, piece):
        @pl.loop(0, rows // 16)
        def _(i):
            a = rows_at(first + i * 16, 16)
            part[zz, yy, a, :] = (
                part[zz, yy, a, :].astype(jnp.float32) + piece(i).astype(jnp.float32)).astype(jnp.bfloat16)

    def x_stage(g, side):
        yy = 1 - y if side == 0 else y
        xcopy(g, side).wait_recv()

        @pl.loop(0, 4)
        def _(k):
            add(k, yy, lone(g, x), R_LONE, lambda r: xin[k, yy, rows_at(g * R_LONE + r * 16, 16), :])

        if side == 0:
            ycopy(g).start()

    def y_stage(g):
        ycopy(g).wait_recv()

        @pl.loop(0, 4)
        def _(k):
            add(k, y, plane(g), PL, lambda r: yin[k, rows_at(g * PL + r * 16, 16), :])

    def take(g, way, to_z):
        zcopy(g, to_z, way).wait_recv()
        add(to_z, y, plane(g), PL, lambda r: zin[way, to_z, rows_at(g * PL + r * 16, 16), :])

    def up_stage(g):
        for j in (3, 2, 1):
            @pl.when(z + j <= 3)
            def _():
                pl.when(z > 0)(lambda: take(g, 0, z + j))
                zcopy(g, z + j, 0).start()

    def down_stage(g):
        for j in (3, 2, 1):
            @pl.when(z >= j)
            def _():
                pl.when(z < 3)(lambda: take(g, 1, z - j))
                zcopy(g, z - j, 1).start()

    def own_stage(g):
        pl.when(z > 0)(lambda: take(g, 0, z))
        pl.when(z < 3)(lambda: take(g, 1, z))
        rows = lone(g, x)
        out[c, rows_at(rows, R_LONE), :] = part[z, y, rows_at(rows, R_LONE), :]
        fcopy(g, 0).start()
        fcopy(g, 1).start()

    def f_stage(g):
        fcopy(g, 0).wait_recv()
        fcopy(g, 1).wait_recv()
        first = g * R_STAGE + R_LONE

        @pl.loop(0, MID // 16)
        def _(i):
            a = rows_at(first + i * 16, 16)
            out[c, a, :] = (part[z, y, a, :].astype(jnp.float32) + fin[a, :].astype(jnp.float32)).astype(jnp.bfloat16)

        rows = rows_at(g * R_STAGE, R_STAGE)
        remote(out.at[c, rows], out.at[c, rows], fs.at[g, 2], fr.at[g, 2], core).start()

    def x_send(g):
        xcopy(g, 0).start()
        xcopy(g, 1).start()

    x_send(0)
    x_send(1)

    def service(i):
        def on(g, act):
            pl.when(jnp.logical_and(g >= 0, g < R_STAGES))(lambda: act(g))

        on(i, lambda g: x_stage(g, 0))
        on(i, lambda g: x_stage(g, 1))
        on(i + 2, x_send)
        on(i - 1, y_stage)
        on(i - 1 - z, up_stage)
        on(i - 4 + z, down_stage)
        on(i - 4, own_stage)
        on(i - 5, f_stage)

    @pl.loop(0, R_STAGES + 5)
    def _(i):
        service(i)

    @pl.loop(0, R_STAGES)
    def _(g):
        xcopy(g, 0).wait_send()
        xcopy(g, 1).wait_send()
        ycopy(g).wait_send()

        for j in (3, 2, 1):
            pl.when(z + j <= 3)(lambda: zcopy(g, z + j, 0).wait_send())
            pl.when(z >= j)(lambda: zcopy(g, z - j, 1).wait_send())
        fcopy(g, 0).wait_send()
        fcopy(g, 1).wait_send()
        rows = rows_at(g * R_STAGE, R_STAGE)
        mine = remote(out.at[c, rows], out.at[c, rows], fs.at[g, 2], fr.at[g, 2], core)
        mine.wait_send()
        remote(out.at[c, rows], out.at[1 - c, rows], fs.at[g, 2], fr.at[g, 2], core).wait_recv()

    @pl.loop(1, 32)
    def _(k):
        pay_copy(k).wait()


def reduce_grads(part, pay):
    vm = pltpu.VMEM
    dma = pltpu.SemaphoreType.DMA
    PL = R_STAGE - R_LONE
    anywhere = pl.BlockSpec(memory_space=pl.ANY)
    return pl.pallas_call(
        reduce_kernel,
        out_shape=(
            jax.ShapeDtypeStruct((2, ROWS_ALL, D), jnp.bfloat16),
            jax.ShapeDtypeStruct((32, PAY, D), jnp.bfloat16),
        ),
        in_specs=[anywhere, anywhere],
        out_specs=(pl.BlockSpec(memory_space=pltpu.VMEM), anywhere),
        scratch_shapes=[
            vm((4, 2, ROWS_ALL, D), jnp.bfloat16),
            vm((4, 2, R_STAGES * R_LONE, D), jnp.bfloat16),
            vm((4, R_STAGES * PL, D), jnp.bfloat16),
            vm((2, 4, R_STAGES * PL, D), jnp.bfloat16),
            vm((ROWS_ALL, D), jnp.bfloat16),
            dma((R_STAGES, 2)), dma((R_STAGES, 2)), dma((R_STAGES,)), dma((R_STAGES,)),
            dma((R_STAGES, 2, 4)), dma((R_STAGES, 2, 4)), dma((R_STAGES, 3)), dma((R_STAGES, 3)),
            dma((32,)), dma((32,)), dma((2,)),
        ],
        compiler_params=pltpu.CompilerParams(
            collective_id=1, has_side_effects=True, vmem_limit_bytes=60 * 2**20),
        name="reduce_grads",
    )(part.reshape(4, 2, ROWS_ALL, D), pay)


def normalize(vectors, axis=-1, count=None):
    count = count or vectors.shape[axis]
    inverse = lax.rsqrt(jnp.sum(vectors * vectors, axis=axis, keepdims=True) / count + epsilon)
    return (vectors * inverse, inverse)


def normalize_back(grad, normed, inverse, axis=-1, count=None):
    count = count or grad.shape[axis]
    return inverse * (grad - normed * (jnp.sum(grad * normed, axis=axis, keepdims=True) / count))


def silu_slope(values):
    sigma = jax.nn.sigmoid(values)
    return sigma * (1.0 + values * (1.0 - sigma))


def pair_rows(heads):
    lead, n = heads.shape[:-2], heads.shape[-1]
    split = heads.reshape(lead + (2, 2, 18, n))
    split = jnp.swapaxes(split, -4, -3).reshape(lead + (2, 36, n))
    return jnp.pad(split, [(0, 0)] * len(lead) + [(0, 0), (0, 4), (0, 0)]).reshape(lead + (HEAD, n))


def unpair_rows(rows):
    lead, n = rows.shape[:-2], rows.shape[-1]
    split = rows.reshape(lead + (2, HALF, n))[..., :36, :].reshape(lead + (2, 2, 18, n))
    return jnp.swapaxes(split, -4, -3).reshape(lead + (HD, n))


def pad_rows(rows):
    return jnp.pad(rows, [(0, 0)] * (rows.ndim - 2) + [(0, 8), (0, 0)])


def pair_tables():
    pairs = HD // 4
    theta = np.exp(-math.log(100.0) * np.arange(pairs, dtype=np.float32) / pairs)
    spot = np.arange(PATCH)
    angle = np.concatenate([theta[:, None] * (spot // GRID)[None], theta[:, None] * (spot % GRID)[None]])
    pad = ((0, HALF - 36), (0, 0))
    return (
        np.pad(np.cos(angle), pad).astype(np.float32),
        np.pad(np.sin(angle), pad).astype(np.float32),
    )


def rotate_pairs(v, cos, sin):
    a, b = v[..., :HALF, :], v[..., HALF:, :]
    return jnp.concatenate([a * cos - b * sin, b * cos + a * sin], axis=-2)


def pack_weights(qkv_weight, out_weight, gate_up_weight, down_weight, c):
    heads = lax.dynamic_slice_in_dim(qkv_weight, c * HD, HD, 2).transpose(1, 2, 0)
    qk = pair_rows(heads[:2]).reshape(2 * HEAD, D)
    v = pad_rows(heads[2])
    o = pad_rows(lax.dynamic_slice_in_dim(out_weight, c * HD, HD, 0))
    gu = lax.dynamic_slice_in_dim(gate_up_weight, c * SHARD_FF, SHARD_FF, 2)
    gu = gu.transpose(1, 2, 0).reshape(B_ROWS, D)
    dn = lax.dynamic_slice_in_dim(down_weight, c * SHARD_FF, SHARD_FF, 0)
    return jnp.concatenate([qk, v, o, gu, dn], axis=0)


def unpack_grads(both):
    both = both.astype(jnp.float32)
    qk = unpair_rows(both[:, : 2 * HEAD].reshape(2, 2, HEAD, D))
    v = both[:, 2 * HEAD : 2 * HEAD + HD].reshape(2, 1, HD, D)
    qkv = jnp.concatenate([qk, v], axis=1).transpose(3, 1, 0, 2).reshape(D, 3, 2 * HD)
    o = both[:, 3 * HEAD : 3 * HEAD + HD].reshape(2 * HD, D)
    gu = both[:, A_ROWS : A_ROWS + B_ROWS].reshape(2, 2, SHARD_FF, D)
    gu = gu.transpose(3, 1, 0, 2).reshape(D, 2, 2 * SHARD_FF)
    dn = both[:, A_ROWS + B_ROWS :].reshape(2 * SHARD_FF, D)
    return qkv, o, gu, dn


def fast(
    tokens, labels, timesteps, image_counts, class_table, ada_weight, ada_bias,
    qkv_weight, qkv_bias, qk_scale, out_weight, gate_up_weight, down_weight, out_grad,
):
    dot = lambda s, a, b: jnp.einsum(s, a, b, preferred_element_type=jnp.float32)
    t = lax.axis_index("tensor")
    c = lax.axis_index("dp") % 2
    own = pack_weights(qkv_weight, out_weight, gate_up_weight, down_weight, c)
    sib = lambda v: lax.ppermute(v, "dp", [(0, 1), (1, 0), (2, 3), (3, 2)])
    both = lambda v: jnp.concatenate([v, sib(v)])
    half = tokens.shape[0]
    images = labels.shape[0]
    meet = lambda v: v[:half] + sib(low(v[half:])).astype(jnp.float32)

    columns_here = class_table.shape[1]
    column = t * columns_here + jnp.arange(columns_here)
    half_width = D // 2
    frequency = jnp.exp(-math.log(10000.0) * (column % half_width).astype(jnp.float32) / half_width)
    angles = timesteps.astype(jnp.float32)[:, None] * frequency[None, :]
    time_embed = jnp.where(column[None, :] < half_width, jnp.cos(angles), jnp.sin(angles))
    classes = jnp.arange(class_table.shape[0])
    condition = dot("in,nc->ic", low(labels[:, None] == classes[None, :]), class_table) + time_embed
    mod_part = dot("ic,ckd->ikd", low(jax.nn.silu(condition)), ada_weight)
    heads = qkv_bias.reshape(3, 2, HD).swapaxes(0, 1)[..., None]
    bias_row = jnp.concatenate([pair_rows(heads[:, :2]).reshape(2, -1), pad_rows(heads[:, 2])[..., 0]], axis=1)
    bias_row = jnp.pad(bias_row, ((0, 0), (0, 16))).reshape(1, 1, -1)
    bias_row = jnp.pad(bias_row, ((0, 0), (0, 0), (0, D - bias_row.size)))
    bias_row = jnp.broadcast_to(bias_row, (images, 1, D))
    mod_part = jnp.concatenate([low(mod_part), bias_row, jnp.zeros_like(bias_row)], axis=1)
    cond_part = jnp.concatenate(
        [condition, labels.astype(jnp.float32)[:, None], jnp.zeros((images, 256 - columns_here - 1), jnp.float32)], axis=1)
    mod_images = images // 8
    kept = (t * mod_images + jnp.arange(mod_images) < image_counts[0]).astype(jnp.float32)
    ada = jnp.pad(ada_bias.astype(jnp.float32), ((0, 2), (0, 0)))
    ada = jnp.tile(ada, (mod_images, 1))
    gate_rows = jnp.array([0, 0, 1, 0, 0, 1, 0, 0], jnp.float32)
    keep = jnp.where(gate_rows[None, :] > 0, kept[:, None], 1.0).reshape(-1, 1)
    keep = jnp.broadcast_to(keep, ada.shape)
    gain_rows = jnp.broadcast_to(pair_rows(qk_scale.astype(jnp.float32)[..., None]).reshape(2 * HEAD, 1), (2 * HEAD, 128))
    cos, sin = pair_tables()
    table = np.tile(np.concatenate([cos, sin]), (1, tokens.shape[0] // PATCH))
    (weights, cond_all, mod, first_in, second_in, feed_grad, attention, qkv_t, norm_t, stat_t, mixed, gu_t, hidden) = forward(
        own, mod_part.reshape(8, images, D), cond_part, tokens, out_grad, ada, keep, gain_rows, table)
    cond_all = cond_all.reshape(4 * images, 256)
    condition = cond_all[:, :columns_here]
    labels_all = cond_all[:, columns_here].astype(jnp.int32)
    chosen = low(labels_all[:, None] == classes[None, :])
    cond_act = low(jax.nn.silu(condition))
    first_image = lax.axis_index("dp") * images
    mod = mod.reshape(mod_images, 8, D)
    mod_rows = jnp.repeat(mod, PATCH, axis=0)
    shift_one, scale_one, gate_one, shift_two, scale_two, gate_two = [mod_rows[:, i] for i in range(6)]
    gains = pair_rows(qk_scale.astype(jnp.float32)[..., None])
    cos, sin = np.tile(cos, (1, 4)), np.tile(sin, (1, 4))
    flat = lambda v: v.swapaxes(-3, -2).reshape(v.shape[:-3] + (v.shape[-2], 1024))
    qkv_t, norm_t, stat_t, gu_t, hidden = [flat(v) for v in (qkv_t, norm_t, stat_t, gu_t, hidden)]
    mixed = flat(mixed).reshape(8, HEAD, 1024)
    first_in, second_in, feed_grad = [v.reshape(1024, D) for v in (first_in, second_in, feed_grad)]
    q_t, k_t, v_t = [qkv_t[:, i * HEAD : (i + 1) * HEAD] for i in range(3)]
    q_norm, k_norm = [norm_t[:, i * HEAD : (i + 1) * HEAD].astype(jnp.float32) for i in range(2)]
    q_inv, k_inv, logsum = [stat_t[:, i : i + 1] for i in range(3)]
    g, u = [gu_t[:, i * SHARD_FF : (i + 1) * SHARD_FF].astype(jnp.float32) for i in range(2)]
    act = jax.nn.silu(g)
    factor = FACTOR
    cut = lambda v: v.reshape(8, HEAD, 4, PATCH)
    scores = dot("heiq,heik->hikq", cut(q_t), cut(k_t)) * factor
    prob = jnp.exp(scores - logsum.reshape(8, 4, 1, PATCH))
    prob_low = low(prob)
    wo = weights[:, 3 * HEAD : 4 * HEAD]
    wg = weights[:, A_ROWS : A_ROWS + SHARD_FF]
    wu = weights[:, A_ROWS + SHARD_FF : A_ROWS + B_ROWS]
    wd = weights[:, A_ROWS + B_ROWS :]
    tokens_f = tokens.astype(jnp.float32)
    first_norm, first_inverse = normalize(tokens_f)
    after_attn = tokens_f + gate_one * attention
    second_norm, second_inverse = normalize(after_attn)
    feed = meet(dot("sfn,sfd->nd", hidden, wd))
    result = low(after_attn + gate_two * feed)

    grad_out = out_grad.astype(jnp.float32)
    hidden_grad = dot("sfd,nd->sfn", wd, feed_grad)
    g_grad = low(hidden_grad * u * silu_slope(g))
    u_grad = low(hidden_grad * act)
    d_part = low(dot("sfn,nd->sfd", hidden, feed_grad))
    g_part = low(dot("sfn,nd->sfd", g_grad, second_in))
    u_part = low(dot("sfn,nd->sfd", u_grad, second_in))
    second_grad = meet(dot("sfn,sfd->nd", g_grad, wg) + dot("sfn,sfd->nd", u_grad, wu))
    after_grad = grad_out + normalize_back(second_grad * (1.0 + scale_two), second_norm, second_inverse)
    attn_grad = both(low(after_grad * gate_one))
    mixed_grad = low(dot("hed,nd->hen", wo, attn_grad))
    o_part = low(dot("hen,nd->hed", mixed, attn_grad))
    v_grad = low(dot("hikq,heiq->heik", prob_low, cut(mixed_grad))).reshape(8, HEAD, 1024)
    prob_grad = dot("heik,heiq->hikq", cut(v_t), cut(mixed_grad))
    score_grad = low(prob * (prob_grad - jnp.sum(prob * prob_grad, axis=2, keepdims=True)))
    q_back = dot("hikq,heik->heiq", score_grad, cut(k_t)).reshape(8, HEAD, 1024) * factor
    k_back = dot("hikq,heiq->heik", score_grad, cut(q_t)).reshape(8, HEAD, 1024) * factor
    q_back = rotate_pairs(q_back, cos, -sin)
    k_back = rotate_pairs(k_back, cos, -sin)
    scale_part = jnp.stack([jnp.sum(q_back * q_norm, axis=(0, 2)), jnp.sum(k_back * k_norm, axis=(0, 2))])
    q_grad = low(normalize_back(q_back * gains[0], q_norm, q_inv, 1, HD))
    k_grad = low(normalize_back(k_back * gains[1], k_norm, k_inv, 1, HD))
    qkv_grad = jnp.concatenate([q_grad, k_grad, v_grad], axis=1)
    bias_part = jnp.sum(qkv_grad.astype(jnp.float32), axis=2)
    qkv_part = low(dot("hen,nd->hed", qkv_grad, first_in))
    first_grad = meet(dot("hen,hed->nd", qkv_grad, weights[:, : 3 * HEAD]))
    tokens_grad = after_grad + normalize_back(first_grad * (1.0 + scale_one), first_norm, first_inverse)

    per_image = lambda v: jnp.sum(v.reshape(mod_images, PATCH, D), axis=1)
    mod_grad = low(jnp.stack([
        per_image(first_grad), per_image(first_grad * first_norm), per_image(after_grad * attention) * kept[:, None],
        per_image(second_grad), per_image(second_grad * second_norm), per_image(grad_out * feed) * kept[:, None],
    ], axis=1))
    tail = jnp.concatenate([low(bias_part).reshape(-1), low(scale_part).reshape(-1)])
    tail = jnp.pad(tail, (0, (PAY - 6 * mod_images) * D - tail.size)).reshape(-1, D)
    pay = jnp.concatenate([mod_grad.reshape(6 * mod_images, D), tail], axis=0)
    summed, pay_all = reduce_grads(jnp.concatenate([qkv_part, o_part, g_part, u_part, d_part], axis=1), pay)
    qkv_weight_grad, out_weight_grad, gate_up_grad, down_grad = unpack_grads(summed)

    mod_grad = pay_all[:, : 6 * mod_images].reshape(-1, 6, D)
    tail = pay_all[:, 6 * mod_images :].reshape(32, -1).astype(jnp.float32)
    bias_all = tail[:, : bias_part.size].reshape(32, 8, 3 * HEAD)
    scale_all = tail[:, bias_part.size : bias_part.size + scale_part.size].reshape(32, 2, HEAD)
    qk_scale_grad = unpair_rows(jnp.sum(scale_all, axis=0)[..., None])[..., 0]
    bias_all = lax.dynamic_index_in_dim(bias_all, t, 1, keepdims=False).reshape(2, 2, 8, 3, HEAD)
    bias_sum = jnp.sum(bias_all, axis=(0, 2))
    qk_bias = unpair_rows(bias_sum[:, :2, :, None])[..., 0]
    qkv_bias_grad = jnp.concatenate([qk_bias, bias_sum[:, 2:, :HD]], axis=1).transpose(1, 0, 2).reshape(3, 2 * HD)

    ada_weight_grad = dot("ic,ikd->ckd", cond_act, mod_grad)
    ada_bias_grad = jnp.sum(mod_grad.astype(jnp.float32), axis=0)
    act_grad = dot("ikd,ckd->ic", mod_grad, ada_weight)
    cond_grad_all = act_grad * silu_slope(condition)
    table_grad = jnp.dot(chosen.astype(jnp.float32).T, cond_grad_all, precision=HIGH)
    cond_grad = lax.dynamic_slice_in_dim(cond_grad_all, first_image, images, 0)
    return (
        result, tokens_grad, cond_grad, table_grad, ada_weight_grad, ada_bias_grad,
        qkv_weight_grad, qkv_bias_grad, qk_scale_grad, out_weight_grad, gate_up_grad, down_grad,
    )


def rope_tables(count):
    pairs = HD // 4
    theta = jnp.exp(-math.log(100.0) * jnp.arange(pairs, dtype=jnp.float32) / pairs)
    place = jnp.arange(count) % PATCH
    row_angle = (place // GRID).astype(jnp.float32)[:, None] * theta
    col_angle = (place % GRID).astype(jnp.float32)[:, None] * theta
    return ((jnp.cos(row_angle), jnp.sin(row_angle)), (jnp.cos(col_angle), jnp.sin(col_angle)))


def rotate_part(segment, cosine, sine, direction):
    half_len = segment.shape[-1] // 2
    first, second = (segment[..., :half_len], segment[..., half_len:])
    cosine = cosine[:, None, :]
    sine = direction * sine[:, None, :]
    return jnp.concatenate(
        [first * cosine - second * sine, second * cosine + first * sine], axis=-1
    )


def rotate(vectors, tables, direction):
    half_len = vectors.shape[-1] // 2
    return jnp.concatenate(
        [
            rotate_part(vectors[..., :half_len], tables[0][0], tables[0][1], direction),
            rotate_part(vectors[..., half_len:], tables[1][0], tables[1][1], direction),
        ],
        axis=-1,
    )


def general(
    tokens,
    labels,
    timesteps,
    image_counts,
    class_table,
    ada_weight,
    ada_bias,
    qkv_weight,
    qkv_bias,
    qk_scale,
    out_weight,
    gate_up_weight,
    down_weight,
    out_grad,
):
    width = tokens.shape[1]
    local_rows = tokens.shape[0]
    members = lax.axis_size("tensor")
    place = lax.axis_index("tensor")
    images = labels.shape[0]
    all_rows = local_rows * members
    columns_here = class_table.shape[1]
    heads_here = columns_here // HD
    column = place * columns_here + jnp.arange(columns_here)
    half_width = width // 2
    frequency = jnp.exp(-math.log(10000.0) * (column % half_width).astype(jnp.float32) / half_width)
    angles = timesteps.astype(jnp.float32)[:, None] * frequency[None, :]
    time_embed = jnp.where(column[None, :] < half_width, jnp.cos(angles), jnp.sin(angles))
    chosen = (labels[:, None] == jnp.arange(class_table.shape[0])[None, :]).astype(jnp.bfloat16)
    condition = jnp.dot(chosen, class_table, preferred_element_type=jnp.float32) + time_embed
    cond_act = jax.nn.silu(condition).astype(jnp.bfloat16)
    mod_part = jnp.einsum("ic,ckd->ikd", cond_act, ada_weight, preferred_element_type=jnp.float32)
    modulation = lax.psum(mod_part, "tensor") + ada_bias.astype(jnp.float32)
    row_index = place * local_rows + jnp.arange(local_rows)
    row_image = row_index // PATCH
    selector = (row_image[:, None] == jnp.arange(images)[None, :]).astype(jnp.float32)
    mod_rows = jnp.dot(selector, modulation.reshape(images, 6 * width), precision=HIGH).reshape(
        local_rows, 6, width
    )
    kept = (row_image < image_counts[0]).astype(jnp.float32)[:, None]
    shift_one, scale_one, gate_one, shift_two, scale_two, gate_two = [
        mod_rows[:, index] for index in range(6)
    ]
    tokens_f = tokens.astype(jnp.float32)
    first_norm, first_inverse = normalize(tokens_f)
    first_in = (first_norm * (1.0 + scale_one) + shift_one).astype(jnp.bfloat16)
    first_all = lax.all_gather(first_in, "tensor", axis=0, tiled=True)
    qkv = jnp.einsum(
        "nd,dkc->nkc", first_all, qkv_weight, preferred_element_type=jnp.float32
    ) + qkv_bias.astype(jnp.float32)
    head_view = qkv.reshape(all_rows, 3, heads_here, HD)
    tables = rope_tables(all_rows)
    qk_gains = qk_scale.astype(jnp.float32)
    query_normed, query_inverse = normalize(head_view[:, 0])
    key_normed, key_inverse = normalize(head_view[:, 1])
    block_shape = (all_rows // PATCH, PATCH, heads_here, HD)
    queries = (
        rotate(query_normed * qk_gains[0], tables, 1.0).astype(jnp.bfloat16).reshape(block_shape)
    )
    keys_rot = (
        rotate(key_normed * qk_gains[1], tables, 1.0).astype(jnp.bfloat16).reshape(block_shape)
    )
    values = head_view[:, 2].astype(jnp.bfloat16).reshape(block_shape)
    factor = HD ** (-0.5)
    scores = (
        jnp.einsum("iqhe,ikhe->ihqk", queries, keys_rot, preferred_element_type=jnp.float32)
        * factor
    )
    row_max = jnp.max(scores, axis=-1, keepdims=True)
    exponent = jnp.exp(scores - row_max)
    totals = jnp.sum(exponent, axis=-1, keepdims=True)
    logsum = row_max + jnp.log(totals)
    probability = (exponent / totals).astype(jnp.bfloat16)
    mixed_heads = (
        jnp.einsum("ihqk,ikhe->iqhe", probability, values, preferred_element_type=jnp.float32)
        .reshape(all_rows, columns_here)
        .astype(jnp.bfloat16)
    )
    attention = lax.psum_scatter(
        jnp.dot(mixed_heads, out_weight, preferred_element_type=jnp.float32).astype(jnp.bfloat16),
        "tensor",
        scatter_dimension=0,
        tiled=True,
    ).astype(jnp.float32)
    after_attn = tokens_f + kept * gate_one * attention
    second_norm, second_inverse = normalize(after_attn)
    second_in = (second_norm * (1.0 + scale_two) + shift_two).astype(jnp.bfloat16)
    second_all = lax.all_gather(second_in, "tensor", axis=0, tiled=True)
    gate_up = jnp.einsum(
        "nd,dkf->nkf", second_all, gate_up_weight, preferred_element_type=jnp.float32
    )
    gate_value, up_value = (gate_up[:, 0], gate_up[:, 1])
    activated = jax.nn.silu(gate_value)
    hidden = (activated * up_value).astype(jnp.bfloat16)
    feed = lax.psum_scatter(
        jnp.dot(hidden, down_weight, preferred_element_type=jnp.float32).astype(jnp.bfloat16),
        "tensor",
        scatter_dimension=0,
        tiled=True,
    ).astype(jnp.float32)
    result = (after_attn + kept * gate_two * feed).astype(jnp.bfloat16)
    grad_out = out_grad.astype(jnp.float32)
    feed_grad = (grad_out * kept * gate_two).astype(jnp.bfloat16)
    gate_two_grad = grad_out * kept * feed
    feed_grad_all = lax.all_gather(feed_grad, "tensor", axis=0, tiled=True)
    hidden_grad = jnp.einsum(
        "nd,fd->nf", feed_grad_all, down_weight, preferred_element_type=jnp.float32
    )
    down_grad = jnp.einsum("nf,nd->fd", hidden, feed_grad_all, preferred_element_type=jnp.float32)
    gate_grad = hidden_grad * up_value * silu_slope(gate_value)
    up_grad = hidden_grad * activated
    gu_grad = jnp.stack([gate_grad, up_grad], axis=1).astype(jnp.bfloat16)
    gate_up_grad = jnp.einsum(
        "nd,nkf->dkf", second_all, gu_grad, preferred_element_type=jnp.float32
    )
    second_grad = lax.psum_scatter(
        jnp.einsum(
            "nkf,dkf->nd", gu_grad, gate_up_weight, preferred_element_type=jnp.float32
        ).astype(jnp.bfloat16),
        "tensor",
        scatter_dimension=0,
        tiled=True,
    ).astype(jnp.float32)
    after_grad = grad_out + normalize_back(
        second_grad * (1.0 + scale_two), second_norm, second_inverse
    )
    attention_grad = (after_grad * kept * gate_one).astype(jnp.bfloat16)
    gate_one_grad = after_grad * kept * attention
    attention_grad_all = lax.all_gather(attention_grad, "tensor", axis=0, tiled=True)
    mixed_grad = jnp.einsum(
        "nd,cd->nc", attention_grad_all, out_weight, preferred_element_type=jnp.float32
    ).astype(jnp.bfloat16)
    out_weight_grad = jnp.einsum(
        "nc,nd->cd", mixed_heads, attention_grad_all, preferred_element_type=jnp.float32
    )
    scores_again = (
        jnp.einsum("iqhe,ikhe->ihqk", queries, keys_rot, preferred_element_type=jnp.float32)
        * factor
    )
    prob_again = jnp.exp(scores_again - logsum)
    mixed_blocks = mixed_grad.reshape(block_shape)
    values_grad = jnp.einsum(
        "ihqk,iqhe->ikhe",
        prob_again.astype(jnp.bfloat16),
        mixed_blocks,
        preferred_element_type=jnp.float32,
    )
    prob_grad = jnp.einsum(
        "iqhe,ikhe->ihqk", mixed_blocks, values, preferred_element_type=jnp.float32
    )
    score_grad = (
        prob_again * (prob_grad - jnp.sum(prob_again * prob_grad, axis=-1, keepdims=True))
    ).astype(jnp.bfloat16)
    queries_grad = (
        jnp.einsum("ihqk,ikhe->iqhe", score_grad, keys_rot, preferred_element_type=jnp.float32)
        * factor
    )
    keys_grad = (
        jnp.einsum("ihqk,iqhe->ikhe", score_grad, queries, preferred_element_type=jnp.float32)
        * factor
    )
    query_back = rotate(queries_grad.reshape(all_rows, heads_here, HD), tables, -1.0)
    key_back = rotate(keys_grad.reshape(all_rows, heads_here, HD), tables, -1.0)
    scale_part = jnp.stack(
        [
            jnp.sum(query_back * query_normed, axis=(0, 1)),
            jnp.sum(key_back * key_normed, axis=(0, 1)),
        ]
    )
    query_raw = normalize_back(query_back * qk_gains[0], query_normed, query_inverse)
    key_raw = normalize_back(key_back * qk_gains[1], key_normed, key_inverse)
    qkv_grad = (
        jnp.stack([query_raw, key_raw, values_grad.reshape(all_rows, heads_here, HD)], axis=1)
        .reshape(all_rows, 3, columns_here)
        .astype(jnp.bfloat16)
    )
    qkv_weight_grad = jnp.einsum(
        "nd,nkc->dkc", first_all, qkv_grad, preferred_element_type=jnp.float32
    )
    qkv_bias_grad = jnp.sum(qkv_grad.astype(jnp.float32), axis=0)
    first_grad = lax.psum_scatter(
        jnp.einsum("nkc,dkc->nd", qkv_grad, qkv_weight, preferred_element_type=jnp.float32).astype(
            jnp.bfloat16
        ),
        "tensor",
        scatter_dimension=0,
        tiled=True,
    ).astype(jnp.float32)
    tokens_grad = after_grad + normalize_back(
        first_grad * (1.0 + scale_one), first_norm, first_inverse
    )
    row_mod_grad = jnp.stack(
        [
            first_grad,
            first_grad * first_norm,
            gate_one_grad,
            second_grad,
            second_grad * second_norm,
            gate_two_grad,
        ],
        axis=1,
    ).reshape(local_rows, 6 * width)
    mod_grad_part = jnp.dot(selector.T, row_mod_grad, precision=HIGH).reshape(images, 6, width)
    mod_grad, scale_grad = (
        lax.psum(mod_grad_part.astype(jnp.bfloat16), "tensor").astype(jnp.float32),
        lax.psum(scale_part.astype(jnp.bfloat16), "tensor").astype(jnp.float32),
    )
    mod_grad_low = mod_grad.astype(jnp.bfloat16)
    ada_weight_grad = jnp.einsum(
        "ic,ikd->ckd", cond_act, mod_grad_low, preferred_element_type=jnp.float32
    )
    ada_bias_grad = jnp.sum(mod_grad_low.astype(jnp.float32), axis=0)
    act_grad = jnp.einsum(
        "ikd,ckd->ic", mod_grad_low, ada_weight, preferred_element_type=jnp.float32
    )
    cond_grad = act_grad * silu_slope(condition)
    table_grad = jnp.dot(chosen.astype(jnp.float32).T, cond_grad, precision=HIGH)
    summed = (
        lax.psum(table_grad.astype(jnp.bfloat16), "dp").astype(jnp.float32),
        lax.psum(ada_weight_grad.astype(jnp.bfloat16), "dp").astype(jnp.float32),
        lax.psum(ada_bias_grad.astype(jnp.bfloat16), "dp").astype(jnp.float32),
        lax.psum(qkv_weight_grad.astype(jnp.bfloat16), "dp").astype(jnp.float32),
        lax.psum(qkv_bias_grad.astype(jnp.bfloat16), "dp").astype(jnp.float32),
        lax.psum(scale_grad.astype(jnp.bfloat16), "dp").astype(jnp.float32),
        lax.psum(out_weight_grad.astype(jnp.bfloat16), "dp").astype(jnp.float32),
        lax.psum(gate_up_grad.astype(jnp.bfloat16), "dp").astype(jnp.float32),
        lax.psum(down_grad.astype(jnp.bfloat16), "dp").astype(jnp.float32),
    )
    return (result, tokens_grad, cond_grad) + tuple(summed)


def solution(mesh):
    placed = (
        P(("dp", "tensor"), None),
        P("dp"),
        P("dp"),
        P("dp"),
        P(None, "tensor"),
        P("tensor", None, None),
        P(),
        P(None, None, "tensor"),
        P(None, "tensor"),
        P(),
        P("tensor", None),
        P(None, None, "tensor"),
        P("tensor", None),
        P(("dp", "tensor"), None),
    )
    plain = mesh.shape["dp"] != 4 or mesh.shape["tensor"] != 8
    return jax.shard_map(
        general if plain else fast,
        mesh=mesh,
        in_specs=placed,
        out_specs=(
            P(("dp", "tensor"), None),
            P(("dp", "tensor"), None),
            P("dp", "tensor"),
            P(None, "tensor"),
            P("tensor", None, None),
            P(),
            P(None, None, "tensor"),
            P(None, "tensor"),
            P(),
            P("tensor", None),
            P(None, None, "tensor"),
            P("tensor", None),
        ),
        check_vma=False,
    )
```

```python
import math

import jax
import jax.numpy as jnp
import numpy as np
from jax import lax
from jax.experimental import pallas as pl
from jax.experimental.pallas import tpu as pltpu
from jax.sharding import PartitionSpec as P

HD = 72
GRID = 16
PATCH = 256
HIGH = lax.Precision.HIGHEST
MESH = pl.DeviceIdType.MESH
epsilon = 1e-06

HEAD = 80
HALF = 40
SHARD_FF = 192
A_ROWS = 4 * HEAD
B_ROWS = 2 * SHARD_FF
C_ROWS = SHARD_FF
ROWS_ALL = A_ROWS + B_ROWS + C_ROWS
D = 1152

G_STAGE, G_LONE = 128, 48
G_STAGES = ROWS_ALL // G_STAGE
PAY = 16


def place():
    d = lax.axis_index("dp")
    t = lax.axis_index("tensor")
    return d // 2, d % 2, t // 2, t % 2


def at(x, c, z, y):
    return (x * 2 + c, z * 2 + y)


def greet(targets):
    barrier = pltpu.get_barrier_semaphore()
    for o in targets:
        pl.semaphore_signal(barrier, inc=1, device_id=o, device_id_type=MESH)
    pl.semaphore_wait(barrier, len(targets))


def rows_at(first, size):
    return pl.ds(pl.multiple_of(first, 16), size)


def nt(a, b):
    return lax.dot_general(a, b, (((1,), (1,)), ((), ())), preferred_element_type=jnp.float32)


def tn(a, b):
    return lax.dot_general(a, b, (((0,), (0,)), ((), ())), preferred_element_type=jnp.float32)


def nn(a, b):
    return lax.dot_general(a, b, (((1,), (0,)), ((), ())), preferred_element_type=jnp.float32)


def low(v):
    return v.astype(jnp.bfloat16)


def wide(v):
    return v.astype(jnp.float32)


def turn(v, cos, sin):
    a, b = v[:HALF], v[HALF:]
    return jnp.concatenate([a * cos - b * sin, b * cos + a * sin], axis=0)


def remote(src, dst, ss, rs, to):
    return pltpu.make_async_remote_copy(
        src_ref=src, dst_ref=dst, send_sem=ss, recv_sem=rs, device_id=to, device_id_type=MESH)


CHUNK = 64
FACTOR = HD ** (-0.5)


def forward_kernel(
    own, mod_in, cond_in, tokens, out_grad, ada, keep, gains, table,
    full, cond_out, mod_out, fi_out, si_out, fg_out, att_out, qkv_out, norm_out, stat_out, mixed_out, gu_out, hid_out,
    mod_all, mod, fi, si, fg, att, att_send, att_recv, wa, ow, mixed, qkv, norm, stat, wb, gu, hid,
    send, recv, ms, mr, cs, cr, es, er, ls, qs, hs, ws, save,
):
    x, c, z, y = place()
    t = z * 2 + y
    d = x * 2 + c
    peers = [lax.rem(t + k, 8) for k in range(1, 8)]
    groups = [lax.rem(d + k, 4) for k in range(1, 4)]
    greet([(d, p) for p in peers] + [(g, t) for g in groups])
    y_side, x_side, core = at(x, c, z, 1 - y), at(1 - x, c, z, y), at(x, 1 - c, z, y)
    up, down = at(x, c, z + 1, y), at(x, c, z - 1, y)
    small = []
    for k, p in enumerate(peers):
        small.append(remote(mod_in.at[p], mod_all.at[t], ms.at[k], mr.at[t], (d, p)))
    for k, g in enumerate(groups):
        small.append(remote(cond_in, cond_out.at[d], cs.at[k], cr.at[d], (g, t)))
    for cp in small:
        cp.start()
    kept = [
        pltpu.make_async_copy(own, full.at[t], ls.at[0]),
        pltpu.make_async_copy(mod_in.at[t], mod_all.at[t], ls.at[1]),
        pltpu.make_async_copy(cond_in, cond_out.at[d], ls.at[2]),
    ]
    for cp in kept:
        cp.start()

    def plane(g):
        return rows_at(g * G_STAGE + x * G_LONE, G_STAGE - G_LONE)

    def lone(g, side):
        return rows_at(g * G_STAGE + side * (G_STAGE - G_LONE), G_LONE)

    def copy(g, kind, src, slot, rows, path, to):
        return remote(src.at[rows], full.at[slot, rows], send.at[g, kind], recv.at[g, slot, path], to)

    def arrived(g, slot, rows, path):
        copy(g, 0, own, slot, rows, path, x_side).wait_recv()

    def issue(g):
        copy(g, 2, own, t, plane(g), 0, y_side).start()
        pl.when(z < 3)(lambda: copy(g, 0, own, t, plane(g), 0, up).start())
        pl.when(z > 0)(lambda: copy(g, 1, own, t, plane(g), 0, down).start())

    def along_z(g, j):
        def below():
            slot = (z - j) * 2 + y
            arrived(g, slot, plane(g), 0)
            pl.when(z < 3)(lambda: copy(g, 1 + 2 * j, full.at[slot], slot, plane(g), 0, up).start())
            copy(g, 8 + j, full.at[slot], slot, plane(g), 0, y_side).start()
            copy(g, 11 + j, full.at[slot], slot, lone(g, x), 1, x_side).start()

        def above():
            slot = (z + j) * 2 + y
            arrived(g, slot, plane(g), 0)
            pl.when(z > 0)(lambda: copy(g, 2 + 2 * j, full.at[slot], slot, plane(g), 0, down).start())
            copy(g, 14 + j, full.at[slot], slot, plane(g), 0, y_side).start()
            copy(g, 17 + j, full.at[slot], slot, lone(g, x), 1, x_side).start()

        pl.when(z >= j)(below)
        pl.when(z + j <= 3)(above)

    def along_y(g, zz):
        slot = zz * 2 + 1 - y
        arrived(g, slot, plane(g), 0)
        copy(g, 21 + zz, full.at[slot], slot, lone(g, x), 1, x_side).start()

    def service(i):
        def on(g, act):
            pl.when(jnp.logical_and(g >= 0, g < G_STAGES))(lambda: act(g))

        on(i, issue)
        for j in (1, 2, 3):
            on(i - j, lambda g: along_z(g, j))
        on(i - 1, lambda g: along_y(g, z))
        for j in (1, 2, 3):
            @pl.when(z >= j)
            def _():
                on(i - j - 1, lambda g: along_y(g, z - j))

            @pl.when(z + j <= 3)
            def _():
                on(i - j - 1, lambda g: along_y(g, z + j))

    def lone_in(first, last):
        @pl.loop(first, last)
        def _(g):
            for k in range(1, 8):
                arrived(g, lax.rem(t + k, 8), lone(g, 1 - x), 1)

    def mod_row(image, k):
        return mod[pl.ds(image * 8 + k, 1), :]

    def by_rows(act):
        for image in range(2):
            @pl.loop(0, PATCH // CHUNK)
            def _(i):
                act(image, rows_at(image * PATCH + i * CHUNK, CHUNK))

    service(0)

    for k, p in enumerate(peers):
        remote(mod_in.at[p], mod_all.at[p], ms.at[0], mr.at[p], (d, p)).wait_recv()
    kept[1].wait()
    total = ada[...]
    for s in range(8):
        total = total + wide(mod_all[s])
    mod[...] = total * keep[...]

    def first_rows(image, rows):
        v = wide(tokens[rows, :])
        n = v * lax.rsqrt(jnp.mean(v * v, axis=-1, keepdims=True) + epsilon)
        fi[0, rows, :] = low(n * (1.0 + mod_row(image, 1)) + mod_row(image, 0))

    by_rows(first_rows)
    share_fi = remote(fi.at[0], fi.at[1], es.at[0], er.at[0], core)
    share_fi.start()
    service(1)

    def feed_rows(image, rows):
        fg[0, rows, :] = low(wide(out_grad[rows, :]) * mod_row(image, 5))

    by_rows(feed_rows)
    share_fg = remote(fg.at[0], fg.at[1], es.at[1], er.at[1], core)
    share_fg.start()

    @pl.loop(2, 7)
    def _(i):
        service(i)

    kept[0].wait()
    lone_in(0, 3)
    share_fi.wait_recv()
    share_fg.wait_recv()
    saves = [
        pltpu.make_async_copy(fi, fi_out, save.at[0]),
        pltpu.make_async_copy(fg, fg_out, save.at[1]),
        pltpu.make_async_copy(mod, mod_out, save.at[2]),
    ]
    for cp in saves:
        cp.start()

    def load_a(s):
        return pltpu.make_async_copy(full.at[s, pl.ds(0, 3 * HEAD)], wa.at[lax.rem(s, 2)], ws.at[lax.rem(s, 2)])

    load_o = pltpu.make_async_copy(full.at[:, pl.ds(3 * HEAD, HEAD)], ow, ls.at[3])
    load_o.start()
    load_a(0).start()

    def save_head(s):
        b = lax.rem(s, 2)
        return [
            pltpu.make_async_copy(qkv.at[b], qkv_out.at[s], qs.at[b, 0]),
            pltpu.make_async_copy(norm.at[b], norm_out.at[s], qs.at[b, 1]),
            pltpu.make_async_copy(stat.at[b], stat_out.at[s], qs.at[b, 2]),
        ]

    @pl.loop(0, 8)
    def _(s):
        b = lax.rem(s, 2)
        load_a(s).wait()
        pl.when(s < 7)(lambda: load_a(s + 1).start())

        @pl.when(s > 1)
        def _():
            for cp in save_head(s - 2):
                cp.wait()

        bias_row = wide(mod_all[s, 6:7, :512])
        bias_row = jnp.where(c == 0, bias_row[:, :256], bias_row[:, 256:])
        bias = jnp.transpose(jnp.broadcast_to(bias_row, (128, 256)))[: 3 * HEAD, :1]
        cos, sin = table[:HALF, :], table[HALF:, :]
        for h in range(2):
            raw = nt(wa[b], fi[h]) + bias
            turned = []
            for i in range(2):
                v = raw[i * HEAD : (i + 1) * HEAD]
                inv = lax.rsqrt(jnp.sum(v * v, axis=0, keepdims=True) * (1.0 / HD) + epsilon)
                n = v * inv
                norm[b, h, i * HEAD : (i + 1) * HEAD, :] = low(n)
                stat[b, h, i : i + 1, :] = inv
                turned.append(low(turn(n * gains[i * HEAD : (i + 1) * HEAD, :1], cos, sin)))
            q, k = turned
            v = low(raw[2 * HEAD :])
            qkv[b, h, :HEAD, :] = q
            qkv[b, h, HEAD : 2 * HEAD, :] = k
            qkv[b, h, 2 * HEAD :, :] = v
            for image in range(2):
                cut = slice(image * PATCH, (image + 1) * PATCH)
                e = jnp.exp(tn(k[:, cut], q[:, cut]) * FACTOR)
                row_sum = jnp.sum(e, axis=0, keepdims=True)
                stat[b, h, 2:3, cut] = jnp.log(row_sum)
                p = low(e * (1.0 / row_sum))
                mixed[h, pl.ds(pl.multiple_of(s * HEAD, 16), HEAD), cut] = low(nn(v[:, cut], p))
        for cp in save_head(s):
            cp.start()

        @pl.when(lax.rem(s, 4) == 3)
        def _():
            service(7 + s // 4)

    for s in (6, 7):
        for cp in save_head(s):
            cp.wait()
    load_o.wait()
    saves.append(pltpu.make_async_copy(mixed, mixed_out, save.at[3]))
    saves[-1].start()

    for image in range(2):
        cut = slice(image * PATCH, (image + 1) * PATCH)
        att_send[cut, :] = low(tn(mixed[1, :, cut], ow[...].reshape(8 * HEAD, D)))
    share_att = remote(att_send, att_recv, es.at[2], er.at[2], core)
    share_att.start()
    for image in range(2):
        cut = slice(image * PATCH, (image + 1) * PATCH)
        att[cut, :] = tn(mixed[0, :, cut], ow[...].reshape(8 * HEAD, D))
    share_att.wait_recv()

    def second_rows(image, rows):
        a = att[rows, :] + wide(att_recv[rows, :])
        att[rows, :] = a
        v = wide(tokens[rows, :]) + mod_row(image, 2) * a
        n = v * lax.rsqrt(jnp.mean(v * v, axis=-1, keepdims=True) + epsilon)
        si[0, rows, :] = low(n * (1.0 + mod_row(image, 4)) + mod_row(image, 3))

    by_rows(second_rows)
    share_si = remote(si.at[0], si.at[1], es.at[3], er.at[3], core)
    share_si.start()
    service(9)
    lone_in(3, 6)
    share_si.wait_recv()
    saves += [
        pltpu.make_async_copy(att, att_out, save.at[4]),
        pltpu.make_async_copy(si, si_out, save.at[5]),
    ]
    saves[-2].start()
    saves[-1].start()

    def load_b(s):
        return pltpu.make_async_copy(full.at[s, pl.ds(A_ROWS, B_ROWS)], wb.at[lax.rem(s, 2)], ws.at[2 + lax.rem(s, 2)])

    def save_shard(s):
        b = lax.rem(s, 2)
        return [
            pltpu.make_async_copy(gu.at[b], gu_out.at[s], hs.at[b, 0]),
            pltpu.make_async_copy(hid.at[b], hid_out.at[s], hs.at[b, 1]),
        ]

    load_b(0).start()

    @pl.loop(0, 8)
    def _(s):
        b = lax.rem(s, 2)
        load_b(s).wait()
        pl.when(s < 7)(lambda: load_b(s + 1).start())

        @pl.when(s > 1)
        def _():
            for cp in save_shard(s - 2):
                cp.wait()

        for h in range(2):
            both = nt(wb[b], si[h])
            g, u = both[:SHARD_FF], both[SHARD_FF:]
            gu[b, h] = low(both)
            hid[b, h] = low(g * (1.0 / (1.0 + jnp.exp(-g))) * u)
        for cp in save_shard(s):
            cp.start()

        pl.when(s == 3)(lambda: service(10))

    lone_in(6, 7)
    for s in (6, 7):
        for cp in save_shard(s):
            cp.wait()

    @pl.loop(0, G_STAGES)
    def _(g):
        def sent(kind, rows):
            copy(g, kind, own, t, rows, 0, x_side).wait_send()

        sent(2, plane(g))
        pl.when(z < 3)(lambda: sent(0, plane(g)))
        pl.when(z > 0)(lambda: sent(1, plane(g)))
        for k in range(4):
            sent(21 + k, lone(g, x))
        for j in (1, 2, 3):
            @pl.when(z >= j)
            def _():
                pl.when(z < 3)(lambda: sent(1 + 2 * j, plane(g)))
                sent(8 + j, plane(g))
                sent(11 + j, lone(g, x))

            @pl.when(z + j <= 3)
            def _():
                pl.when(z > 0)(lambda: sent(2 + 2 * j, plane(g)))
                sent(14 + j, plane(g))
                sent(17 + j, lone(g, x))

    for cp in small + [share_fi, share_fg, share_att, share_si]:
        cp.wait_send()
    for g in groups:
        remote(cond_in, cond_out.at[g], cs.at[0], cr.at[g], (g, t)).wait_recv()
    kept[2].wait()
    for cp in saves:
        cp.wait()


def forward(own, mod_in, cond_in, tokens, out_grad, ada, keep, gains, table):
    dma = pltpu.SemaphoreType.DMA
    vm = pltpu.VMEM
    bf, f32 = jnp.bfloat16, jnp.float32
    anywhere = pl.BlockSpec(memory_space=pl.ANY)
    inside = pl.BlockSpec(memory_space=pltpu.VMEM)
    R = tokens.shape[0]
    outs = [
        ((8, ROWS_ALL, D), bf), ((4,) + cond_in.shape, f32), ((16, D), f32),
        ((2, R, D), bf), ((2, R, D), bf), ((2, R, D), bf), ((R, D), f32),
        ((8, 2, 3 * HEAD, R), bf), ((8, 2, 2 * HEAD, R), bf), ((8, 2, 8, R), f32), ((2, 8 * HEAD, R), bf),
        ((8, 2, B_ROWS, R), bf), ((8, 2, SHARD_FF, R), bf),
    ]
    return pl.pallas_call(
        forward_kernel,
        out_shape=tuple(jax.ShapeDtypeStruct(s, e) for s, e in outs),
        in_specs=[anywhere] * 3 + [inside] * 6,
        out_specs=(anywhere,) * len(outs),
        scratch_shapes=[
            vm((8, 16, D), bf), vm((16, D), f32),
            vm((2, R, D), bf), vm((2, R, D), bf), vm((2, R, D), bf), vm((R, D), f32), vm((R, D), bf), vm((R, D), bf),
            vm((2, 3 * HEAD, D), bf), vm((8, HEAD, D), bf), vm((2, 8 * HEAD, R), bf),
            vm((2, 2, 3 * HEAD, R), bf), vm((2, 2, 2 * HEAD, R), bf), vm((2, 2, 8, R), f32),
            vm((2, B_ROWS, D), bf), vm((2, 2, B_ROWS, R), bf), vm((2, 2, SHARD_FF, R), bf),
            dma((G_STAGES, 25)), dma((G_STAGES, 8, 2)), dma((7,)), dma((8,)), dma((3,)), dma((4,)),
            dma((4,)), dma((4,)), dma((4,)), dma((2, 3)), dma((2, 2)), dma((4,)), dma((6,)),
        ],
        compiler_params=pltpu.CompilerParams(
            collective_id=0, has_side_effects=True, vmem_limit_bytes=60 * 2**20),
        name="forward",
    )(own, mod_in, cond_in, tokens, out_grad, ada, keep, gains, table)


R_STAGE, R_LONE = 64, 16
R_STAGES = ROWS_ALL // R_STAGE
R_PLANE = R_STAGE - R_LONE
R_MID = R_STAGE - 2 * R_LONE
X_RING, Y_RING, Z_RING = 8, 4, 6
D_STAGES = C_ROWS // R_STAGE
GU_STAGES = B_ROWS // R_STAGE


def backward_kernel(
    full, fi_in, si_in, fg_in, att_in, qkv_in, norm_in, stat_in, mixed_in, gu_in, hid_in,
    tokens, out_grad, mod, keep, gains, table,
    result_out, tokens_out, grads, pay_all,
    part, xin, yin, zin, fin, buf_a, buf_b, acc, after, att, sent, came, came_feed, result,
    wd, wb, wa, hid, gu, qkv, norm, stat, mixed, dqkv, gain_sum, payf, pay,
    xs, xr, ys, yr, zs, zr, fs, fr, es, er, ps, pr, ls, lw, x_free, y_free, z_free,
):
    x, c, z, y = place()
    t = z * 2 + y
    d = x * 2 + c
    y_side, x_side, core = at(x, c, z, 1 - y), at(1 - x, c, z, y), at(x, 1 - c, z, y)
    up, down = at(x, c, z + 1, y), at(x, c, z - 1, y)
    spot = x * 8 + t
    mates = []
    for k in range(1, 16):
        o = lax.rem(spot + k, 16)
        mates.append(((o // 8) * 2 + c, lax.rem(o, 8)))
    greet(mates + [core])

    loads = [
        pltpu.make_async_copy(fg_in, buf_a, ls.at[0]),
        pltpu.make_async_copy(si_in, buf_b, ls.at[1]),
        pltpu.make_async_copy(att_in, att, ls.at[2]),
    ]
    for cp in loads:
        cp.start()

    def base(g):
        return (R_STAGES - 1 - g) * R_STAGE

    def lone(g, side):
        return rows_at(base(g) + side * (R_STAGE - R_LONE), R_LONE)

    def plane(g):
        return rows_at(base(g) + x * R_LONE, R_PLANE)

    def side_y(side):
        return 1 - y if side == 0 else y

    def xcopy(g, side):
        yy = side_y(side)
        return remote(
            part.at[:, yy, lone(g, 1 - x)], xin.at[lax.rem(g, X_RING), :, yy], xs.at[g, side], xr.at[g, side], x_side)

    def ycopy(g):
        return remote(part.at[:, 1 - y, plane(g)], yin.at[lax.rem(g, Y_RING)], ys.at[g], yr.at[g], y_side)

    def zcopy(g, to_z, way):
        spot = to_z - (z + 1) if way == 0 else 4 - to_z
        return remote(
            part.at[to_z, y, plane(g)], zin.at[lax.rem(g, Z_RING), spot],
            zs.at[g, way, to_z], zr.at[g, way, to_z], up if way == 0 else down)

    def fcopy(g, what):
        if what == 0:
            return remote(part.at[z, y, lone(g, x)], grads.at[c, lone(g, x)], fs.at[g, 0], fr.at[g, 0], x_side)
        if what == 1:
            mid = rows_at(base(g) + R_LONE, R_MID)
            return remote(part.at[z, y, mid], fin.at[rows_at(g * R_MID, R_MID)], fs.at[g, 1], fr.at[g, 1], x_side)
        if what == 2:
            return remote(part.at[z, y, plane(g)], grads.at[c, plane(g)], fs.at[g, 2], fr.at[g, 2], core)
        return remote(grads.at[c, lone(g, 1 - x)], grads.at[c, lone(g, 1 - x)], fs.at[g, 3], fr.at[g, 3], core)

    def own_copy(g):
        return pltpu.make_async_copy(part.at[z, y, plane(g)], grads.at[c, plane(g)], fs.at[g, 4])

    def add(zz, yy, rows, size, piece):
        @pl.loop(0, size // 16)
        def _(i):
            a = rows_at(rows + i * 16, 16)
            part[zz, yy, a, :] = low(wide(part[zz, yy, a, :]) + wide(piece(rows_at(i * 16, 16))))

    def x_send(g, side):
        if side == 0:
            pl.when(g >= X_RING)(lambda: pl.semaphore_wait(x_free, 1))
        xcopy(g, side).start()

    def x_stage(g):
        b = lax.rem(g, X_RING)
        for side in (0, 1):
            yy = side_y(side)
            xcopy(g, side).wait_recv()

            @pl.loop(0, 4)
            def _(k):
                add(k, yy, base(g) + x * (R_STAGE - R_LONE), R_LONE, lambda r: xin[b, k, yy, r, :])

            if side == 0:
                pl.when(g >= Y_RING)(lambda: pl.semaphore_wait(y_free, 1))
                ycopy(g).start()
        pl.when(g + X_RING < R_STAGES)(
            lambda: pl.semaphore_signal(x_free, inc=1, device_id=x_side, device_id_type=MESH))

    def y_stage(g):
        b = lax.rem(g, Y_RING)
        ycopy(g).wait_recv()

        @pl.loop(0, 4)
        def _(k):
            add(k, y, base(g) + x * R_LONE, R_PLANE, lambda r: yin[b, k, r, :])

        pl.when(g + Y_RING < R_STAGES)(
            lambda: pl.semaphore_signal(y_free, inc=1, device_id=y_side, device_id_type=MESH))

    def take(g, way, to_z):
        b = lax.rem(g, Z_RING)
        spot = to_z - z if way == 0 else 4 - to_z
        remote(
            part.at[to_z, y, plane(g)], zin.at[b, spot], zs.at[g, way, to_z], zr.at[g, way, to_z], y_side).wait_recv()
        add(to_z, y, base(g) + x * R_LONE, R_PLANE, lambda r: zin[b, spot, r, :])

    def up_stage(g):
        pl.when(jnp.logical_and(g >= Z_RING, z < 3))(lambda: pl.semaphore_wait(z_free.at[0], 1))
        for j in (3, 2, 1):
            @pl.when(z + j <= 3)
            def _():
                pl.when(z > 0)(lambda: take(g, 0, z + j))
                zcopy(g, z + j, 0).start()

    def down_stage(g):
        pl.when(jnp.logical_and(g >= Z_RING, z > 0))(lambda: pl.semaphore_wait(z_free.at[1], 1))
        for j in (3, 2, 1):
            @pl.when(z >= j)
            def _():
                pl.when(z < 3)(lambda: take(g, 1, z - j))
                zcopy(g, z - j, 1).start()

    def own_stage(g):
        pl.when(z > 0)(lambda: take(g, 0, z))
        pl.when(z < 3)(lambda: take(g, 1, z))

        @pl.when(g + Z_RING < R_STAGES)
        def _():
            pl.when(z > 0)(
                lambda: pl.semaphore_signal(z_free.at[0], inc=1, device_id=down, device_id_type=MESH))
            pl.when(z < 3)(
                lambda: pl.semaphore_signal(z_free.at[1], inc=1, device_id=up, device_id_type=MESH))

        fcopy(g, 0).start()
        fcopy(g, 1).start()

    def f_stage(g):
        fcopy(g, 1).wait()
        mid = base(g) + R_LONE

        @pl.loop(0, R_MID // 16)
        def _(i):
            a = rows_at(mid + i * 16, 16)
            part[z, y, a, :] = low(wide(part[z, y, a, :]) + wide(fin[rows_at(g * R_MID + i * 16, 16), :]))

        own_copy(g).start()
        fcopy(g, 2).start()
        fcopy(g, 0).wait_recv()
        fcopy(g, 3).start()

    def service(i):
        def on(g, act):
            pl.when(jnp.logical_and(g >= 0, g < R_STAGES))(lambda: act(g))

        on(i, x_stage)
        on(i - 1, y_stage)
        on(i - 1 - z, up_stage)
        on(i - 4 + z, down_stage)
        on(i - 4, own_stage)
        on(i - 5, f_stage)

    def send_stages(first, last, side):
        @pl.loop(first, last)
        def _(g):
            x_send(g, side)

    def shard(k):
        return lax.rem(k, 4), jnp.where(k < 4, 1 - y, y)

    def slot(k):
        zz, yy = shard(k)
        return zz * 2 + yy

    def stream(pairs):
        def fetch(k):
            b = lax.rem(k, 2)
            return [pltpu.make_async_copy(src(slot(k)), buf.at[b], lw.at[n, b]) for src, buf, n in pairs]

        def begin(k):
            for cp in fetch(k):
                cp.start()

        def turn_to(k):
            for cp in fetch(k):
                cp.wait()
            pl.when(k < 7)(lambda: begin(k + 1))

        return begin, turn_to

    def mod_row(image, k):
        return mod[pl.ds(image * 8 + k, 1), :]

    def by_rows(act):
        for image in range(2):
            @pl.loop(0, PATCH // CHUNK)
            def _(i):
                act(image, rows_at(image * PATCH + i * CHUNK, CHUNK))

    def count(image, k, v):
        payf[pl.ds(image * 8 + k, 1), :] += jnp.sum(v, axis=0, keepdims=True)

    def clear(ref):
        @pl.loop(0, ref.shape[0] // 16)
        def _(i):
            ref[rows_at(i * 16, 16), :] = jnp.zeros((16, D), jnp.float32)

    def gather_sum(h, left, right):
        for image in range(2):
            cut = slice(image * PATCH, (image + 1) * PATCH)
            rows = slice(h * 512 + image * PATCH, h * 512 + (image + 1) * PATCH)
            acc[rows, :] += tn(left[:, cut], right)

    def share_half(number, landing):
        @pl.loop(0, 512 // CHUNK)
        def _(i):
            sent[rows_at(i * CHUNK, CHUNK), :] = low(acc[rows_at(512 + i * CHUNK, CHUNK), :])

        cp = remote(sent, landing, es.at[number], er.at[number], core)
        cp.start()
        return cp

    payf[...] = jnp.zeros_like(payf)
    gain_sum[...] = jnp.zeros_like(gain_sum)
    clear(acc)
    begin_d, turn_d = stream([(lambda s: hid_in.at[s], hid, 0)])
    begin_g, turn_g = stream([
        (lambda s: full.at[s, pl.ds(A_ROWS + B_ROWS, C_ROWS)], wd, 1),
        (lambda s: full.at[s, pl.ds(A_ROWS, B_ROWS)], wb, 2),
        (lambda s: gu_in.at[s], gu, 3),
    ])
    begin_a, turn_a = stream([
        (lambda s: full.at[s, pl.ds(0, A_ROWS)], wa, 4),
        (lambda s: qkv_in.at[s], qkv, 5),
        (lambda s: norm_in.at[s], norm, 6),
        (lambda s: stat_in.at[s], stat, 7),
        (lambda s: mixed_in.at[:, rows_at(s * HEAD, HEAD)], mixed, 8),
    ])
    begin_f, turn_f = stream([
        (lambda s: hid_in.at[s], hid, 0),
        (lambda s: full.at[s, pl.ds(A_ROWS + B_ROWS, C_ROWS)], wd, 1),
    ])
    begin_d(0)
    begin_g(0)
    loads[0].wait()

    @pl.loop(0, 8)
    def _(k):
        b = lax.rem(k, 2)
        zz, yy = shard(k)
        turn_d(k)
        grad = nn(hid[b, 0], buf_a[0]) + nn(hid[b, 1], buf_a[1])
        part[zz, yy, A_ROWS + B_ROWS :, :] = low(grad)
        pl.when(k == 3)(lambda: send_stages(0, D_STAGES, 0))

    send_stages(0, D_STAGES, 1)
    loads[1].wait()

    @pl.loop(0, 8)
    def _(k):
        b = lax.rem(k, 2)
        zz, yy = shard(k)
        turn_g(k)
        grads_here = []
        for h in range(2):
            hg = nt(wd[b], buf_a[h])
            g, u = wide(gu[b, h, :SHARD_FF]), wide(gu[b, h, SHARD_FF:])
            sig = 1.0 / (1.0 + jnp.exp(-g))
            act = g * sig
            both = low(jnp.concatenate([hg * u * (sig + act * (1.0 - sig)), hg * act], axis=0))
            grads_here.append(both)
            gather_sum(h, both, wb[b])
        part[zz, yy, A_ROWS : A_ROWS + B_ROWS, :] = low(
            nn(grads_here[0], buf_b[0]) + nn(grads_here[1], buf_b[1]))

        @pl.when(k == 3)
        def _():
            service(0)
            send_stages(D_STAGES, 6, 0)

    send_stages(D_STAGES, 6, 1)
    share_second = share_half(0, came)
    service(1)
    begin_a(0)
    load_fi = pltpu.make_async_copy(fi_in, buf_a, ls.at[0])
    load_fi.start()
    send_stages(6, 8, 0)
    send_stages(6, 8, 1)
    loads[2].wait()
    share_second.wait_recv()

    def after_rows(image, rows):
        a = att[rows, :]
        v = wide(tokens[rows, :]) + mod_row(image, 2) * a
        inv = lax.rsqrt(jnp.mean(v * v, axis=-1, keepdims=True) + epsilon)
        n = v * inv
        sg = acc[rows, :] + wide(came[rows, :])
        dn = sg * (1.0 + mod_row(image, 4))
        ag = wide(out_grad[rows, :]) + inv * (dn - n * jnp.mean(dn * n, axis=-1, keepdims=True))
        after[rows, :] = ag
        buf_b[0, rows, :] = low(ag * mod_row(image, 2))
        count(image, 2, ag * a)
        count(image, 3, sg)
        count(image, 4, sg * n)

    by_rows(after_rows)
    share_ag = remote(buf_b.at[0], buf_b.at[1], es.at[1], er.at[1], core)
    share_ag.start()
    service(2)
    clear(acc)
    load_fi.wait()
    share_ag.wait_recv()

    @pl.loop(0, 8)
    def _(k):
        b = lax.rem(k, 2)
        zz, yy = shard(k)
        turn_a(k)
        cos, sin = table[:HALF, :PATCH], table[HALF:, :PATCH]
        part[zz, yy, 3 * HEAD : A_ROWS, :] = low(nn(mixed[b, 0], buf_b[0]) + nn(mixed[b, 1], buf_b[1]))
        for h in range(2):
            mg_all = low(nt(wa[b, 3 * HEAD :], buf_b[h]))
            for image in range(2):
                cut = slice(image * PATCH, (image + 1) * PATCH)
                q, kk, v = [qkv[b, h, i * HEAD : (i + 1) * HEAD, cut] for i in range(3)]
                mg = mg_all[:, cut]
                p = jnp.exp(tn(kk, q) * FACTOR - stat[b, h, 2:3, cut])
                dqkv[h, 2 * HEAD :, cut] = low(nt(mg, low(p)))
                pg = tn(v, mg)
                sg = low(p * (pg - jnp.sum(p * pg, axis=0, keepdims=True)))
                backs = (nn(kk, sg), nt(q, sg))
                for i in range(2):
                    rows = slice(i * HEAD, (i + 1) * HEAD)
                    back = turn(backs[i] * FACTOR, cos, -sin)
                    n = wide(norm[b, h, rows, cut])
                    gain_sum[rows, :] += back * n
                    dn = back * gains[rows, :1]
                    mean = jnp.sum(dn * n, axis=0, keepdims=True) * (1.0 / HD)
                    dqkv[h, rows, cut] = low(stat[b, h, i : i + 1, cut] * (dn - n * mean))
            gather_sum(h, dqkv[h], wa[b, : 3 * HEAD])
        part[zz, yy, : 3 * HEAD, :] = low(nn(dqkv[0], buf_a[0]) + nn(dqkv[1], buf_a[1]))
        ones = jnp.ones((8, 512), jnp.bfloat16)
        sums = nt(ones, dqkv[0]) + nt(ones, dqkv[1])
        s = slot(k)
        payf[pl.ds(6 + s // 4, 1), pl.ds(pl.multiple_of(lax.rem(s, 4) * 256, 128), 3 * HEAD)] = sums[:1]

        @pl.when(lax.rem(k, 3) == 2)
        def _():
            service(3 + k // 3)

        pl.when(k == 3)(lambda: send_stages(8, 9, 0))

    send_stages(8, 9, 1)
    share_second.wait_send()
    begin_f(0)
    share_first = share_half(2, came)
    service(5)
    send_stages(9, 12, 0)
    send_stages(9, 12, 1)
    share_first.wait_recv()

    def first_rows(image, rows):
        v = wide(tokens[rows, :])
        inv = lax.rsqrt(jnp.mean(v * v, axis=-1, keepdims=True) + epsilon)
        n = v * inv
        fgd = acc[rows, :] + wide(came[rows, :])
        dn = fgd * (1.0 + mod_row(image, 1))
        count(image, 0, fgd)
        count(image, 1, fgd * n)
        acc[rows, :] = after[rows, :] + inv * (dn - n * jnp.mean(dn * n, axis=-1, keepdims=True))

    by_rows(first_rows)
    save_tokens = pltpu.make_async_copy(acc.at[pl.ds(0, 512)], tokens_out, ls.at[3])
    save_tokens.start()
    service(6)
    save_tokens.wait()
    clear(acc)

    @pl.loop(0, 8)
    def _(k):
        b = lax.rem(k, 2)
        turn_f(k)
        for h in range(2):
            gather_sum(h, hid[b, h], wd[b])

    share_first.wait_send()
    share_feed = share_half(3, came_feed)
    service(7)
    send_stages(12, 14, 0)
    send_stages(12, 14, 1)
    share_feed.wait_recv()

    def result_rows(image, rows):
        feed = acc[rows, :] + wide(came_feed[rows, :])
        v = wide(tokens[rows, :]) + mod_row(image, 2) * att[rows, :]
        result[rows, :] = low(v + mod_row(image, 5) * feed)
        count(image, 5, wide(out_grad[rows, :]) * feed)

    by_rows(result_rows)
    save_result = pltpu.make_async_copy(result, result_out, ls.at[4])
    save_result.start()
    lanes = gain_sum[:, :128] + gain_sum[:, 128:]
    lanes = jnp.concatenate([lanes, jnp.zeros((96, 128), jnp.float32)], axis=0)
    payf[14:15, :256] = jnp.sum(jnp.transpose(lanes), axis=0, keepdims=True)
    pay[...] = low(payf[...] * keep[...])
    me = d * 8 + t
    keep_pay = pltpu.make_async_copy(pay, pay_all.at[me], ls.at[5])
    keep_pay.start()
    pays = [remote(pay, pay_all.at[me], ps.at[k], pr.at[k], o) for k, o in enumerate(mates)]
    for cp in pays:
        cp.start()

    @pl.loop(8, 14)
    def _(i):
        service(i)

    keep_pay.wait()
    for cp in pays:
        cp.wait()
    swaps = []
    for xx in range(2):
        rows = pl.ds(pl.multiple_of((xx * 2 + c) * 8, 8), 8)
        swaps.append(remote(pay_all.at[rows], pay_all.at[rows], ps.at[15 + xx], pr.at[15 + xx], core))
        swaps[-1].start()

    @pl.loop(14, R_STAGES + 5)
    def _(i):
        service(i)

    @pl.loop(0, R_STAGES)
    def _(g):
        xcopy(g, 0).wait_send()
        xcopy(g, 1).wait_send()
        ycopy(g).wait_send()
        for j in (3, 2, 1):
            pl.when(z + j <= 3)(lambda: zcopy(g, z + j, 0).wait_send())
            pl.when(z >= j)(lambda: zcopy(g, z - j, 1).wait_send())
        fcopy(g, 0).wait_send()
        own_copy(g).wait()
        fcopy(g, 2).wait()
        fcopy(g, 3).wait()

    for cp in swaps:
        cp.wait()
    share_ag.wait_send()
    share_feed.wait_send()
    save_result.wait()


def backward(saved, tokens, out_grad, mod, keep, gains, table):
    dma = pltpu.SemaphoreType.DMA
    regular = pltpu.SemaphoreType.REGULAR
    vm = pltpu.VMEM
    bf, f32 = jnp.bfloat16, jnp.float32
    anywhere = pl.BlockSpec(memory_space=pl.ANY)
    inside = pl.BlockSpec(memory_space=pltpu.VMEM)
    R = tokens.shape[0]
    outs = [((R, D), bf), ((R, D), f32), ((2, ROWS_ALL, D), bf), ((32, PAY, D), bf)]
    return pl.pallas_call(
        backward_kernel,
        out_shape=tuple(jax.ShapeDtypeStruct(s, e) for s, e in outs),
        in_specs=[anywhere] * len(saved) + [inside] * 6,
        out_specs=(anywhere,) * len(outs),
        scratch_shapes=[
            vm((4, 2, ROWS_ALL, D), bf), vm((X_RING, 4, 2, R_LONE, D), bf), vm((Y_RING, 4, R_PLANE, D), bf),
            vm((Z_RING, 5, R_PLANE, D), bf), vm((R_STAGES * R_MID, D), bf),
            vm((2, R, D), bf), vm((2, R, D), bf), vm((2 * R, D), f32), vm((R, D), f32), vm((R, D), f32),
            vm((R, D), bf), vm((R, D), bf), vm((R, D), bf), vm((R, D), bf),
            vm((2, C_ROWS, D), bf), vm((2, B_ROWS, D), bf), vm((2, A_ROWS, D), bf),
            vm((2, 2, SHARD_FF, R), bf), vm((2, 2, B_ROWS, R), bf), vm((2, 2, 3 * HEAD, R), bf),
            vm((2, 2, 2 * HEAD, R), bf), vm((2, 2, 8, R), f32), vm((2, 2, HEAD, R), bf),
            vm((2, 3 * HEAD, R), bf), vm((2 * HEAD, PATCH), f32), vm((16, D), f32), vm((16, D), bf),
            dma((R_STAGES, 2)), dma((R_STAGES, 2)), dma((R_STAGES,)), dma((R_STAGES,)),
            dma((R_STAGES, 2, 4)), dma((R_STAGES, 2, 4)), dma((R_STAGES, 5)), dma((R_STAGES, 4)),
            dma((4,)), dma((4,)), dma((17,)), dma((17,)), dma((6,)), dma((9, 2)),
            regular, regular, regular((2,)),
        ],
        compiler_params=pltpu.CompilerParams(
            collective_id=1, has_side_effects=True, vmem_limit_bytes=62 * 2**20),
        name="backward",
    )(*saved, tokens, out_grad, mod, keep, gains, table)


def normalize(vectors, axis=-1, count=None):
    count = count or vectors.shape[axis]
    inverse = lax.rsqrt(jnp.sum(vectors * vectors, axis=axis, keepdims=True) / count + epsilon)
    return (vectors * inverse, inverse)


def normalize_back(grad, normed, inverse, axis=-1, count=None):
    count = count or grad.shape[axis]
    return inverse * (grad - normed * (jnp.sum(grad * normed, axis=axis, keepdims=True) / count))


def silu_slope(values):
    sigma = jax.nn.sigmoid(values)
    return sigma * (1.0 + values * (1.0 - sigma))


def pair_rows(heads):
    lead, n = heads.shape[:-2], heads.shape[-1]
    split = heads.reshape(lead + (2, 2, 18, n))
    split = jnp.swapaxes(split, -4, -3).reshape(lead + (2, 36, n))
    return jnp.pad(split, [(0, 0)] * len(lead) + [(0, 0), (0, 4), (0, 0)]).reshape(lead + (HEAD, n))


def unpair_rows(rows):
    lead, n = rows.shape[:-2], rows.shape[-1]
    split = rows.reshape(lead + (2, HALF, n))[..., :36, :].reshape(lead + (2, 2, 18, n))
    return jnp.swapaxes(split, -4, -3).reshape(lead + (HD, n))


def pad_rows(rows):
    return jnp.pad(rows, [(0, 0)] * (rows.ndim - 2) + [(0, 8), (0, 0)])


def pair_tables():
    pairs = HD // 4
    theta = np.exp(-math.log(100.0) * np.arange(pairs, dtype=np.float32) / pairs)
    spot = np.arange(PATCH)
    angle = np.concatenate([theta[:, None] * (spot // GRID)[None], theta[:, None] * (spot % GRID)[None]])
    pad = ((0, HALF - 36), (0, 0))
    return (
        np.pad(np.cos(angle), pad).astype(np.float32),
        np.pad(np.sin(angle), pad).astype(np.float32),
    )


def rotate_pairs(v, cos, sin):
    a, b = v[..., :HALF, :], v[..., HALF:, :]
    return jnp.concatenate([a * cos - b * sin, b * cos + a * sin], axis=-2)


def pack_weights(qkv_weight, out_weight, gate_up_weight, down_weight, c):
    heads = lax.dynamic_slice_in_dim(qkv_weight, c * HD, HD, 2).transpose(1, 2, 0)
    qk = pair_rows(heads[:2]).reshape(2 * HEAD, D)
    v = pad_rows(heads[2])
    o = pad_rows(lax.dynamic_slice_in_dim(out_weight, c * HD, HD, 0))
    gu = lax.dynamic_slice_in_dim(gate_up_weight, c * SHARD_FF, SHARD_FF, 2)
    gu = gu.transpose(1, 2, 0).reshape(B_ROWS, D)
    dn = lax.dynamic_slice_in_dim(down_weight, c * SHARD_FF, SHARD_FF, 0)
    return jnp.concatenate([qk, v, o, gu, dn], axis=0)


def unpack_grads(both):
    both = both.astype(jnp.float32)
    qk = unpair_rows(both[:, : 2 * HEAD].reshape(2, 2, HEAD, D))
    v = both[:, 2 * HEAD : 2 * HEAD + HD].reshape(2, 1, HD, D)
    qkv = jnp.concatenate([qk, v], axis=1).transpose(3, 1, 0, 2).reshape(D, 3, 2 * HD)
    o = both[:, 3 * HEAD : 3 * HEAD + HD].reshape(2 * HD, D)
    gu = both[:, A_ROWS : A_ROWS + B_ROWS].reshape(2, 2, SHARD_FF, D)
    gu = gu.transpose(3, 1, 0, 2).reshape(D, 2, 2 * SHARD_FF)
    dn = both[:, A_ROWS + B_ROWS :].reshape(2 * SHARD_FF, D)
    return qkv, o, gu, dn


def fast(
    tokens, labels, timesteps, image_counts, class_table, ada_weight, ada_bias,
    qkv_weight, qkv_bias, qk_scale, out_weight, gate_up_weight, down_weight, out_grad,
):
    dot = lambda s, a, b: jnp.einsum(s, a, b, preferred_element_type=jnp.float32)
    t = lax.axis_index("tensor")
    c = lax.axis_index("dp") % 2
    own = pack_weights(qkv_weight, out_weight, gate_up_weight, down_weight, c)
    images = labels.shape[0]
    columns_here = class_table.shape[1]
    column = t * columns_here + jnp.arange(columns_here)
    half_width = D // 2
    frequency = jnp.exp(-math.log(10000.0) * (column % half_width).astype(jnp.float32) / half_width)
    angles = timesteps.astype(jnp.float32)[:, None] * frequency[None, :]
    time_embed = jnp.where(column[None, :] < half_width, jnp.cos(angles), jnp.sin(angles))
    classes = jnp.arange(class_table.shape[0])
    condition = dot("in,nc->ic", low(labels[:, None] == classes[None, :]), class_table) + time_embed
    mod_part = dot("ic,ckd->ikd", low(jax.nn.silu(condition)), ada_weight)
    heads = qkv_bias.reshape(3, 2, HD).swapaxes(0, 1)[..., None]
    bias_row = jnp.concatenate([pair_rows(heads[:, :2]).reshape(2, -1), pad_rows(heads[:, 2])[..., 0]], axis=1)
    bias_row = jnp.pad(bias_row, ((0, 0), (0, 16))).reshape(1, 1, -1)
    bias_row = jnp.pad(bias_row, ((0, 0), (0, 0), (0, D - bias_row.size)))
    bias_row = jnp.broadcast_to(bias_row, (images, 1, D))
    mod_part = jnp.concatenate([low(mod_part), bias_row, jnp.zeros_like(bias_row)], axis=1)
    cond_part = jnp.concatenate(
        [condition, labels.astype(jnp.float32)[:, None], jnp.zeros((images, 256 - columns_here - 1), jnp.float32)], axis=1)
    mod_images = images // 8
    kept = (t * mod_images + jnp.arange(mod_images) < image_counts[0]).astype(jnp.float32)
    ada = jnp.pad(ada_bias.astype(jnp.float32), ((0, 2), (0, 0)))
    ada = jnp.tile(ada, (mod_images, 1))
    gate_rows = jnp.array([0, 0, 1, 0, 0, 1, 0, 0], jnp.float32)
    keep = jnp.where(gate_rows[None, :] > 0, kept[:, None], 1.0).reshape(-1, 1)
    keep = jnp.broadcast_to(keep, ada.shape)
    gain_rows = jnp.broadcast_to(pair_rows(qk_scale.astype(jnp.float32)[..., None]).reshape(2 * HEAD, 1), (2 * HEAD, 128))
    cos, sin = pair_tables()
    table = np.tile(np.concatenate([cos, sin]), (1, tokens.shape[0] // PATCH))
    (weights, cond_all, mod, first_in, second_in, feed_grad, attention, qkv_t, norm_t, stat_t, mixed, gu_t, hidden) = forward(
        own, mod_part.reshape(8, images, D), cond_part, tokens, out_grad, ada, keep, gain_rows, table)
    cond_all = cond_all.reshape(4 * images, 256)
    condition = cond_all[:, :columns_here]
    labels_all = cond_all[:, columns_here].astype(jnp.int32)
    chosen = low(labels_all[:, None] == classes[None, :])
    cond_act = low(jax.nn.silu(condition))
    first_image = lax.axis_index("dp") * images
    saved = (weights, first_in, second_in, feed_grad, attention, qkv_t, norm_t, stat_t, mixed, gu_t, hidden)
    result, tokens_grad, summed, pay_all = backward(saved, tokens, out_grad, mod, keep, gain_rows, table)
    qkv_weight_grad, out_weight_grad, gate_up_grad, down_grad = unpack_grads(summed)
    pay_all = pay_all.reshape(32, mod_images, 8, D)
    mod_grad = pay_all[:, :, :6].reshape(-1, 6, D)
    bias_all = pay_all[:, 0, 6:, : 4 * 256].astype(jnp.float32).reshape(32, 8, 256)[..., : 3 * HEAD]
    scale_all = pay_all[:, 1, 6, : 2 * HEAD].astype(jnp.float32).reshape(32, 2, HEAD)
    qk_scale_grad = unpair_rows(jnp.sum(scale_all, axis=0)[..., None])[..., 0]
    bias_all = lax.dynamic_index_in_dim(bias_all, t, 1, keepdims=False).reshape(2, 2, 8, 3, HEAD)
    bias_sum = jnp.sum(bias_all, axis=(0, 2))
    qk_bias = unpair_rows(bias_sum[:, :2, :, None])[..., 0]
    qkv_bias_grad = jnp.concatenate([qk_bias, bias_sum[:, 2:, :HD]], axis=1).transpose(1, 0, 2).reshape(3, 2 * HD)

    ada_weight_grad = dot("ic,ikd->ckd", cond_act, mod_grad)
    ada_bias_grad = jnp.sum(mod_grad.astype(jnp.float32), axis=0)
    act_grad = dot("ikd,ckd->ic", mod_grad, ada_weight)
    cond_grad_all = act_grad * silu_slope(condition)
    table_grad = jnp.dot(chosen.astype(jnp.float32).T, cond_grad_all, precision=HIGH)
    cond_grad = lax.dynamic_slice_in_dim(cond_grad_all, first_image, images, 0)
    return (
        result, tokens_grad, cond_grad, table_grad, ada_weight_grad, ada_bias_grad,
        qkv_weight_grad, qkv_bias_grad, qk_scale_grad, out_weight_grad, gate_up_grad, down_grad,
    )


def rope_tables(count):
    pairs = HD // 4
    theta = jnp.exp(-math.log(100.0) * jnp.arange(pairs, dtype=jnp.float32) / pairs)
    place = jnp.arange(count) % PATCH
    row_angle = (place // GRID).astype(jnp.float32)[:, None] * theta
    col_angle = (place % GRID).astype(jnp.float32)[:, None] * theta
    return ((jnp.cos(row_angle), jnp.sin(row_angle)), (jnp.cos(col_angle), jnp.sin(col_angle)))


def rotate_part(segment, cosine, sine, direction):
    half_len = segment.shape[-1] // 2
    first, second = (segment[..., :half_len], segment[..., half_len:])
    cosine = cosine[:, None, :]
    sine = direction * sine[:, None, :]
    return jnp.concatenate(
        [first * cosine - second * sine, second * cosine + first * sine], axis=-1
    )


def rotate(vectors, tables, direction):
    half_len = vectors.shape[-1] // 2
    return jnp.concatenate(
        [
            rotate_part(vectors[..., :half_len], tables[0][0], tables[0][1], direction),
            rotate_part(vectors[..., half_len:], tables[1][0], tables[1][1], direction),
        ],
        axis=-1,
    )


def general(
    tokens,
    labels,
    timesteps,
    image_counts,
    class_table,
    ada_weight,
    ada_bias,
    qkv_weight,
    qkv_bias,
    qk_scale,
    out_weight,
    gate_up_weight,
    down_weight,
    out_grad,
):
    width = tokens.shape[1]
    local_rows = tokens.shape[0]
    members = lax.axis_size("tensor")
    place = lax.axis_index("tensor")
    images = labels.shape[0]
    all_rows = local_rows * members
    columns_here = class_table.shape[1]
    heads_here = columns_here // HD
    column = place * columns_here + jnp.arange(columns_here)
    half_width = width // 2
    frequency = jnp.exp(-math.log(10000.0) * (column % half_width).astype(jnp.float32) / half_width)
    angles = timesteps.astype(jnp.float32)[:, None] * frequency[None, :]
    time_embed = jnp.where(column[None, :] < half_width, jnp.cos(angles), jnp.sin(angles))
    chosen = (labels[:, None] == jnp.arange(class_table.shape[0])[None, :]).astype(jnp.bfloat16)
    condition = jnp.dot(chosen, class_table, preferred_element_type=jnp.float32) + time_embed
    cond_act = jax.nn.silu(condition).astype(jnp.bfloat16)
    mod_part = jnp.einsum("ic,ckd->ikd", cond_act, ada_weight, preferred_element_type=jnp.float32)
    modulation = lax.psum(mod_part, "tensor") + ada_bias.astype(jnp.float32)
    row_index = place * local_rows + jnp.arange(local_rows)
    row_image = row_index // PATCH
    selector = (row_image[:, None] == jnp.arange(images)[None, :]).astype(jnp.float32)
    mod_rows = jnp.dot(selector, modulation.reshape(images, 6 * width), precision=HIGH).reshape(
        local_rows, 6, width
    )
    kept = (row_image < image_counts[0]).astype(jnp.float32)[:, None]
    shift_one, scale_one, gate_one, shift_two, scale_two, gate_two = [
        mod_rows[:, index] for index in range(6)
    ]
    tokens_f = tokens.astype(jnp.float32)
    first_norm, first_inverse = normalize(tokens_f)
    first_in = (first_norm * (1.0 + scale_one) + shift_one).astype(jnp.bfloat16)
    first_all = lax.all_gather(first_in, "tensor", axis=0, tiled=True)
    qkv = jnp.einsum(
        "nd,dkc->nkc", first_all, qkv_weight, preferred_element_type=jnp.float32
    ) + qkv_bias.astype(jnp.float32)
    head_view = qkv.reshape(all_rows, 3, heads_here, HD)
    tables = rope_tables(all_rows)
    qk_gains = qk_scale.astype(jnp.float32)
    query_normed, query_inverse = normalize(head_view[:, 0])
    key_normed, key_inverse = normalize(head_view[:, 1])
    block_shape = (all_rows // PATCH, PATCH, heads_here, HD)
    queries = (
        rotate(query_normed * qk_gains[0], tables, 1.0).astype(jnp.bfloat16).reshape(block_shape)
    )
    keys_rot = (
        rotate(key_normed * qk_gains[1], tables, 1.0).astype(jnp.bfloat16).reshape(block_shape)
    )
    values = head_view[:, 2].astype(jnp.bfloat16).reshape(block_shape)
    factor = HD ** (-0.5)
    scores = (
        jnp.einsum("iqhe,ikhe->ihqk", queries, keys_rot, preferred_element_type=jnp.float32)
        * factor
    )
    row_max = jnp.max(scores, axis=-1, keepdims=True)
    exponent = jnp.exp(scores - row_max)
    totals = jnp.sum(exponent, axis=-1, keepdims=True)
    logsum = row_max + jnp.log(totals)
    probability = (exponent / totals).astype(jnp.bfloat16)
    mixed_heads = (
        jnp.einsum("ihqk,ikhe->iqhe", probability, values, preferred_element_type=jnp.float32)
        .reshape(all_rows, columns_here)
        .astype(jnp.bfloat16)
    )
    attention = lax.psum_scatter(
        jnp.dot(mixed_heads, out_weight, preferred_element_type=jnp.float32).astype(jnp.bfloat16),
        "tensor",
        scatter_dimension=0,
        tiled=True,
    ).astype(jnp.float32)
    after_attn = tokens_f + kept * gate_one * attention
    second_norm, second_inverse = normalize(after_attn)
    second_in = (second_norm * (1.0 + scale_two) + shift_two).astype(jnp.bfloat16)
    second_all = lax.all_gather(second_in, "tensor", axis=0, tiled=True)
    gate_up = jnp.einsum(
        "nd,dkf->nkf", second_all, gate_up_weight, preferred_element_type=jnp.float32
    )
    gate_value, up_value = (gate_up[:, 0], gate_up[:, 1])
    activated = jax.nn.silu(gate_value)
    hidden = (activated * up_value).astype(jnp.bfloat16)
    feed = lax.psum_scatter(
        jnp.dot(hidden, down_weight, preferred_element_type=jnp.float32).astype(jnp.bfloat16),
        "tensor",
        scatter_dimension=0,
        tiled=True,
    ).astype(jnp.float32)
    result = (after_attn + kept * gate_two * feed).astype(jnp.bfloat16)
    grad_out = out_grad.astype(jnp.float32)
    feed_grad = (grad_out * kept * gate_two).astype(jnp.bfloat16)
    gate_two_grad = grad_out * kept * feed
    feed_grad_all = lax.all_gather(feed_grad, "tensor", axis=0, tiled=True)
    hidden_grad = jnp.einsum(
        "nd,fd->nf", feed_grad_all, down_weight, preferred_element_type=jnp.float32
    )
    down_grad = jnp.einsum("nf,nd->fd", hidden, feed_grad_all, preferred_element_type=jnp.float32)
    gate_grad = hidden_grad * up_value * silu_slope(gate_value)
    up_grad = hidden_grad * activated
    gu_grad = jnp.stack([gate_grad, up_grad], axis=1).astype(jnp.bfloat16)
    gate_up_grad = jnp.einsum(
        "nd,nkf->dkf", second_all, gu_grad, preferred_element_type=jnp.float32
    )
    second_grad = lax.psum_scatter(
        jnp.einsum(
            "nkf,dkf->nd", gu_grad, gate_up_weight, preferred_element_type=jnp.float32
        ).astype(jnp.bfloat16),
        "tensor",
        scatter_dimension=0,
        tiled=True,
    ).astype(jnp.float32)
    after_grad = grad_out + normalize_back(
        second_grad * (1.0 + scale_two), second_norm, second_inverse
    )
    attention_grad = (after_grad * kept * gate_one).astype(jnp.bfloat16)
    gate_one_grad = after_grad * kept * attention
    attention_grad_all = lax.all_gather(attention_grad, "tensor", axis=0, tiled=True)
    mixed_grad = jnp.einsum(
        "nd,cd->nc", attention_grad_all, out_weight, preferred_element_type=jnp.float32
    ).astype(jnp.bfloat16)
    out_weight_grad = jnp.einsum(
        "nc,nd->cd", mixed_heads, attention_grad_all, preferred_element_type=jnp.float32
    )
    scores_again = (
        jnp.einsum("iqhe,ikhe->ihqk", queries, keys_rot, preferred_element_type=jnp.float32)
        * factor
    )
    prob_again = jnp.exp(scores_again - logsum)
    mixed_blocks = mixed_grad.reshape(block_shape)
    values_grad = jnp.einsum(
        "ihqk,iqhe->ikhe",
        prob_again.astype(jnp.bfloat16),
        mixed_blocks,
        preferred_element_type=jnp.float32,
    )
    prob_grad = jnp.einsum(
        "iqhe,ikhe->ihqk", mixed_blocks, values, preferred_element_type=jnp.float32
    )
    score_grad = (
        prob_again * (prob_grad - jnp.sum(prob_again * prob_grad, axis=-1, keepdims=True))
    ).astype(jnp.bfloat16)
    queries_grad = (
        jnp.einsum("ihqk,ikhe->iqhe", score_grad, keys_rot, preferred_element_type=jnp.float32)
        * factor
    )
    keys_grad = (
        jnp.einsum("ihqk,iqhe->ikhe", score_grad, queries, preferred_element_type=jnp.float32)
        * factor
    )
    query_back = rotate(queries_grad.reshape(all_rows, heads_here, HD), tables, -1.0)
    key_back = rotate(keys_grad.reshape(all_rows, heads_here, HD), tables, -1.0)
    scale_part = jnp.stack(
        [
            jnp.sum(query_back * query_normed, axis=(0, 1)),
            jnp.sum(key_back * key_normed, axis=(0, 1)),
        ]
    )
    query_raw = normalize_back(query_back * qk_gains[0], query_normed, query_inverse)
    key_raw = normalize_back(key_back * qk_gains[1], key_normed, key_inverse)
    qkv_grad = (
        jnp.stack([query_raw, key_raw, values_grad.reshape(all_rows, heads_here, HD)], axis=1)
        .reshape(all_rows, 3, columns_here)
        .astype(jnp.bfloat16)
    )
    qkv_weight_grad = jnp.einsum(
        "nd,nkc->dkc", first_all, qkv_grad, preferred_element_type=jnp.float32
    )
    qkv_bias_grad = jnp.sum(qkv_grad.astype(jnp.float32), axis=0)
    first_grad = lax.psum_scatter(
        jnp.einsum("nkc,dkc->nd", qkv_grad, qkv_weight, preferred_element_type=jnp.float32).astype(
            jnp.bfloat16
        ),
        "tensor",
        scatter_dimension=0,
        tiled=True,
    ).astype(jnp.float32)
    tokens_grad = after_grad + normalize_back(
        first_grad * (1.0 + scale_one), first_norm, first_inverse
    )
    row_mod_grad = jnp.stack(
        [
            first_grad,
            first_grad * first_norm,
            gate_one_grad,
            second_grad,
            second_grad * second_norm,
            gate_two_grad,
        ],
        axis=1,
    ).reshape(local_rows, 6 * width)
    mod_grad_part = jnp.dot(selector.T, row_mod_grad, precision=HIGH).reshape(images, 6, width)
    mod_grad, scale_grad = (
        lax.psum(mod_grad_part.astype(jnp.bfloat16), "tensor").astype(jnp.float32),
        lax.psum(scale_part.astype(jnp.bfloat16), "tensor").astype(jnp.float32),
    )
    mod_grad_low = mod_grad.astype(jnp.bfloat16)
    ada_weight_grad = jnp.einsum(
        "ic,ikd->ckd", cond_act, mod_grad_low, preferred_element_type=jnp.float32
    )
    ada_bias_grad = jnp.sum(mod_grad_low.astype(jnp.float32), axis=0)
    act_grad = jnp.einsum(
        "ikd,ckd->ic", mod_grad_low, ada_weight, preferred_element_type=jnp.float32
    )
    cond_grad = act_grad * silu_slope(condition)
    table_grad = jnp.dot(chosen.astype(jnp.float32).T, cond_grad, precision=HIGH)
    summed = (
        lax.psum(table_grad.astype(jnp.bfloat16), "dp").astype(jnp.float32),
        lax.psum(ada_weight_grad.astype(jnp.bfloat16), "dp").astype(jnp.float32),
        lax.psum(ada_bias_grad.astype(jnp.bfloat16), "dp").astype(jnp.float32),
        lax.psum(qkv_weight_grad.astype(jnp.bfloat16), "dp").astype(jnp.float32),
        lax.psum(qkv_bias_grad.astype(jnp.bfloat16), "dp").astype(jnp.float32),
        lax.psum(scale_grad.astype(jnp.bfloat16), "dp").astype(jnp.float32),
        lax.psum(out_weight_grad.astype(jnp.bfloat16), "dp").astype(jnp.float32),
        lax.psum(gate_up_grad.astype(jnp.bfloat16), "dp").astype(jnp.float32),
        lax.psum(down_grad.astype(jnp.bfloat16), "dp").astype(jnp.float32),
    )
    return (result, tokens_grad, cond_grad) + tuple(summed)


def solution(mesh):
    placed = (
        P(("dp", "tensor"), None),
        P("dp"),
        P("dp"),
        P("dp"),
        P(None, "tensor"),
        P("tensor", None, None),
        P(),
        P(None, None, "tensor"),
        P(None, "tensor"),
        P(),
        P("tensor", None),
        P(None, None, "tensor"),
        P("tensor", None),
        P(("dp", "tensor"), None),
    )
    plain = mesh.shape["dp"] != 4 or mesh.shape["tensor"] != 8
    return jax.shard_map(
        general if plain else fast,
        mesh=mesh,
        in_specs=placed,
        out_specs=(
            P(("dp", "tensor"), None),
            P(("dp", "tensor"), None),
            P("dp", "tensor"),
            P(None, "tensor"),
            P("tensor", None, None),
            P(),
            P(None, None, "tensor"),
            P(None, "tensor"),
            P(),
            P("tensor", None),
            P(None, None, "tensor"),
            P("tensor", None),
        ),
        check_vma=False,
    )
```

```python
import math

import jax
import jax.numpy as jnp
import numpy as np
from jax import lax
from jax.experimental import pallas as pl
from jax.experimental.pallas import tpu as pltpu
from jax.sharding import PartitionSpec as P

HD = 72
GRID = 16
PATCH = 256
HIGH = lax.Precision.HIGHEST
MESH = pl.DeviceIdType.MESH
epsilon = 1e-06
D = 1152

QKV = 3 * HD
A_ROWS = 4 * HD
SHARD_FF = 192
B_ROWS = 2 * SHARD_FF
C_ROWS = SHARD_FF
ROWS_ALL = A_ROWS + B_ROWS + C_ROWS
HEAD = 80
O_FIRST = A_ROWS - HEAD
QKV_ROWS = 224
CHUNK = 64
FACTOR = HD ** (-0.5)
PAY = 16

G_STAGE, G_LONE = 96, 32
G_STAGES = ROWS_ALL // G_STAGE
A_STAGES = A_ROWS // G_STAGE
AB_STAGES = (A_ROWS + B_ROWS) // G_STAGE

R_STAGE = 48
R_STAGES = ROWS_ALL // R_STAGE
D_STAGES = C_ROWS // R_STAGE
GU_STAGES = (C_ROWS + B_ROWS) // R_STAGE
X_RING, Y_RING, Z_RING = 8, 6, 8
AHEAD = 2


def place():
    d = lax.axis_index("dp")
    t = lax.axis_index("tensor")
    return d // 2, d % 2, t // 2, t % 2


def at(x, c, z, y):
    return (x * 2 + c, z * 2 + y)


def greet(targets):
    barrier = pltpu.get_barrier_semaphore()
    for o in targets:
        pl.semaphore_signal(barrier, inc=1, device_id=o, device_id_type=MESH)
    pl.semaphore_wait(barrier, len(targets))


def rows_at(first, size):
    return pl.ds(pl.multiple_of(first, 16), size)


def nt(a, b):
    return lax.dot_general(a, b, (((1,), (1,)), ((), ())), preferred_element_type=jnp.float32)


def tn(a, b):
    return lax.dot_general(a, b, (((0,), (0,)), ((), ())), preferred_element_type=jnp.float32)


def nn(a, b):
    return lax.dot_general(a, b, (((1,), (0,)), ((), ())), preferred_element_type=jnp.float32)


def low(v):
    return v.astype(jnp.bfloat16)


def wide(v):
    return v.astype(jnp.float32)


def turn(v, cos, sin):
    other = jnp.concatenate([v[18:36], v[:18], v[54:72], v[36:54]], axis=0)
    return v * cos + other * sin


def fill(v):
    return jnp.concatenate([v, jnp.zeros((HEAD - HD, v.shape[1]), v.dtype)], axis=0)


def columns(rows):
    k, n = rows.shape
    rows = jnp.concatenate([rows, jnp.zeros((k, 128 - n), jnp.float32)], axis=1)
    rows = jnp.concatenate([rows, jnp.zeros((128 - k, 128), jnp.float32)], axis=0)
    return jnp.transpose(rows)


def remote(src, dst, ss, rs, to):
    return pltpu.make_async_remote_copy(
        src_ref=src, dst_ref=dst, send_sem=ss, recv_sem=rs, device_id=to, device_id_type=MESH)


def forward_kernel(
    counts, qkv_w, out_w, gu_w, down_w, condition, labels, ada_w, ada_b, bias_w, tokens, out_grad, gains, table,
    full, cond_out, mod_out, fi_out, si_out, fg_out, att_out, qkv_out, norm_out, stat_out, mixed_out, gu_out, hid_out,
    dd_out,
    own, mod_in, mod_send, cond_in, mod_all, mod, fi, si, fg, att, att_send, att_recv, wa, ow, mixed, qkv, norm, stat, wb, gu,
    hid, dd,
    send, recv, ms, mr, cs, cr, es, er, ls, qs, hs, ws, save,
):
    x, c, z, y = place()
    t = z * 2 + y
    d = x * 2 + c
    peers = [lax.rem(t + k, 8) for k in range(1, 8)]
    groups = [lax.rem(d + k, 4) for k in range(1, 4)]
    load_gu = pltpu.make_async_copy(gu_w, own.at[pl.ds(A_ROWS, B_ROWS)], ls.at[4])
    load_gu.start()
    load_down = pltpu.make_async_copy(
        down_w.at[rows_at(c * C_ROWS, C_ROWS)], own.at[pl.ds(A_ROWS + B_ROWS, C_ROWS)], ls.at[5])
    load_down.start()
    for head in range(2):
        @pl.when(c == head)
        def _():
            cut = slice(head * HD, (head + 1) * HD)
            own[:A_ROWS, :] = low(jnp.concatenate(
                [wide(qkv_w[0, cut]), wide(qkv_w[1, cut]), wide(qkv_w[2, cut]), wide(out_w[cut])], axis=0))

    greet([(d, p) for p in peers] + [(g, t) for g in groups])
    y_side, x_side, core = at(x, c, z, 1 - y), at(1 - x, c, z, y), at(x, 1 - c, z, y)
    up, down = at(x, c, z + 1, y), at(x, c, z - 1, y)

    def plane(g):
        return rows_at(g * G_STAGE + x * G_LONE, G_STAGE - G_LONE)

    def lone(g, side):
        return rows_at(g * G_STAGE + side * (G_STAGE - G_LONE), G_LONE)

    def copy(g, kind, src, slot, rows, path, to):
        return remote(src.at[rows], full.at[slot, rows], send.at[g, kind], recv.at[g, slot, path], to)

    def arrived(g, slot, rows, path):
        copy(g, 0, own, slot, rows, path, x_side).wait_recv()

    def issue(g):
        copy(g, 2, own, t, plane(g), 0, y_side).start()
        pl.when(z < 3)(lambda: copy(g, 0, own, t, plane(g), 0, up).start())
        pl.when(z > 0)(lambda: copy(g, 1, own, t, plane(g), 0, down).start())

    def along_z(g, j):
        def below():
            slot = (z - j) * 2 + y
            arrived(g, slot, plane(g), 0)
            pl.when(z < 3)(lambda: copy(g, 1 + 2 * j, full.at[slot], slot, plane(g), 0, up).start())
            copy(g, 8 + j, full.at[slot], slot, plane(g), 0, y_side).start()
            copy(g, 11 + j, full.at[slot], slot, lone(g, x), 1, x_side).start()

        def above():
            slot = (z + j) * 2 + y
            arrived(g, slot, plane(g), 0)
            pl.when(z > 0)(lambda: copy(g, 2 + 2 * j, full.at[slot], slot, plane(g), 0, down).start())
            copy(g, 14 + j, full.at[slot], slot, plane(g), 0, y_side).start()
            copy(g, 17 + j, full.at[slot], slot, lone(g, x), 1, x_side).start()

        pl.when(z >= j)(below)
        pl.when(z + j <= 3)(above)

    def along_y(g, zz):
        slot = zz * 2 + 1 - y
        arrived(g, slot, plane(g), 0)
        copy(g, 21 + zz, full.at[slot], slot, lone(g, x), 1, x_side).start()

    def service(i):
        def on(g, act):
            pl.when(jnp.logical_and(g >= 0, g < G_STAGES))(lambda: act(g))

        on(i, issue)
        for j in (1, 2, 3):
            on(i - j, lambda g: along_z(g, j))
        on(i - 1, lambda g: along_y(g, z))
        for j in (1, 2, 3):
            @pl.when(z >= j)
            def _():
                on(i - j - 1, lambda g: along_y(g, z - j))

            @pl.when(z + j <= 3)
            def _():
                on(i - j - 1, lambda g: along_y(g, z + j))

    def lone_in(first, last):
        @pl.loop(first, last)
        def _(g):
            for k in range(1, 8):
                arrived(g, lax.rem(t + k, 8), lone(g, 1 - x), 1)

    def mod_row(image, k):
        return mod[pl.ds(image * 8 + k, 1), :]

    def by_rows(act):
        for image in range(2):
            @pl.loop(0, PATCH // CHUNK)
            def _(i):
                act(image, rows_at(image * PATCH + i * CHUNK, CHUNK))

    service(0)

    cond_in[...] = jnp.zeros_like(cond_in)
    cond_in[:, :144] = condition[...]
    cond_in[:, 144:145] = wide(labels[...])
    mod_in[...] = jnp.zeros_like(mod_in)
    v = condition[...]
    act = low(v * (1.0 / (1.0 + jnp.exp(-v))))
    for k in range(6):
        share = nn(act, ada_w[k])
        for image in range(16):
            mod_in[image // 2, image % 2 * 8 + k : image % 2 * 8 + k + 1, :] = share[image : image + 1]
    for p in range(8):
        for k, row in enumerate((6, 7, 14)):
            mod_in[p, row : row + 1, :144] = wide(bias_w[k : k + 1, :])
    mod_send[...] = low(mod_in[...])
    small = []
    for k, p in enumerate(peers):
        small.append(remote(mod_send.at[p], mod_all.at[t], ms.at[k], mr.at[t], (d, p)))
    for k, g in enumerate(groups):
        small.append(remote(cond_in, cond_out.at[d], cs.at[k], cr.at[d], (g, t)))
    for cp in small:
        cp.start()
    kept = [
        pltpu.make_async_copy(mod_send.at[t], mod_all.at[t], ls.at[1]),
        pltpu.make_async_copy(cond_in, cond_out.at[d], ls.at[2]),
    ]
    for cp in kept:
        cp.start()
    load_gu.wait()
    load_down.wait()
    kept.append(pltpu.make_async_copy(own, full.at[t], ls.at[0]))
    kept[2].start()
    service(1)

    for p in peers:
        remote(mod_send.at[p], mod_all.at[p], ms.at[0], mr.at[p], (d, p)).wait_recv()
    kept[0].wait()
    for image in range(2):
        total = jnp.concatenate([wide(ada_b[...]), jnp.zeros((2, D), jnp.float32)], axis=0)
        for s in range(8):
            total = total + wide(mod_all[s])[image * 8 : image * 8 + 8]
        real = jnp.where(t * 2 + image < counts[0], 1.0, 0.0)
        row = lax.broadcasted_iota(jnp.int32, (8, D), 0)
        gate = jnp.logical_or(row == 2, row == 5)
        mod[image * 8 : image * 8 + 8, :] = jnp.where(gate, total * real, total)

    def first_rows(image, rows):
        v = wide(tokens[rows, :])
        n = v * lax.rsqrt(jnp.mean(v * v, axis=-1, keepdims=True) + epsilon)
        fi[0, rows, :] = low(n * (1.0 + mod_row(image, 1)) + mod_row(image, 0))

    by_rows(first_rows)
    share_fi = remote(fi.at[0], fi.at[1], es.at[0], er.at[0], core)
    share_fi.start()

    def feed_rows(image, rows):
        fg[0, rows, :] = low(wide(out_grad[rows, :]) * mod_row(image, 5))

    by_rows(feed_rows)
    share_fg = remote(fg.at[0], fg.at[1], es.at[1], er.at[1], core)
    share_fg.start()

    @pl.loop(2, A_STAGES + 4)
    def _(i):
        service(i)

    kept[2].wait()
    lone_in(0, A_STAGES)
    share_fi.wait_recv()
    share_fg.wait_recv()
    saves = [
        pltpu.make_async_copy(fi, fi_out, save.at[0]),
        pltpu.make_async_copy(fg, fg_out, save.at[1]),
        pltpu.make_async_copy(mod, mod_out, save.at[2]),
    ]
    for cp in saves:
        cp.start()

    def load_a(s):
        return pltpu.make_async_copy(full.at[s, pl.ds(0, QKV_ROWS)], wa.at[lax.rem(s, 2)], ws.at[lax.rem(s, 2)])

    load_o = pltpu.make_async_copy(full.at[:, pl.ds(O_FIRST, HEAD)], ow, ls.at[3])
    load_o.start()
    load_a(0).start()
    gain_cols = columns(wide(gains[...]))

    def save_head(s):
        b = lax.rem(s, 2)
        return [
            pltpu.make_async_copy(qkv.at[b], qkv_out.at[s], qs.at[b, 0]),
            pltpu.make_async_copy(norm.at[b], norm_out.at[s], qs.at[b, 1]),
            pltpu.make_async_copy(stat.at[b], stat_out.at[s], qs.at[b, 2]),
        ]

    @pl.loop(0, 8)
    def _(s):
        b = lax.rem(s, 2)
        load_a(s).wait()
        pl.when(s < 7)(lambda: load_a(s + 1).start())

        @pl.when(s > 1)
        def _():
            for cp in save_head(s - 2):
                cp.wait()

        bias_rows = wide(mod_all[s, :, :256])
        bias_rows = jnp.concatenate([bias_rows[6:8, :144], bias_rows[14:15, :144]], axis=0)
        bias = columns(jnp.where(c == 0, bias_rows[:, :HD], bias_rows[:, HD:]))
        cos, sin = table[:HD, :], table[HD:, :]
        for h in range(2):
            raw = nt(wa[b], fi[h])
            for i in range(2):
                v = raw[i * HD : (i + 1) * HD] + bias[:HD, i : i + 1]
                inv = lax.rsqrt(jnp.sum(v * v, axis=0, keepdims=True) * (1.0 / HD) + epsilon)
                n = v * inv
                norm[b, h, i * HEAD : (i + 1) * HEAD, :] = low(fill(n))
                stat[b, h, i : i + 1, :] = inv
                qkv[b, h, i * HEAD : (i + 1) * HEAD, :] = low(fill(turn(n * gain_cols[:HD, i : i + 1], cos, sin)))
            v = low(fill(raw[2 * HD : 3 * HD] + bias[:HD, 2:3]))
            qkv[b, h, 2 * HEAD :, :] = v
            for image in range(2):
                cut = slice(image * PATCH, (image + 1) * PATCH)
                e = jnp.exp(tn(qkv[b, h, HEAD : 2 * HEAD, cut], qkv[b, h, :HEAD, cut]) * FACTOR)
                row_sum = jnp.sum(e, axis=0, keepdims=True)
                stat[b, h, 2:3, cut] = jnp.log(row_sum)
                p = low(e * (1.0 / row_sum))
                m = nn(v[:, cut], p)
                m = jnp.concatenate([m[HD:], m[:HD]], axis=0)
                mixed[h, pl.ds(pl.multiple_of(s * HEAD, 16), HEAD), cut] = low(m)
        for cp in save_head(s):
            cp.start()

        pl.when(s == 3)(lambda: service(A_STAGES + 4))
        pl.when(s == 7)(lambda: service(A_STAGES + 5))

    for s in (6, 7):
        for cp in save_head(s):
            cp.wait()
    load_o.wait()
    saves.append(pltpu.make_async_copy(mixed, mixed_out, save.at[3]))
    saves[-1].start()

    for image in range(2):
        cut = slice(image * PATCH, (image + 1) * PATCH)
        att_send[cut, :] = low(tn(mixed[1, :, cut], ow[...].reshape(8 * HEAD, D)))
    share_att = remote(att_send, att_recv, es.at[2], er.at[2], core)
    share_att.start()
    for image in range(2):
        cut = slice(image * PATCH, (image + 1) * PATCH)
        att[cut, :] = tn(mixed[0, :, cut], ow[...].reshape(8 * HEAD, D))
    share_att.wait_recv()

    def second_rows(image, rows):
        a = att[rows, :] + wide(att_recv[rows, :])
        att[rows, :] = a
        v = wide(tokens[rows, :]) + mod_row(image, 2) * a
        n = v * lax.rsqrt(jnp.mean(v * v, axis=-1, keepdims=True) + epsilon)
        si[0, rows, :] = low(n * (1.0 + mod_row(image, 4)) + mod_row(image, 3))

    by_rows(second_rows)
    share_si = remote(si.at[0], si.at[1], es.at[3], er.at[3], core)
    share_si.start()

    @pl.loop(A_STAGES + 6, AB_STAGES + 4)
    def _(i):
        service(i)

    lone_in(A_STAGES, AB_STAGES)
    share_si.wait_recv()
    saves += [
        pltpu.make_async_copy(att, att_out, save.at[4]),
        pltpu.make_async_copy(si, si_out, save.at[5]),
    ]
    saves[-2].start()
    saves[-1].start()

    def load_b(s):
        return pltpu.make_async_copy(full.at[s, pl.ds(A_ROWS, B_ROWS)], wb.at[lax.rem(s, 2)], ws.at[2 + lax.rem(s, 2)])

    def save_shard(s):
        b = lax.rem(s, 2)
        return [
            pltpu.make_async_copy(gu.at[b], gu_out.at[s], hs.at[b, 0]),
            pltpu.make_async_copy(hid.at[b], hid_out.at[s], hs.at[b, 1]),
            pltpu.make_async_copy(dd.at[b], dd_out.at[s], hs.at[b, 2]),
        ]

    load_b(0).start()

    @pl.loop(0, 8)
    def _(s):
        b = lax.rem(s, 2)
        load_b(s).wait()
        pl.when(s < 7)(lambda: load_b(s + 1).start())

        @pl.when(s > 1)
        def _():
            for cp in save_shard(s - 2):
                cp.wait()

        for h in range(2):
            both = nt(wb[b], si[h])
            g, u = both[:SHARD_FF], both[SHARD_FF:]
            gu[b, h] = low(both)
            hid[b, h] = low(g * (1.0 / (1.0 + jnp.exp(-g))) * u)
        dd[b] = low(nn(hid[b, 0], fg[0]) + nn(hid[b, 1], fg[1]))
        for cp in save_shard(s):
            cp.start()

        pl.when(s == 3)(lambda: service(AB_STAGES + 4))

    service(AB_STAGES + 5)
    lone_in(AB_STAGES, G_STAGES)
    for s in (6, 7):
        for cp in save_shard(s):
            cp.wait()

    @pl.loop(0, G_STAGES)
    def _(g):
        def sent(kind, rows):
            copy(g, kind, own, t, rows, 0, x_side).wait_send()

        sent(2, plane(g))
        pl.when(z < 3)(lambda: sent(0, plane(g)))
        pl.when(z > 0)(lambda: sent(1, plane(g)))
        for k in range(4):
            sent(21 + k, lone(g, x))
        for j in (1, 2, 3):
            @pl.when(z >= j)
            def _():
                pl.when(z < 3)(lambda: sent(1 + 2 * j, plane(g)))
                sent(8 + j, plane(g))
                sent(11 + j, lone(g, x))

            @pl.when(z + j <= 3)
            def _():
                pl.when(z > 0)(lambda: sent(2 + 2 * j, plane(g)))
                sent(14 + j, plane(g))
                sent(17 + j, lone(g, x))

    for cp in small + [share_fi, share_fg, share_att, share_si]:
        cp.wait_send()
    for g in groups:
        remote(cond_in, cond_out.at[g], cs.at[0], cr.at[g], (g, t)).wait_recv()
    kept[1].wait()
    for cp in saves:
        cp.wait()


def forward(counts, qkv_w, out_w, gu_w, down_w, condition, labels, ada_w, ada_b, bias_w, tokens, out_grad, gains, table):
    dma = pltpu.SemaphoreType.DMA
    vm = pltpu.VMEM
    bf, f32 = jnp.bfloat16, jnp.float32
    anywhere = pl.BlockSpec(memory_space=pl.ANY)
    inside = pl.BlockSpec(memory_space=pltpu.VMEM)
    scalar = pl.BlockSpec(memory_space=pltpu.SMEM)
    R = tokens.shape[0]
    outs = [
        ((8, ROWS_ALL, D), bf), ((4, 16, 256), f32), ((16, D), f32),
        ((2, R, D), bf), ((2, R, D), bf), ((2, R, D), bf), ((R, D), f32),
        ((8, 2, 3 * HEAD, R), bf), ((8, 2, 2 * HEAD, R), bf), ((8, 2, 8, R), f32), ((2, 8 * HEAD, R), bf),
        ((8, 2, B_ROWS, R), bf), ((8, 2, SHARD_FF, R), bf), ((8, C_ROWS, D), bf),
    ]
    return pl.pallas_call(
        forward_kernel,
        out_shape=tuple(jax.ShapeDtypeStruct(s, e) for s, e in outs),
        in_specs=[scalar, inside, inside, anywhere, anywhere] + [inside] * 9,
        out_specs=(anywhere,) * len(outs),
        scratch_shapes=[
            vm((ROWS_ALL, D), bf), vm((8, 16, D), f32), vm((8, 16, D), bf), vm((16, 256), f32), vm((8, 16, D), bf),
            vm((16, D), f32),
            vm((2, R, D), bf), vm((2, R, D), bf), vm((2, R, D), bf), vm((R, D), f32), vm((R, D), bf), vm((R, D), bf),
            vm((2, QKV_ROWS, D), bf), vm((8, HEAD, D), bf), vm((2, 8 * HEAD, R), bf),
            vm((2, 2, 3 * HEAD, R), bf), vm((2, 2, 2 * HEAD, R), bf), vm((2, 2, 8, R), f32),
            vm((2, B_ROWS, D), bf), vm((2, 2, B_ROWS, R), bf), vm((2, 2, SHARD_FF, R), bf), vm((2, C_ROWS, D), bf),
            dma((G_STAGES, 25)), dma((G_STAGES, 8, 2)), dma((7,)), dma((8,)), dma((3,)), dma((4,)),
            dma((4,)), dma((4,)), dma((6,)), dma((2, 3)), dma((2, 3)), dma((4,)), dma((6,)),
        ],
        compiler_params=pltpu.CompilerParams(
            collective_id=0, has_side_effects=True, vmem_limit_bytes=60 * 2**20),
        name="forward",
    )(counts, qkv_w, out_w, gu_w, down_w, condition, labels, ada_w, ada_b, bias_w, tokens, out_grad, gains, table)


def backward_kernel(
    full, fi_in, si_in, fg_in, att_in, qkv_in, norm_in, stat_in, mixed_in, gu_in, hid_in, dd_in,
    counts, tokens, out_grad, mod, gains, table,
    result_out, tokens_out, grads, pay_all,
    part, xin, yin, zin, fin, buf_a, buf_b, acc, after, att, sent, came, came_feed, result,
    wd, wb, wa, hid, gu, qkv, norm, stat, mixed, dqkv, dlow, gain_sum, payf, pay,
    xs, xr, ys, yr, zs, zr, fs, fr, es, er, ps, pr, ls, lw, x_free, y_free, z_free,
):
    x, c, z, y = place()
    t = z * 2 + y
    d = x * 2 + c
    y_side, x_side, core = at(x, c, z, 1 - y), at(1 - x, c, z, y), at(x, 1 - c, z, y)
    up, down = at(x, c, z + 1, y), at(x, c, z - 1, y)
    spot = x * 8 + t
    mates = []
    for k in range(1, 16):
        o = lax.rem(spot + k, 16)
        mates.append(((o // 8) * 2 + c, lax.rem(o, 8)))
    greet(mates + [core])

    loads = [
        pltpu.make_async_copy(fg_in, buf_a, ls.at[0]),
        pltpu.make_async_copy(si_in, buf_b, ls.at[1]),
        pltpu.make_async_copy(att_in, att, ls.at[2]),
    ]
    load_dd = pltpu.make_async_copy(
        dd_in, part.at[:, :, pl.ds(A_ROWS + B_ROWS, C_ROWS)], ls.at[6])
    load_dd.start()
    for cp in loads:
        cp.start()

    def rows_of(g):
        return rows_at((R_STAGES - 1 - g) * R_STAGE, R_STAGE)

    def side_y(side):
        return 1 - y if side == 0 else y

    def lone_z(g, yy):
        return jnp.where(yy == lax.rem(x + g, 2), 1, 2)

    def xcopy(g, side):
        yy = side_y(side)
        return remote(
            part.at[3 - lone_z(g, yy), yy, rows_of(g)], xin.at[lax.rem(g, X_RING), side],
            xs.at[g, side], xr.at[g, side], x_side)

    def ycopy(g, k):
        yy = 1 - y
        zz = (0, 3, lone_z(g, yy))[k]
        return remote(part.at[zz, yy, rows_of(g)], yin.at[lax.rem(g, Y_RING), k], ys.at[g, k], yr.at[g, k], y_side)

    def zcopy(g, way, k):
        zz = (3 - 3 * way) if k == 0 else lone_z(g, y)
        return remote(
            part.at[zz, y, rows_of(g)], zin.at[lax.rem(g, Z_RING), way * 2 + k],
            zs.at[g, way * 2 + k], zr.at[g, way * 2 + k], up if way == 0 else down)

    def plane_sum(g):
        return remote(part.at[z, y, rows_of(g)], fin.at[rows_of(g)], fs.at[g, 0], fr.at[g, 0], x_side)

    def finished(g):
        return remote(part.at[z, y, rows_of(g)], grads.at[c, rows_of(g)], fs.at[g, 0], fr.at[g, 0], x_side)

    def core_copy(g, here):
        src = part.at[z, y, rows_of(g)] if here else grads.at[c, rows_of(g)]
        return remote(src, grads.at[c, rows_of(g)], fs.at[g, 1], fr.at[g, 1], core)

    def own_copy(g):
        return pltpu.make_async_copy(part.at[z, y, rows_of(g)], grads.at[c, rows_of(g)], fs.at[g, 2])

    def add(zz, yy, g, piece):
        first = (R_STAGES - 1 - g) * R_STAGE

        @pl.loop(0, R_STAGE // 16)
        def _(i):
            a = rows_at(first + i * 16, 16)
            part[zz, yy, a, :] = low(wide(part[zz, yy, a, :]) + wide(piece(rows_at(i * 16, 16))))

    def send(g, side):
        if side == 0:
            pl.when(g >= X_RING)(lambda: pl.semaphore_wait(x_free, 1))
            pl.when(g >= Y_RING)(lambda: pl.semaphore_wait(y_free, 1))
        xcopy(g, side).start()
        if side == 0:
            ycopy(g, 0).start()
            ycopy(g, 1).start()

    def x_stage(g):
        b = lax.rem(g, X_RING)
        for side in (0, 1):
            yy = side_y(side)
            xcopy(g, side).wait_recv()
            add(lone_z(g, yy), yy, g, lambda r: xin[b, side, r, :])
            if side == 0:
                ycopy(g, 2).start()
        pl.when(g + X_RING < R_STAGES)(
            lambda: pl.semaphore_signal(x_free, inc=1, device_id=x_side, device_id_type=MESH))

    def y_stage(g):
        b = lax.rem(g, Y_RING)
        for k in range(3):
            ycopy(g, k).wait_recv()
            add((0, 3, lone_z(g, y))[k], y, g, lambda r: yin[b, k, r, :])
        pl.when(g + Y_RING < R_STAGES)(
            lambda: pl.semaphore_signal(y_free, inc=1, device_id=y_side, device_id_type=MESH))

    def take(g, way, k):
        zcopy(g, way, k).wait_recv()
        zz = (3 - 3 * way) if k == 0 else lone_z(g, y)
        add(zz, y, g, lambda r: zin[lax.rem(g, Z_RING), way * 2 + k, r, :])

    def z_stage(g, way):
        further = z < 3 if way == 0 else z > 0
        first = z == 0 if way == 0 else z == 3

        @pl.when(further)
        def _():
            pl.when(g >= Z_RING)(lambda: pl.semaphore_wait(z_free.at[way], 1))
            pl.when(jnp.logical_not(first))(lambda: take(g, way, 0))
            zcopy(g, way, 0).start()

        lone = lone_z(g, y)

        @pl.when(z < lone if way == 0 else z > lone)
        def _():
            pl.when(jnp.logical_not(first))(lambda: take(g, way, 1))
            zcopy(g, way, 1).start()

    def own_stage(g):
        pl.when(z == 3)(lambda: take(g, 0, 0))
        pl.when(z == 0)(lambda: take(g, 1, 0))

        @pl.when(z == lone_z(g, y))
        def _():
            take(g, 0, 1)
            take(g, 1, 1)
            finished(g).start()

        pl.when(jnp.logical_or(z == 0, z == 3))(lambda: plane_sum(g).start())

        @pl.when(g + Z_RING < R_STAGES)
        def _():
            pl.when(z > 0)(
                lambda: pl.semaphore_signal(z_free.at[0], inc=1, device_id=down, device_id_type=MESH))
            pl.when(z < 3)(
                lambda: pl.semaphore_signal(z_free.at[1], inc=1, device_id=up, device_id_type=MESH))

    def f_stage(g):
        ends = jnp.logical_or(z == 0, z == 3)
        here = z == lone_z(g, y)

        @pl.when(ends)
        def _():
            plane_sum(g).wait()
            add(z, y, g, lambda r: fin[rows_at((R_STAGES - 1 - g) * R_STAGE + r.start, 16), :])

        @pl.when(jnp.logical_or(ends, here))
        def _():
            own_copy(g).start()
            core_copy(g, True).start()

        @pl.when(z == 3 - lone_z(g, y))
        def _():
            finished(g).wait_recv()
            core_copy(g, False).start()

    def service(i, ready):
        def on(g, act):
            pl.when(jnp.logical_and(g >= 0, g < R_STAGES))(lambda: act(g))

        on(i, x_stage)
        on(i - 1, y_stage)
        on(i - 1 - z, lambda g: z_stage(g, 0))
        on(i - 4 + z, lambda g: z_stage(g, 1))
        on(i - 4, own_stage)
        on(i - 5, f_stage)

        @pl.when(i + AHEAD < ready)
        def _():
            send(i + AHEAD, 0)
            send(i + AHEAD, 1)

    def send_stages(first, last):
        @pl.loop(first, last)
        def _(g):
            send(g, 0)
            send(g, 1)

    def shard(k):
        return lax.rem(k, 4), jnp.where(k < 4, 1 - y, y)

    def slot(k):
        zz, yy = shard(k)
        return zz * 2 + yy

    def stream(pairs):
        def fetch(k):
            b = lax.rem(k, 2)
            return [pltpu.make_async_copy(src(slot(k)), buf.at[b], lw.at[n, b]) for src, buf, n in pairs]

        def begin(k):
            for cp in fetch(k):
                cp.start()

        def turn_to(k):
            for cp in fetch(k):
                cp.wait()
            pl.when(k < 7)(lambda: begin(k + 1))

        return begin, turn_to

    def mod_row(image, k):
        return mod[pl.ds(image * 8 + k, 1), :]

    def by_rows(act):
        for image in range(2):
            @pl.loop(0, PATCH // CHUNK)
            def _(i):
                act(image, rows_at(image * PATCH + i * CHUNK, CHUNK))

    def count(image, k, v):
        payf[pl.ds(image * 8 + k, 1), :] += jnp.sum(v, axis=0, keepdims=True)

    def clear(ref):
        @pl.loop(0, ref.shape[0] // 16)
        def _(i):
            ref[rows_at(i * 16, 16), :] = jnp.zeros((16, D), jnp.float32)

    def gather_sum(h, left, right):
        for image in range(2):
            cut = slice(image * PATCH, (image + 1) * PATCH)
            rows = slice(h * 512 + image * PATCH, h * 512 + (image + 1) * PATCH)
            acc[rows, :] += tn(left[:, cut], right)

    def share_half(number, landing):
        @pl.loop(0, 512 // CHUNK)
        def _(i):
            sent[rows_at(i * CHUNK, CHUNK), :] = low(acc[rows_at(512 + i * CHUNK, CHUNK), :])

        cp = remote(sent, landing, es.at[number], er.at[number], core)
        cp.start()
        return cp

    payf[...] = jnp.zeros_like(payf)
    gain_sum[...] = jnp.zeros_like(gain_sum)
    clear(acc)
    begin_g, turn_g = stream([
        (lambda s: full.at[s, pl.ds(A_ROWS + B_ROWS, C_ROWS)], wd, 1),
        (lambda s: full.at[s, pl.ds(A_ROWS, B_ROWS)], wb, 2),
        (lambda s: gu_in.at[s], gu, 3),
    ])
    begin_a, turn_a = stream([
        (lambda s: full.at[s, pl.ds(0, A_ROWS)], wa, 4),
        (lambda s: qkv_in.at[s], qkv, 5),
        (lambda s: norm_in.at[s], norm, 6),
        (lambda s: stat_in.at[s], stat, 7),
        (lambda s: mixed_in.at[:, rows_at(s * HEAD, HEAD)], mixed, 8),
    ])
    begin_f, turn_f = stream([
        (lambda s: hid_in.at[s], hid, 0),
        (lambda s: full.at[s, pl.ds(A_ROWS + B_ROWS, C_ROWS)], wd, 1),
    ])
    begin_g(0)
    load_dd.wait()
    send_stages(0, AHEAD)
    loads[0].wait()
    loads[1].wait()

    @pl.loop(0, 8)
    def _(k):
        b = lax.rem(k, 2)
        zz, yy = shard(k)
        turn_g(k)
        grads_here = []
        for h in range(2):
            hg = nt(wd[b], buf_a[h])
            g, u = wide(gu[b, h, :SHARD_FF]), wide(gu[b, h, SHARD_FF:])
            sig = 1.0 / (1.0 + jnp.exp(-g))
            act = g * sig
            both = low(jnp.concatenate([hg * u * (sig + act * (1.0 - sig)), hg * act], axis=0))
            grads_here.append(both)
            gather_sum(h, both, wb[b])
        part[zz, yy, A_ROWS : A_ROWS + B_ROWS, :] = low(
            nn(grads_here[0], buf_b[0]) + nn(grads_here[1], buf_b[1]))

        pl.when(lax.rem(k, 2) == 1)(lambda: service(k // 2, D_STAGES))

    send_stages(D_STAGES, D_STAGES + AHEAD)
    share_second = share_half(0, came)
    service(D_STAGES, GU_STAGES)
    begin_a(0)
    load_fi = pltpu.make_async_copy(fi_in, buf_a, ls.at[0])
    load_fi.start()
    loads[2].wait()
    share_second.wait_recv()

    def after_rows(image, rows):
        a = att[rows, :]
        v = wide(tokens[rows, :]) + mod_row(image, 2) * a
        inv = lax.rsqrt(jnp.mean(v * v, axis=-1, keepdims=True) + epsilon)
        n = v * inv
        sg = acc[rows, :] + wide(came[rows, :])
        dn = sg * (1.0 + mod_row(image, 4))
        ag = wide(out_grad[rows, :]) + inv * (dn - n * jnp.mean(dn * n, axis=-1, keepdims=True))
        after[rows, :] = ag
        buf_b[0, rows, :] = low(ag * mod_row(image, 2))
        count(image, 2, ag * a)
        count(image, 3, sg)
        count(image, 4, sg * n)

    by_rows(after_rows)
    share_ag = remote(buf_b.at[0], buf_b.at[1], es.at[1], er.at[1], core)
    share_ag.start()
    service(D_STAGES + 1, GU_STAGES)
    clear(acc)
    load_fi.wait()
    share_ag.wait_recv()

    gain_cols = columns(wide(gains[...]))

    @pl.loop(0, 8)
    def _(k):
        b = lax.rem(k, 2)
        zz, yy = shard(k)
        turn_a(k)
        cos, sin = table[:HD, :PATCH], table[HD:, :PATCH]
        out_part = nn(mixed[b, 0], buf_b[0]) + nn(mixed[b, 1], buf_b[1])
        for h in range(2):
            mg_all = nt(wa[b, O_FIRST:], buf_b[h])
            mg_all = low(fill(mg_all[HEAD - HD :]))
            dqkv[h, 3 * HD :, :] = jnp.zeros((QKV_ROWS - 3 * HD, 512), jnp.float32)
            for image in range(2):
                cut = slice(image * PATCH, (image + 1) * PATCH)
                q, kk, v = [qkv[b, h, i * HEAD : (i + 1) * HEAD, cut] for i in range(3)]
                mg = mg_all[:, cut]
                p = jnp.exp(tn(kk, q) * FACTOR - stat[b, h, 2:3, cut])
                dqkv[h, 2 * HD : 3 * HD, cut] = nt(mg, low(p))[:HD]
                pg = tn(v, mg)
                sg = low(p * (pg - jnp.sum(p * pg, axis=0, keepdims=True)))
                backs = (nn(kk, sg), nt(q, sg))
                for i in range(2):
                    rows = slice(i * HD, (i + 1) * HD)
                    back = turn(backs[i][:HD] * FACTOR, cos, -sin)
                    n = wide(norm[b, h, i * HEAD : (i + 1) * HEAD, cut])[:HD]
                    gain_sum[rows, :] += back * n
                    dn = back * gain_cols[:HD, i : i + 1]
                    mean = jnp.sum(dn * n, axis=0, keepdims=True) * (1.0 / HD)
                    dqkv[h, rows, cut] = stat[b, h, i : i + 1, cut] * (dn - n * mean)
            dlow[h] = low(dqkv[h])
            gather_sum(h, dlow[h], wa[b, :QKV_ROWS])
        qkv_part = nn(dlow[0], buf_a[0]) + nn(dlow[1], buf_a[1])
        part[zz, yy, :A_ROWS, :] = low(jnp.concatenate([qkv_part[:QKV], out_part[HEAD - HD :]], axis=0))
        ones = jnp.ones((8, 512), jnp.bfloat16)
        sums = nt(ones, dlow[0]) + nt(ones, dlow[1])
        s = slot(k)
        payf[pl.ds(6 + s // 4, 1), pl.ds(pl.multiple_of(lax.rem(s, 4) * 256, 128), QKV)] = sums[:1, :QKV]

        pl.when(lax.rem(k, 3) != 0)(lambda: service(D_STAGES + 1 + k - k // 3, GU_STAGES))

    send_stages(GU_STAGES, GU_STAGES - 1 + AHEAD)
    share_second.wait_send()
    begin_f(0)
    share_first = share_half(2, came)
    service(GU_STAGES - 1, R_STAGES)
    share_first.wait_recv()

    def first_rows(image, rows):
        v = wide(tokens[rows, :])
        inv = lax.rsqrt(jnp.mean(v * v, axis=-1, keepdims=True) + epsilon)
        n = v * inv
        fgd = acc[rows, :] + wide(came[rows, :])
        dn = fgd * (1.0 + mod_row(image, 1))
        count(image, 0, fgd)
        count(image, 1, fgd * n)
        acc[rows, :] = after[rows, :] + inv * (dn - n * jnp.mean(dn * n, axis=-1, keepdims=True))

    by_rows(first_rows)
    save_tokens = pltpu.make_async_copy(acc.at[pl.ds(0, 512)], tokens_out, ls.at[3])
    save_tokens.start()
    service(GU_STAGES, R_STAGES)
    save_tokens.wait()
    clear(acc)

    @pl.loop(0, 8)
    def _(k):
        b = lax.rem(k, 2)
        turn_f(k)
        for h in range(2):
            gather_sum(h, hid[b, h], wd[b])

    share_first.wait_send()
    share_feed = share_half(3, came_feed)
    service(GU_STAGES + 1, R_STAGES)
    share_feed.wait_recv()

    def result_rows(image, rows):
        feed = acc[rows, :] + wide(came_feed[rows, :])
        v = wide(tokens[rows, :]) + mod_row(image, 2) * att[rows, :]
        result[rows, :] = low(v + mod_row(image, 5) * feed)
        count(image, 5, wide(out_grad[rows, :]) * feed)

    by_rows(result_rows)
    save_result = pltpu.make_async_copy(result, result_out, ls.at[4])
    save_result.start()
    lanes = gain_sum[:, :128] + gain_sum[:, 128:]
    lanes = jnp.concatenate([lanes, jnp.zeros((256 - 2 * HD, 128), jnp.float32)], axis=0)
    payf[14:15, :256] = jnp.sum(jnp.transpose(lanes), axis=0, keepdims=True)
    for image in range(2):
        real = jnp.where(t * 2 + image < counts[0], 1.0, 0.0)
        for k in (2, 5):
            row = slice(image * 8 + k, image * 8 + k + 1)
            payf[row, :] = payf[row, :] * real
    pay[...] = low(payf[...])
    me = d * 8 + t
    keep_pay = pltpu.make_async_copy(pay, pay_all.at[me], ls.at[5])
    keep_pay.start()
    pays = [remote(pay, pay_all.at[me], ps.at[k], pr.at[k], o) for k, o in enumerate(mates)]
    for cp in pays:
        cp.start()

    @pl.loop(GU_STAGES + 2, GU_STAGES + 6)
    def _(i):
        service(i, R_STAGES)

    keep_pay.wait()
    for cp in pays:
        cp.wait()
    swaps = []
    for xx in range(2):
        rows = pl.ds(pl.multiple_of((xx * 2 + c) * 8, 8), 8)
        swaps.append(remote(pay_all.at[rows], pay_all.at[rows], ps.at[15 + xx], pr.at[15 + xx], core))
        swaps[-1].start()

    @pl.loop(GU_STAGES + 6, R_STAGES + 5)
    def _(i):
        service(i, R_STAGES)

    @pl.loop(0, R_STAGES)
    def _(g):
        for side in (0, 1):
            xcopy(g, side).wait_send()
        for k in range(3):
            ycopy(g, k).wait_send()
        lone = lone_z(g, y)
        pl.when(z < 3)(lambda: zcopy(g, 0, 0).wait_send())
        pl.when(z > 0)(lambda: zcopy(g, 1, 0).wait_send())
        pl.when(z < lone)(lambda: zcopy(g, 0, 1).wait_send())
        pl.when(z > lone)(lambda: zcopy(g, 1, 1).wait_send())
        pl.when(z == lone)(lambda: finished(g).wait_send())
        pl.when(z != 3 - lone)(lambda: own_copy(g).wait())
        core_copy(g, True).wait()

    for cp in swaps:
        cp.wait()
    share_ag.wait_send()
    share_feed.wait_send()
    save_result.wait()


def backward(saved, counts, tokens, out_grad, mod, gains, table):
    dma = pltpu.SemaphoreType.DMA
    regular = pltpu.SemaphoreType.REGULAR
    vm = pltpu.VMEM
    bf, f32 = jnp.bfloat16, jnp.float32
    anywhere = pl.BlockSpec(memory_space=pl.ANY)
    inside = pl.BlockSpec(memory_space=pltpu.VMEM)
    R = tokens.shape[0]
    outs = [((R, D), bf), ((R, D), f32), ((2, ROWS_ALL, D), bf), ((32, PAY, D), bf)]
    return pl.pallas_call(
        backward_kernel,
        out_shape=tuple(jax.ShapeDtypeStruct(s, e) for s, e in outs),
        in_specs=[anywhere] * len(saved) + [pl.BlockSpec(memory_space=pltpu.SMEM)] + [inside] * 5,
        out_specs=(anywhere,) * len(outs),
        scratch_shapes=[
            vm((4, 2, ROWS_ALL, D), bf), vm((X_RING, 2, R_STAGE, D), bf), vm((Y_RING, 3, R_STAGE, D), bf),
            vm((Z_RING, 4, R_STAGE, D), bf), vm((ROWS_ALL, D), bf),
            vm((2, R, D), bf), vm((2, R, D), bf), vm((2 * R, D), f32), vm((R, D), f32), vm((R, D), f32),
            vm((R, D), bf), vm((R, D), bf), vm((R, D), bf), vm((R, D), bf),
            vm((2, C_ROWS, D), bf), vm((2, B_ROWS, D), bf), vm((2, A_ROWS, D), bf),
            vm((2, 2, SHARD_FF, R), bf), vm((2, 2, B_ROWS, R), bf), vm((2, 2, 3 * HEAD, R), bf),
            vm((2, 2, 2 * HEAD, R), bf), vm((2, 2, 8, R), f32), vm((2, 2, HEAD, R), bf),
            vm((2, QKV_ROWS, R), f32), vm((2, QKV_ROWS, R), bf), vm((2 * HD, PATCH), f32), vm((16, D), f32),
            vm((16, D), bf),
            dma((R_STAGES, 2)), dma((R_STAGES, 2)), dma((R_STAGES, 3)), dma((R_STAGES, 3)),
            dma((R_STAGES, 4)), dma((R_STAGES, 4)), dma((R_STAGES, 3)), dma((R_STAGES, 2)),
            dma((4,)), dma((4,)), dma((17,)), dma((17,)), dma((7,)), dma((9, 2)),
            regular, regular, regular((2,)),
        ],
        compiler_params=pltpu.CompilerParams(
            collective_id=1, has_side_effects=True, vmem_limit_bytes=62 * 2**20),
        name="backward",
    )(*saved, counts, tokens, out_grad, mod, gains, table)


def normalize(vectors, axis=-1, count=None):
    count = count or vectors.shape[axis]
    inverse = lax.rsqrt(jnp.sum(vectors * vectors, axis=axis, keepdims=True) / count + epsilon)
    return (vectors * inverse, inverse)


def normalize_back(grad, normed, inverse, axis=-1, count=None):
    count = count or grad.shape[axis]
    return inverse * (grad - normed * (jnp.sum(grad * normed, axis=axis, keepdims=True) / count))


def silu_slope(values):
    sigma = jax.nn.sigmoid(values)
    return sigma * (1.0 + values * (1.0 - sigma))


def pair_tables(count):
    pairs = HD // 4
    theta = np.exp(-math.log(100.0) * np.arange(pairs, dtype=np.float32) / pairs)
    spot = np.arange(count) % PATCH
    a, b = theta[:, None] * (spot // GRID)[None], theta[:, None] * (spot % GRID)[None]
    cos = np.concatenate([np.cos(a), np.cos(a), np.cos(b), np.cos(b)])
    sin = np.concatenate([-np.sin(a), np.sin(a), -np.sin(b), np.sin(b)])
    return np.concatenate([cos, sin]).astype(np.float32)


def unpack_grads(both):
    qkv = both[:, :QKV].reshape(2, 3, HD, D).swapaxes(0, 1).reshape(3, 2 * HD, D)
    o = both[:, QKV:A_ROWS].reshape(2 * HD, D)
    gu = both[:, A_ROWS : A_ROWS + B_ROWS].reshape(2, 2, SHARD_FF, D)
    gu = gu.transpose(3, 1, 0, 2).reshape(D, 2, 2 * SHARD_FF)
    dn = both[:, A_ROWS + B_ROWS :].reshape(2 * SHARD_FF, D)
    return [wide(v) for v in (qkv.transpose(2, 0, 1), o, gu, dn)]


def fast(
    tokens, labels, timesteps, image_counts, class_table, ada_weight, ada_bias,
    qkv_weight, qkv_bias, qk_scale, out_weight, gate_up_weight, down_weight, out_grad,
):
    dot = lambda s, a, b: jnp.einsum(s, a, b, preferred_element_type=jnp.float32)
    t = lax.axis_index("tensor")
    c = lax.axis_index("dp") % 2
    images = labels.shape[0]
    columns_here = class_table.shape[1]
    column = t * columns_here + jnp.arange(columns_here)
    half_width = D // 2
    frequency = jnp.exp(-math.log(10000.0) * (column % half_width).astype(jnp.float32) / half_width)
    angles = timesteps.astype(jnp.float32)[:, None] * frequency[None, :]
    time_embed = jnp.where(column[None, :] < half_width, jnp.cos(angles), jnp.sin(angles))
    classes = jnp.arange(class_table.shape[0])
    condition = dot("in,nc->ic", low(labels[:, None] == classes[None, :]), class_table) + time_embed
    gu = lax.dynamic_slice_in_dim(gate_up_weight, c * SHARD_FF, SHARD_FF, 2)
    gu = gu.transpose(1, 2, 0).reshape(B_ROWS, D)
    table = pair_tables(tokens.shape[0])
    (weights, cond_all, mod, first_in, second_in, feed_grad, attention, qkv_t, norm_t, stat_t, mixed, gu_t, hidden,
     down_part) = forward(
        image_counts, qkv_weight.transpose(1, 2, 0), out_weight, gu, down_weight, condition, labels[:, None],
        ada_weight.transpose(1, 0, 2), ada_bias, qkv_bias, tokens, out_grad, qk_scale, table)
    saved = (weights, first_in, second_in, feed_grad, attention, qkv_t, norm_t, stat_t, mixed, gu_t, hidden,
             down_part.reshape(4, 2, C_ROWS, D))
    result, tokens_grad, summed, pay_all = backward(saved, image_counts, tokens, out_grad, mod, qk_scale, table)
    qkv_weight_grad, out_weight_grad, gate_up_grad, down_grad = unpack_grads(summed)

    cond_all = cond_all.reshape(4 * images, -1)
    condition = cond_all[:, :columns_here]
    chosen = low(cond_all[:, columns_here].astype(jnp.int32)[:, None] == classes[None, :])
    cond_act = low(jax.nn.silu(condition))
    first_image = lax.axis_index("dp") * images
    pay_all = pay_all.reshape(32, 2, 8, D)
    mod_grad = pay_all[:, :, :6].reshape(-1, 6, D)
    scale_all = wide(pay_all[:, 1, 6, : 2 * HD])
    qk_scale_grad = jnp.sum(scale_all, axis=0).reshape(2, HD)
    bias_all = wide(pay_all[:, 0, 6:, : 4 * 256]).reshape(32, 8, 256)[..., :QKV]
    bias_all = lax.dynamic_index_in_dim(bias_all, t, 1, keepdims=False).reshape(2, 2, 8, 3, HD)
    bias_sum = jnp.sum(bias_all, axis=(0, 2))
    qkv_bias_grad = bias_sum.swapaxes(0, 1).reshape(3, 2 * HD)
    ada_weight_grad = dot("ic,ikd->ckd", cond_act, mod_grad)
    ada_bias_grad = jnp.sum(wide(mod_grad), axis=0)
    act_grad = dot("ikd,ckd->ic", mod_grad, ada_weight)
    cond_grad_all = act_grad * silu_slope(condition)
    table_grad = jnp.dot(wide(chosen).T, cond_grad_all, precision=HIGH)
    cond_grad = lax.dynamic_slice_in_dim(cond_grad_all, first_image, images, 0)
    return (
        result, tokens_grad, cond_grad, table_grad, ada_weight_grad, ada_bias_grad,
        qkv_weight_grad, qkv_bias_grad, qk_scale_grad, out_weight_grad, gate_up_grad, down_grad,
    )


def rope_tables(count):
    pairs = HD // 4
    theta = jnp.exp(-math.log(100.0) * jnp.arange(pairs, dtype=jnp.float32) / pairs)
    place = jnp.arange(count) % PATCH
    row_angle = (place // GRID).astype(jnp.float32)[:, None] * theta
    col_angle = (place % GRID).astype(jnp.float32)[:, None] * theta
    return ((jnp.cos(row_angle), jnp.sin(row_angle)), (jnp.cos(col_angle), jnp.sin(col_angle)))


def rotate_part(segment, cosine, sine, direction):
    half_len = segment.shape[-1] // 2
    first, second = (segment[..., :half_len], segment[..., half_len:])
    cosine = cosine[:, None, :]
    sine = direction * sine[:, None, :]
    return jnp.concatenate(
        [first * cosine - second * sine, second * cosine + first * sine], axis=-1
    )


def rotate(vectors, tables, direction):
    half_len = vectors.shape[-1] // 2
    return jnp.concatenate(
        [
            rotate_part(vectors[..., :half_len], tables[0][0], tables[0][1], direction),
            rotate_part(vectors[..., half_len:], tables[1][0], tables[1][1], direction),
        ],
        axis=-1,
    )


def general(
    tokens,
    labels,
    timesteps,
    image_counts,
    class_table,
    ada_weight,
    ada_bias,
    qkv_weight,
    qkv_bias,
    qk_scale,
    out_weight,
    gate_up_weight,
    down_weight,
    out_grad,
):
    width = tokens.shape[1]
    local_rows = tokens.shape[0]
    members = lax.axis_size("tensor")
    place = lax.axis_index("tensor")
    images = labels.shape[0]
    all_rows = local_rows * members
    columns_here = class_table.shape[1]
    heads_here = columns_here // HD
    column = place * columns_here + jnp.arange(columns_here)
    half_width = width // 2
    frequency = jnp.exp(-math.log(10000.0) * (column % half_width).astype(jnp.float32) / half_width)
    angles = timesteps.astype(jnp.float32)[:, None] * frequency[None, :]
    time_embed = jnp.where(column[None, :] < half_width, jnp.cos(angles), jnp.sin(angles))
    chosen = (labels[:, None] == jnp.arange(class_table.shape[0])[None, :]).astype(jnp.bfloat16)
    condition = jnp.dot(chosen, class_table, preferred_element_type=jnp.float32) + time_embed
    cond_act = jax.nn.silu(condition).astype(jnp.bfloat16)
    mod_part = jnp.einsum("ic,ckd->ikd", cond_act, ada_weight, preferred_element_type=jnp.float32)
    modulation = lax.psum(mod_part, "tensor") + ada_bias.astype(jnp.float32)
    row_index = place * local_rows + jnp.arange(local_rows)
    row_image = row_index // PATCH
    selector = (row_image[:, None] == jnp.arange(images)[None, :]).astype(jnp.float32)
    mod_rows = jnp.dot(selector, modulation.reshape(images, 6 * width), precision=HIGH).reshape(
        local_rows, 6, width
    )
    kept = (row_image < image_counts[0]).astype(jnp.float32)[:, None]
    shift_one, scale_one, gate_one, shift_two, scale_two, gate_two = [
        mod_rows[:, index] for index in range(6)
    ]
    tokens_f = tokens.astype(jnp.float32)
    first_norm, first_inverse = normalize(tokens_f)
    first_in = (first_norm * (1.0 + scale_one) + shift_one).astype(jnp.bfloat16)
    first_all = lax.all_gather(first_in, "tensor", axis=0, tiled=True)
    qkv = jnp.einsum(
        "nd,dkc->nkc", first_all, qkv_weight, preferred_element_type=jnp.float32
    ) + qkv_bias.astype(jnp.float32)
    head_view = qkv.reshape(all_rows, 3, heads_here, HD)
    tables = rope_tables(all_rows)
    qk_gains = qk_scale.astype(jnp.float32)
    query_normed, query_inverse = normalize(head_view[:, 0])
    key_normed, key_inverse = normalize(head_view[:, 1])
    block_shape = (all_rows // PATCH, PATCH, heads_here, HD)
    queries = (
        rotate(query_normed * qk_gains[0], tables, 1.0).astype(jnp.bfloat16).reshape(block_shape)
    )
    keys_rot = (
        rotate(key_normed * qk_gains[1], tables, 1.0).astype(jnp.bfloat16).reshape(block_shape)
    )
    values = head_view[:, 2].astype(jnp.bfloat16).reshape(block_shape)
    factor = HD ** (-0.5)
    scores = (
        jnp.einsum("iqhe,ikhe->ihqk", queries, keys_rot, preferred_element_type=jnp.float32)
        * factor
    )
    row_max = jnp.max(scores, axis=-1, keepdims=True)
    exponent = jnp.exp(scores - row_max)
    totals = jnp.sum(exponent, axis=-1, keepdims=True)
    logsum = row_max + jnp.log(totals)
    probability = (exponent / totals).astype(jnp.bfloat16)
    mixed_heads = (
        jnp.einsum("ihqk,ikhe->iqhe", probability, values, preferred_element_type=jnp.float32)
        .reshape(all_rows, columns_here)
        .astype(jnp.bfloat16)
    )
    attention = lax.psum_scatter(
        jnp.dot(mixed_heads, out_weight, preferred_element_type=jnp.float32).astype(jnp.bfloat16),
        "tensor",
        scatter_dimension=0,
        tiled=True,
    ).astype(jnp.float32)
    after_attn = tokens_f + kept * gate_one * attention
    second_norm, second_inverse = normalize(after_attn)
    second_in = (second_norm * (1.0 + scale_two) + shift_two).astype(jnp.bfloat16)
    second_all = lax.all_gather(second_in, "tensor", axis=0, tiled=True)
    gate_up = jnp.einsum(
        "nd,dkf->nkf", second_all, gate_up_weight, preferred_element_type=jnp.float32
    )
    gate_value, up_value = (gate_up[:, 0], gate_up[:, 1])
    activated = jax.nn.silu(gate_value)
    hidden = (activated * up_value).astype(jnp.bfloat16)
    feed = lax.psum_scatter(
        jnp.dot(hidden, down_weight, preferred_element_type=jnp.float32).astype(jnp.bfloat16),
        "tensor",
        scatter_dimension=0,
        tiled=True,
    ).astype(jnp.float32)
    result = (after_attn + kept * gate_two * feed).astype(jnp.bfloat16)
    grad_out = out_grad.astype(jnp.float32)
    feed_grad = (grad_out * kept * gate_two).astype(jnp.bfloat16)
    gate_two_grad = grad_out * kept * feed
    feed_grad_all = lax.all_gather(feed_grad, "tensor", axis=0, tiled=True)
    hidden_grad = jnp.einsum(
        "nd,fd->nf", feed_grad_all, down_weight, preferred_element_type=jnp.float32
    )
    down_grad = jnp.einsum("nf,nd->fd", hidden, feed_grad_all, preferred_element_type=jnp.float32)
    gate_grad = hidden_grad * up_value * silu_slope(gate_value)
    up_grad = hidden_grad * activated
    gu_grad = jnp.stack([gate_grad, up_grad], axis=1).astype(jnp.bfloat16)
    gate_up_grad = jnp.einsum(
        "nd,nkf->dkf", second_all, gu_grad, preferred_element_type=jnp.float32
    )
    second_grad = lax.psum_scatter(
        jnp.einsum(
            "nkf,dkf->nd", gu_grad, gate_up_weight, preferred_element_type=jnp.float32
        ).astype(jnp.bfloat16),
        "tensor",
        scatter_dimension=0,
        tiled=True,
    ).astype(jnp.float32)
    after_grad = grad_out + normalize_back(
        second_grad * (1.0 + scale_two), second_norm, second_inverse
    )
    attention_grad = (after_grad * kept * gate_one).astype(jnp.bfloat16)
    gate_one_grad = after_grad * kept * attention
    attention_grad_all = lax.all_gather(attention_grad, "tensor", axis=0, tiled=True)
    mixed_grad = jnp.einsum(
        "nd,cd->nc", attention_grad_all, out_weight, preferred_element_type=jnp.float32
    ).astype(jnp.bfloat16)
    out_weight_grad = jnp.einsum(
        "nc,nd->cd", mixed_heads, attention_grad_all, preferred_element_type=jnp.float32
    )
    scores_again = (
        jnp.einsum("iqhe,ikhe->ihqk", queries, keys_rot, preferred_element_type=jnp.float32)
        * factor
    )
    prob_again = jnp.exp(scores_again - logsum)
    mixed_blocks = mixed_grad.reshape(block_shape)
    values_grad = jnp.einsum(
        "ihqk,iqhe->ikhe",
        prob_again.astype(jnp.bfloat16),
        mixed_blocks,
        preferred_element_type=jnp.float32,
    )
    prob_grad = jnp.einsum(
        "iqhe,ikhe->ihqk", mixed_blocks, values, preferred_element_type=jnp.float32
    )
    score_grad = (
        prob_again * (prob_grad - jnp.sum(prob_again * prob_grad, axis=-1, keepdims=True))
    ).astype(jnp.bfloat16)
    queries_grad = (
        jnp.einsum("ihqk,ikhe->iqhe", score_grad, keys_rot, preferred_element_type=jnp.float32)
        * factor
    )
    keys_grad = (
        jnp.einsum("ihqk,iqhe->ikhe", score_grad, queries, preferred_element_type=jnp.float32)
        * factor
    )
    query_back = rotate(queries_grad.reshape(all_rows, heads_here, HD), tables, -1.0)
    key_back = rotate(keys_grad.reshape(all_rows, heads_here, HD), tables, -1.0)
    scale_part = jnp.stack(
        [
            jnp.sum(query_back * query_normed, axis=(0, 1)),
            jnp.sum(key_back * key_normed, axis=(0, 1)),
        ]
    )
    query_raw = normalize_back(query_back * qk_gains[0], query_normed, query_inverse)
    key_raw = normalize_back(key_back * qk_gains[1], key_normed, key_inverse)
    qkv_grad = (
        jnp.stack([query_raw, key_raw, values_grad.reshape(all_rows, heads_here, HD)], axis=1)
        .reshape(all_rows, 3, columns_here)
        .astype(jnp.bfloat16)
    )
    qkv_weight_grad = jnp.einsum(
        "nd,nkc->dkc", first_all, qkv_grad, preferred_element_type=jnp.float32
    )
    qkv_bias_grad = jnp.sum(qkv_grad.astype(jnp.float32), axis=0)
    first_grad = lax.psum_scatter(
        jnp.einsum("nkc,dkc->nd", qkv_grad, qkv_weight, preferred_element_type=jnp.float32).astype(
            jnp.bfloat16
        ),
        "tensor",
        scatter_dimension=0,
        tiled=True,
    ).astype(jnp.float32)
    tokens_grad = after_grad + normalize_back(
        first_grad * (1.0 + scale_one), first_norm, first_inverse
    )
    row_mod_grad = jnp.stack(
        [
            first_grad,
            first_grad * first_norm,
            gate_one_grad,
            second_grad,
            second_grad * second_norm,
            gate_two_grad,
        ],
        axis=1,
    ).reshape(local_rows, 6 * width)
    mod_grad_part = jnp.dot(selector.T, row_mod_grad, precision=HIGH).reshape(images, 6, width)
    mod_grad, scale_grad = (
        lax.psum(mod_grad_part.astype(jnp.bfloat16), "tensor").astype(jnp.float32),
        lax.psum(scale_part.astype(jnp.bfloat16), "tensor").astype(jnp.float32),
    )
    mod_grad_low = mod_grad.astype(jnp.bfloat16)
    ada_weight_grad = jnp.einsum(
        "ic,ikd->ckd", cond_act, mod_grad_low, preferred_element_type=jnp.float32
    )
    ada_bias_grad = jnp.sum(mod_grad_low.astype(jnp.float32), axis=0)
    act_grad = jnp.einsum(
        "ikd,ckd->ic", mod_grad_low, ada_weight, preferred_element_type=jnp.float32
    )
    cond_grad = act_grad * silu_slope(condition)
    table_grad = jnp.dot(chosen.astype(jnp.float32).T, cond_grad, precision=HIGH)
    summed = (
        lax.psum(table_grad.astype(jnp.bfloat16), "dp").astype(jnp.float32),
        lax.psum(ada_weight_grad.astype(jnp.bfloat16), "dp").astype(jnp.float32),
        lax.psum(ada_bias_grad.astype(jnp.bfloat16), "dp").astype(jnp.float32),
        lax.psum(qkv_weight_grad.astype(jnp.bfloat16), "dp").astype(jnp.float32),
        lax.psum(qkv_bias_grad.astype(jnp.bfloat16), "dp").astype(jnp.float32),
        lax.psum(scale_grad.astype(jnp.bfloat16), "dp").astype(jnp.float32),
        lax.psum(out_weight_grad.astype(jnp.bfloat16), "dp").astype(jnp.float32),
        lax.psum(gate_up_grad.astype(jnp.bfloat16), "dp").astype(jnp.float32),
        lax.psum(down_grad.astype(jnp.bfloat16), "dp").astype(jnp.float32),
    )
    return (result, tokens_grad, cond_grad) + tuple(summed)


def solution(mesh):
    placed = (
        P(("dp", "tensor"), None),
        P("dp"),
        P("dp"),
        P("dp"),
        P(None, "tensor"),
        P("tensor", None, None),
        P(),
        P(None, None, "tensor"),
        P(None, "tensor"),
        P(),
        P("tensor", None),
        P(None, None, "tensor"),
        P("tensor", None),
        P(("dp", "tensor"), None),
    )
    plain = mesh.shape["dp"] != 4 or mesh.shape["tensor"] != 8
    return jax.shard_map(
        general if plain else fast,
        mesh=mesh,
        in_specs=placed,
        out_specs=(
            P(("dp", "tensor"), None),
            P(("dp", "tensor"), None),
            P("dp", "tensor"),
            P(None, "tensor"),
            P("tensor", None, None),
            P(),
            P(None, None, "tensor"),
            P(None, "tensor"),
            P(),
            P("tensor", None),
            P(None, None, "tensor"),
            P("tensor", None),
        ),
        check_vma=False,
    )
```

```python
import math

import jax
import jax.numpy as jnp
import numpy as np
from jax import lax
from jax.experimental import pallas as pl
from jax.experimental.pallas import tpu as pltpu
from jax.sharding import PartitionSpec as P

HD = 72
GRID = 16
PATCH = 256
HIGH = lax.Precision.HIGHEST
MESH = pl.DeviceIdType.MESH
epsilon = 1e-06
D = 1152

QKV = 3 * HD
A_ROWS = 4 * HD
SHARD_FF = 192
HALF_FF = SHARD_FF // 2
B_ROWS = 2 * SHARD_FF
C_ROWS = SHARD_FF
ROWS_ALL = A_ROWS + B_ROWS + C_ROWS
B_FIRST = A_ROWS
C_FIRST = A_ROWS + B_ROWS
HEAD = 80
O_FIRST = A_ROWS - HEAD
QKV_ROWS = 224
CHUNK = 64
FACTOR = HD ** (-0.5)
PAY = 16

G_STAGE, G_LONE = 48, 16
G_STAGES = ROWS_ALL // G_STAGE
G_TURNED = (3, 9, 15)
A_STAGES = A_ROWS // G_STAGE
HALF_STAGES = (A_ROWS + SHARD_FF) // G_STAGE
AB_STAGES = C_FIRST // G_STAGE

R_STAGE = 48
R_STAGES = ROWS_ALL // R_STAGE
D_STAGES = C_ROWS // R_STAGE
GU_STAGES = (C_ROWS + B_ROWS) // R_STAGE
X_RING, Y_RING, Z_RING = 8, 6, 8
AHEAD = 2


def place():
    d = lax.axis_index("dp")
    t = lax.axis_index("tensor")
    return d // 2, d % 2, t // 2, t % 2


def at(x, c, z, y):
    return (x * 2 + c, z * 2 + y)


def greet(targets):
    barrier = pltpu.get_barrier_semaphore()
    for o in targets:
        pl.semaphore_signal(barrier, inc=1, device_id=o, device_id_type=MESH)
    pl.semaphore_wait(barrier, len(targets))


def rows_at(first, size):
    return pl.ds(pl.multiple_of(first, 16), size)


def nt(a, b):
    return lax.dot_general(a, b, (((1,), (1,)), ((), ())), preferred_element_type=jnp.float32)


def tn(a, b):
    return lax.dot_general(a, b, (((0,), (0,)), ((), ())), preferred_element_type=jnp.float32)


def nn(a, b):
    return lax.dot_general(a, b, (((1,), (0,)), ((), ())), preferred_element_type=jnp.float32)


def low(v):
    return v.astype(jnp.bfloat16)


def wide(v):
    return v.astype(jnp.float32)


def turn(v, cos, sin):
    other = jnp.concatenate([v[18:36], v[:18], v[54:72], v[36:54]], axis=0)
    return v * cos + other * sin


def fill(v):
    return jnp.concatenate([v, jnp.zeros((HEAD - HD, v.shape[1]), v.dtype)], axis=0)


def columns(rows):
    k, n = rows.shape
    rows = jnp.concatenate([rows, jnp.zeros((k, 128 - n), jnp.float32)], axis=1)
    rows = jnp.concatenate([rows, jnp.zeros((128 - k, 128), jnp.float32)], axis=0)
    return jnp.transpose(rows)


def remote(src, dst, ss, rs, to):
    return pltpu.make_async_remote_copy(
        src_ref=src, dst_ref=dst, send_sem=ss, recv_sem=rs, device_id=to, device_id_type=MESH)


def forward_kernel(
    counts, qkv_hbm, out_hbm, gu_w, down_w, condition, labels, ada_hbm, ada_b, bias_w, tokens_hbm, out_grad_hbm, gains, table,
    full, cond_out, mod_out, fi_out, si_out, fg_out, att_out, qkv_out, norm_out, stat_out, mixed_out, gu_out, hid_out,
    dd_out,
    qkv_w, out_w, ada_w, tokens, out_grad, own, mod_in, mod_send, cond_in, mod_all, mod, fi, si, fg, att, att_send, att_recv, wa, ow, mixed, qkv, norm, stat, wb, gu,
    hid, dd,
    send, recv, ms, mr, cs, cr, es, er, ls, qs, hs, ws, save, fs,
):
    x, c, z, y = place()
    t = z * 2 + y
    d = x * 2 + c
    peers = [lax.rem(t + k, 8) for k in range(1, 8)]
    groups = [lax.rem(d + k, 4) for k in range(1, 4)]
    fetch = [
        pltpu.make_async_copy(src, dst, fs.at[i])
        for i, (src, dst) in enumerate(
            [(qkv_hbm, qkv_w), (out_hbm, out_w), (ada_hbm, ada_w), (tokens_hbm, tokens), (out_grad_hbm, out_grad)])
    ]
    for cp in fetch:
        cp.start()
    load_gu = pltpu.make_async_copy(gu_w, own.at[pl.ds(B_FIRST, B_ROWS)], ls.at[4])
    load_gu.start()
    load_down = pltpu.make_async_copy(
        down_w.at[rows_at(c * C_ROWS, C_ROWS)], own.at[pl.ds(C_FIRST, C_ROWS)], ls.at[5])
    load_down.start()
    fetch[0].wait()
    fetch[1].wait()
    for head in range(2):
        @pl.when(c == head)
        def _():
            cut = slice(head * HD, (head + 1) * HD)
            own[:A_ROWS, :] = low(jnp.concatenate(
                [wide(qkv_w[0, cut]), wide(qkv_w[1, cut]), wide(qkv_w[2, cut]), wide(out_w[cut])], axis=0))

    greet([(d, p) for p in peers] + [(g, t) for g in groups])
    y_side, x_side, core = at(x, c, z, 1 - y), at(1 - x, c, z, y), at(x, 1 - c, z, y)
    up, down = at(x, c, z + 1, y), at(x, c, z - 1, y)

    def plane(g):
        return rows_at(g * G_STAGE + x * G_LONE, G_STAGE - G_LONE)

    def lone(g, side):
        return rows_at(g * G_STAGE + side * (G_STAGE - G_LONE), G_LONE)

    def copy(g, kind, src, slot, rows, path, to):
        return remote(src.at[rows], full.at[slot, rows], send.at[g, kind], recv.at[g, slot, path], to)

    def arrived(g, slot, rows, path):
        copy(g, 0, own, slot, rows, path, x_side).wait_recv()

    def turned(g):
        found = g == G_TURNED[0]
        for other in G_TURNED[1:]:
            found = jnp.logical_or(found, g == other)
        return found

    def straight(g):
        return jnp.logical_not(turned(g))

    def issue(g):
        copy(g, 2, own, t, plane(g), 0, y_side).start()
        pl.when(z < 3)(lambda: copy(g, 0, own, t, plane(g), 0, up).start())
        pl.when(z > 0)(lambda: copy(g, 1, own, t, plane(g), 0, down).start())

    def along_z(g, j):
        def below():
            slot = (z - j) * 2 + y
            arrived(g, slot, plane(g), 0)
            pl.when(z < 3)(lambda: copy(g, 1 + 2 * j, full.at[slot], slot, plane(g), 0, up).start())
            pl.when(straight(g))(lambda: copy(g, 8 + j, full.at[slot], slot, plane(g), 0, y_side).start())
            copy(g, 11 + j, full.at[slot], slot, lone(g, x), 1, x_side).start()

        def above():
            slot = (z + j) * 2 + y
            arrived(g, slot, plane(g), 0)
            pl.when(z > 0)(lambda: copy(g, 2 + 2 * j, full.at[slot], slot, plane(g), 0, down).start())
            pl.when(straight(g))(lambda: copy(g, 14 + j, full.at[slot], slot, plane(g), 0, y_side).start())
            copy(g, 17 + j, full.at[slot], slot, lone(g, x), 1, x_side).start()

        pl.when(z >= j)(below)
        pl.when(z + j <= 3)(above)

    def along_y(g, j, above):
        zz = z + j if above else z - j
        slot = zz * 2 + 1 - y
        arrived(g, slot, plane(g), 0)

        @pl.when(turned(g))
        def _():
            if j == 0 or not above:
                kind = 25 if j == 0 else 8 + j
                pl.when(z < 3)(lambda: copy(g, kind, full.at[slot], slot, plane(g), 0, up).start())
            if j == 0 or above:
                kind = 26 if j == 0 else 14 + j
                pl.when(z > 0)(lambda: copy(g, kind, full.at[slot], slot, plane(g), 0, down).start())

        copy(g, 21 + zz, full.at[slot], slot, lone(g, x), 1, x_side).start()

    def service(i):
        def on(g, act):
            pl.when(jnp.logical_and(g >= 0, g < G_STAGES))(lambda: act(g))

        on(i, issue)
        for j in (1, 2, 3):
            on(i - j, lambda g: along_z(g, j))
        on(i - 1, lambda g: along_y(g, 0, False))
        for j in (1, 2, 3):
            @pl.when(z >= j)
            def _():
                on(i - j - 1, lambda g: along_y(g, j, False))

            @pl.when(z + j <= 3)
            def _():
                on(i - j - 1, lambda g: along_y(g, j, True))

    def lone_in(first, last):
        @pl.loop(first, last)
        def _(g):
            for k in range(1, 8):
                arrived(g, lax.rem(t + k, 8), lone(g, 1 - x), 1)

    def mod_row(image, k):
        return mod[pl.ds(image * 8 + k, 1), :]

    def by_rows(act):
        for image in range(2):
            @pl.loop(0, PATCH // CHUNK)
            def _(i):
                act(image, rows_at(image * PATCH + i * CHUNK, CHUNK))

    service(0)

    cond_in[...] = jnp.zeros_like(cond_in)
    cond_in[:, :144] = condition[...]
    cond_in[:, 144:145] = wide(labels[...])
    mod_in[...] = jnp.zeros_like(mod_in)
    for p in range(8):
        for k, row in enumerate((6, 7, 14)):
            mod_in[p, row : row + 1, :144] = wide(bias_w[k : k + 1, :])
    load_gu.wait()
    load_down.wait()
    kept = [pltpu.make_async_copy(own, full.at[t], ls.at[0])]
    kept[0].start()
    fetch[2].wait()
    service(1)
    v = condition[...]
    act = low(v * (1.0 / (1.0 + jnp.exp(-v))))
    for k in range(6):
        share = nn(act, ada_w[k])
        for image in range(16):
            mod_in[image // 2, image % 2 * 8 + k : image % 2 * 8 + k + 1, :] = share[image : image + 1]
    mod_send[...] = low(mod_in[...])
    small = []
    for k, p in enumerate(peers):
        small.append(remote(mod_send.at[p], mod_all.at[t], ms.at[k], mr.at[t], (d, p)))
    for k, g in enumerate(groups):
        small.append(remote(cond_in, cond_out.at[d], cs.at[k], cr.at[d], (g, t)))
    for cp in small:
        cp.start()
    kept += [
        pltpu.make_async_copy(mod_send.at[t], mod_all.at[t], ls.at[1]),
        pltpu.make_async_copy(cond_in, cond_out.at[d], ls.at[2]),
    ]
    kept[1].start()
    kept[2].start()
    service(2)
    fetch[3].wait()
    fetch[4].wait()
    service(3)
    for p in peers:
        remote(mod_send.at[p], mod_all.at[p], ms.at[0], mr.at[p], (d, p)).wait_recv()
    kept[1].wait()
    for image in range(2):
        total = jnp.concatenate([wide(ada_b[...]), jnp.zeros((2, D), jnp.float32)], axis=0)
        for s in range(8):
            total = total + wide(mod_all[s])[image * 8 : image * 8 + 8]
        real = jnp.where(t * 2 + image < counts[0], 1.0, 0.0)
        row = lax.broadcasted_iota(jnp.int32, (8, D), 0)
        gate = jnp.logical_or(row == 2, row == 5)
        mod[image * 8 : image * 8 + 8, :] = jnp.where(gate, total * real, total)
    service(4)

    def first_rows(image, rows):
        v = wide(tokens[rows, :])
        n = v * lax.rsqrt(jnp.mean(v * v, axis=-1, keepdims=True) + epsilon)
        fi[0, rows, :] = low(n * (1.0 + mod_row(image, 1)) + mod_row(image, 0))

    def feed_rows(image, rows):
        fg[0, rows, :] = low(wide(out_grad[rows, :]) * mod_row(image, 5))

    by_rows(first_rows)
    share_fi = remote(fi.at[0], fi.at[1], es.at[0], er.at[0], core)
    share_fi.start()
    service(5)
    by_rows(feed_rows)
    share_fg = remote(fg.at[0], fg.at[1], es.at[1], er.at[1], core)
    share_fg.start()

    @pl.loop(6, A_STAGES + 4)
    def _(i):
        service(i)

    kept[0].wait()
    lone_in(0, A_STAGES)
    share_fi.wait_recv()
    share_fg.wait_recv()
    saves = [
        pltpu.make_async_copy(fi, fi_out, save.at[0]),
        pltpu.make_async_copy(fg, fg_out, save.at[1]),
        pltpu.make_async_copy(mod, mod_out, save.at[2]),
    ]
    for cp in saves:
        cp.start()

    def load_a(s):
        return pltpu.make_async_copy(full.at[s, pl.ds(0, QKV_ROWS)], wa.at[lax.rem(s, 2)], ws.at[lax.rem(s, 2)])

    load_o = pltpu.make_async_copy(full.at[:, pl.ds(O_FIRST, HEAD)], ow, ls.at[3])
    load_o.start()
    load_a(0).start()
    gain_cols = columns(wide(gains[...]))

    def save_head(s):
        b = lax.rem(s, 2)
        return [
            pltpu.make_async_copy(qkv.at[b], qkv_out.at[s], qs.at[b, 0]),
            pltpu.make_async_copy(norm.at[b], norm_out.at[s], qs.at[b, 1]),
            pltpu.make_async_copy(stat.at[b], stat_out.at[s], qs.at[b, 2]),
        ]

    @pl.loop(0, 8)
    def _(s):
        b = lax.rem(s, 2)
        load_a(s).wait()
        pl.when(s < 7)(lambda: load_a(s + 1).start())

        @pl.when(s > 1)
        def _():
            for cp in save_head(s - 2):
                cp.wait()

        bias_rows = wide(mod_all[s, :, :256])
        bias_rows = jnp.concatenate([bias_rows[6:8, :144], bias_rows[14:15, :144]], axis=0)
        bias = columns(jnp.where(c == 0, bias_rows[:, :HD], bias_rows[:, HD:]))
        cos, sin = table[:HD, :], table[HD:, :]
        for h in range(2):
            raw = nt(wa[b], fi[h])
            for i in range(2):
                v = raw[i * HD : (i + 1) * HD] + bias[:HD, i : i + 1]
                inv = lax.rsqrt(jnp.sum(v * v, axis=0, keepdims=True) * (1.0 / HD) + epsilon)
                n = v * inv
                norm[b, h, i * HEAD : (i + 1) * HEAD, :] = low(fill(n))
                stat[b, h, i : i + 1, :] = inv
                qkv[b, h, i * HEAD : (i + 1) * HEAD, :] = low(fill(turn(n * gain_cols[:HD, i : i + 1], cos, sin)))
            v = low(fill(raw[2 * HD : 3 * HD] + bias[:HD, 2:3]))
            qkv[b, h, 2 * HEAD :, :] = v
            for image in range(2):
                cut = slice(image * PATCH, (image + 1) * PATCH)
                e = jnp.exp(tn(qkv[b, h, HEAD : 2 * HEAD, cut], qkv[b, h, :HEAD, cut]) * FACTOR)
                row_sum = jnp.sum(e, axis=0, keepdims=True)
                stat[b, h, 2:3, cut] = jnp.log(row_sum)
                p = low(e * (1.0 / row_sum))
                m = nn(v[:, cut], p)
                m = jnp.concatenate([m[HD:], m[:HD]], axis=0)
                mixed[h, pl.ds(pl.multiple_of(s * HEAD, 16), HEAD), cut] = low(m)
        for cp in save_head(s):
            cp.start()

        pl.when(jnp.logical_or(lax.rem(s, 5) == 0, jnp.logical_or(lax.rem(s, 5) == 2, s == 3)))(
            lambda: service(A_STAGES + 4 + (s + 1) // 2))

    for s in (6, 7):
        for cp in save_head(s):
            cp.wait()
    load_o.wait()
    saves.append(pltpu.make_async_copy(mixed, mixed_out, save.at[3]))
    saves[-1].start()

    for image in range(2):
        cut = slice(image * PATCH, (image + 1) * PATCH)
        att_send[cut, :] = low(tn(mixed[1, :, cut], ow[...].reshape(8 * HEAD, D)))
    share_att = remote(att_send, att_recv, es.at[2], er.at[2], core)
    share_att.start()
    for image in range(2):
        cut = slice(image * PATCH, (image + 1) * PATCH)
        att[cut, :] = tn(mixed[0, :, cut], ow[...].reshape(8 * HEAD, D))
    service(A_STAGES + 9)
    share_att.wait_recv()

    def second_rows(image, rows):
        a = att[rows, :] + wide(att_recv[rows, :])
        att[rows, :] = a
        v = wide(tokens[rows, :]) + mod_row(image, 2) * a
        n = v * lax.rsqrt(jnp.mean(v * v, axis=-1, keepdims=True) + epsilon)
        si[0, rows, :] = low(n * (1.0 + mod_row(image, 4)) + mod_row(image, 3))

    by_rows(second_rows)
    share_si = remote(si.at[0], si.at[1], es.at[3], er.at[3], core)
    share_si.start()
    service(A_STAGES + 10)

    share_si.wait_recv()
    saves += [
        pltpu.make_async_copy(att, att_out, save.at[4]),
        pltpu.make_async_copy(si, si_out, save.at[5]),
    ]
    saves[-2].start()
    saves[-1].start()

    def load_b(half, p):
        b = lax.rem(p, 2)
        return pltpu.make_async_copy(
            full.at[pl.ds(p * 2, 2), pl.ds(B_FIRST + half * SHARD_FF, SHARD_FF)], wb.at[b], ws.at[2 + b])

    def save_pair(half, p):
        b = lax.rem(p, 2)
        both = pl.ds(p * 2, 2)
        return [
            pltpu.make_async_copy(gu.at[b], gu_out.at[both, half], hs.at[b, 0]),
            pltpu.make_async_copy(hid.at[b], hid_out.at[both, half], hs.at[b, 1]),
            pltpu.make_async_copy(dd.at[b], dd_out.at[both, half], hs.at[b, 2]),
        ]

    for half in range(2):
        lone_in(A_STAGES + half * (HALF_STAGES - A_STAGES), HALF_STAGES + half * (HALF_STAGES - A_STAGES))
        load_b(half, 0).start()

        @pl.loop(0, 4)
        def _(p):
            b = lax.rem(p, 2)
            load_b(half, p).wait()
            pl.when(p < 3)(lambda: load_b(half, p + 1).start())

            @pl.when(p > 1)
            def _():
                for cp in save_pair(half, p - 2):
                    cp.wait()

            for h in range(2):
                both = nt(wb[b].reshape(2 * SHARD_FF, D), si[h])
                for i in range(2):
                    g = both[i * SHARD_FF : i * SHARD_FF + HALF_FF]
                    u = both[i * SHARD_FF + HALF_FF : (i + 1) * SHARD_FF]
                    hid[b, i, h] = low(g * (1.0 / (1.0 + jnp.exp(-g))) * u)
                    gu[b, i, h] = low(both[i * SHARD_FF : (i + 1) * SHARD_FF])
            grad = sum(
                nn(jnp.concatenate([hid[b, 0, h], hid[b, 1, h]], axis=0), fg[h]) for h in range(2))
            dd[b] = low(grad).reshape(2, HALF_FF, D)
            for cp in save_pair(half, p):
                cp.start()

            if half == 0:
                service(A_STAGES + 11 + p)
            else:
                pl.when(p == 2)(lambda: service(A_STAGES + 15))

        for p in (2, 3):
            for cp in save_pair(half, p):
                cp.wait()

    lone_in(AB_STAGES, G_STAGES)

    @pl.loop(0, G_STAGES)
    def _(g):
        def sent(kind, rows):
            copy(g, kind, own, t, rows, 0, x_side).wait_send()

        sent(2, plane(g))
        pl.when(z < 3)(lambda: sent(0, plane(g)))
        pl.when(z > 0)(lambda: sent(1, plane(g)))
        for k in range(4):
            sent(21 + k, lone(g, x))
        pl.when(jnp.logical_and(turned(g), z < 3))(lambda: sent(25, plane(g)))
        pl.when(jnp.logical_and(turned(g), z > 0))(lambda: sent(26, plane(g)))
        for j in (1, 2, 3):
            @pl.when(z >= j)
            def _():
                pl.when(z < 3)(lambda: sent(1 + 2 * j, plane(g)))
                pl.when(jnp.logical_or(straight(g), z < 3))(lambda: sent(8 + j, plane(g)))
                sent(11 + j, lone(g, x))

            @pl.when(z + j <= 3)
            def _():
                pl.when(z > 0)(lambda: sent(2 + 2 * j, plane(g)))
                pl.when(jnp.logical_or(straight(g), z > 0))(lambda: sent(14 + j, plane(g)))
                sent(17 + j, lone(g, x))

    for cp in small + [share_fi, share_fg, share_att, share_si]:
        cp.wait_send()
    for g in groups:
        remote(cond_in, cond_out.at[g], cs.at[0], cr.at[g], (g, t)).wait_recv()
    kept[2].wait()
    for cp in saves:
        cp.wait()


def forward(counts, qkv_w, out_w, gu_w, down_w, condition, labels, ada_w, ada_b, bias_w, tokens, out_grad, gains, table):
    dma = pltpu.SemaphoreType.DMA
    vm = pltpu.VMEM
    bf, f32 = jnp.bfloat16, jnp.float32
    anywhere = pl.BlockSpec(memory_space=pl.ANY)
    inside = pl.BlockSpec(memory_space=pltpu.VMEM)
    scalar = pl.BlockSpec(memory_space=pltpu.SMEM)
    R = tokens.shape[0]
    outs = [
        ((8, ROWS_ALL, D), bf), ((4, 16, 256), f32), ((16, D), f32),
        ((2, R, D), bf), ((2, R, D), bf), ((2, R, D), bf), ((R, D), f32),
        ((8, 2, 3 * HEAD, R), bf), ((8, 2, 2 * HEAD, R), bf), ((8, 2, 8, R), f32), ((2, 8 * HEAD, R), bf),
        ((8, 2, 2, SHARD_FF, R), bf), ((8, 2, 2, HALF_FF, R), bf), ((8, 2, HALF_FF, D), bf),
    ]
    return pl.pallas_call(
        forward_kernel,
        out_shape=tuple(jax.ShapeDtypeStruct(s, e) for s, e in outs),
        in_specs=[scalar] + [anywhere] * 4 + [inside] * 2 + [anywhere] + [inside] * 2 + [anywhere] * 2 + [inside] * 2,
        out_specs=(anywhere,) * len(outs),
        scratch_shapes=[
            vm((3, 144, D), bf), vm((144, D), bf), vm((6, 144, D), bf), vm((R, D), bf), vm((R, D), bf),
            vm((ROWS_ALL, D), bf), vm((8, 16, D), f32), vm((8, 16, D), bf), vm((16, 256), f32), vm((8, 16, D), bf),
            vm((16, D), f32),
            vm((2, R, D), bf), vm((2, R, D), bf), vm((2, R, D), bf), vm((R, D), f32), vm((R, D), bf), vm((R, D), bf),
            vm((2, QKV_ROWS, D), bf), vm((8, HEAD, D), bf), vm((2, 8 * HEAD, R), bf),
            vm((2, 2, 3 * HEAD, R), bf), vm((2, 2, 2 * HEAD, R), bf), vm((2, 2, 8, R), f32),
            vm((2, 2, SHARD_FF, D), bf), vm((2, 2, 2, SHARD_FF, R), bf), vm((2, 2, 2, HALF_FF, R), bf),
            vm((2, 2, HALF_FF, D), bf),
            dma((G_STAGES, 27)), dma((G_STAGES, 8, 2)), dma((7,)), dma((8,)), dma((3,)), dma((4,)),
            dma((4,)), dma((4,)), dma((6,)), dma((2, 3)), dma((2, 3)), dma((6,)), dma((6,)), dma((5,)),
        ],
        compiler_params=pltpu.CompilerParams(
            collective_id=0, has_side_effects=True, vmem_limit_bytes=60 * 2**20),
        name="forward",
    )(counts, qkv_w, out_w, gu_w, down_w, condition, labels, ada_w, ada_b, bias_w, tokens, out_grad, gains, table)


def backward_kernel(
    full, fi_in, si_in, fg_in, att_in, qkv_in, norm_in, stat_in, mixed_in, gu_in, hid_in, dd_in,
    counts, tokens_hbm, out_grad_hbm, ada_hbm, mod, gains, table, cond,
    result_out, tokens_out, grads, pay_all, sums_out, bias_out, cond_out, class_out,
    tokens, out_grad, ada_w, cond_all, part, xin, yin, zin, fin, buf_a, buf_b, acc, after, att, sent, came, came_feed, result,
    wd, wb, wa, hid, gu, qkv, norm, stat, mixed, dqkv, dlow, gain_sum, payf, pay,
    xs, xr, ys, yr, zs, zr, fs, fr, es, er, ps, pr, ls, lw, x_free, y_free, z_free,
):
    x, c, z, y = place()
    t = z * 2 + y
    d = x * 2 + c
    y_side, x_side, core = at(x, c, z, 1 - y), at(1 - x, c, z, y), at(x, 1 - c, z, y)
    up, down = at(x, c, z + 1, y), at(x, c, z - 1, y)
    mates = [at(x, c, lax.rem(z + k, 4), y) for k in (1, 2, 3)] + [x_side, y_side]

    loads = [
        pltpu.make_async_copy(fg_in, buf_a, ls.at[0]),
        pltpu.make_async_copy(si_in, buf_b, ls.at[1]),
        pltpu.make_async_copy(att_in, att, ls.at[2]),
        pltpu.make_async_copy(tokens_hbm, tokens, ls.at[7]),
        pltpu.make_async_copy(out_grad_hbm, out_grad, ls.at[8]),
        pltpu.make_async_copy(ada_hbm, ada_w, ls.at[9]),
    ]
    load_dd = pltpu.make_async_copy(
        dd_in, part.at[:, :, pl.ds(C_FIRST, C_ROWS)], ls.at[6])
    load_dd.start()
    greet(mates + [core])
    for cp in loads:
        cp.start()

    def first_of(g):
        return ROWS_ALL - (g + 1) * R_STAGE

    def rows_of(g):
        return rows_at(first_of(g), R_STAGE)

    def side_y(side):
        return 1 - y if side == 0 else y

    def lone_z(g, yy):
        return jnp.where(yy == lax.rem(x + g, 2), 1, 2)

    def xcopy(g, side):
        yy = side_y(side)
        return remote(
            part.at[3 - lone_z(g, yy), yy, rows_of(g)], xin.at[lax.rem(g, X_RING), side],
            xs.at[g, side], xr.at[g, side], x_side)

    def ycopy(g, k):
        yy = 1 - y
        zz = (0, 3, lone_z(g, yy))[k]
        return remote(part.at[zz, yy, rows_of(g)], yin.at[lax.rem(g, Y_RING), k], ys.at[g, k], yr.at[g, k], y_side)

    def zcopy(g, way, k):
        zz = (3 - 3 * way) if k == 0 else lone_z(g, y)
        return remote(
            part.at[zz, y, rows_of(g)], zin.at[lax.rem(g, Z_RING), way * 2 + k],
            zs.at[g, way * 2 + k], zr.at[g, way * 2 + k], up if way == 0 else down)

    def plane_sum(g):
        return remote(part.at[z, y, rows_of(g)], fin.at[rows_of(g)], fs.at[g, 0], fr.at[g, 0], x_side)

    def finished(g):
        return remote(part.at[z, y, rows_of(g)], grads.at[c, rows_of(g)], fs.at[g, 0], fr.at[g, 0], x_side)

    def core_copy(g, here):
        src = part.at[z, y, rows_of(g)] if here else grads.at[c, rows_of(g)]
        return remote(src, grads.at[c, rows_of(g)], fs.at[g, 1], fr.at[g, 1], core)

    def own_copy(g):
        return pltpu.make_async_copy(part.at[z, y, rows_of(g)], grads.at[c, rows_of(g)], fs.at[g, 2])

    def add(zz, yy, g, piece):
        first = first_of(g)

        @pl.loop(0, R_STAGE // 16)
        def _(i):
            a = rows_at(first + i * 16, 16)
            part[zz, yy, a, :] = low(wide(part[zz, yy, a, :]) + wide(piece(rows_at(i * 16, 16))))

    def send(g, side):
        if side == 0:
            pl.when(g >= X_RING)(lambda: pl.semaphore_wait(x_free, 1))
            pl.when(g >= Y_RING)(lambda: pl.semaphore_wait(y_free, 1))
        xcopy(g, side).start()
        if side == 0:
            ycopy(g, 0).start()
            ycopy(g, 1).start()

    def x_stage(g):
        b = lax.rem(g, X_RING)
        for side in (0, 1):
            yy = side_y(side)
            xcopy(g, side).wait_recv()
            add(lone_z(g, yy), yy, g, lambda r: xin[b, side, r, :])
            if side == 0:
                ycopy(g, 2).start()
        pl.when(g + X_RING < R_STAGES)(
            lambda: pl.semaphore_signal(x_free, inc=1, device_id=x_side, device_id_type=MESH))

    def y_stage(g):
        b = lax.rem(g, Y_RING)
        for k in range(3):
            ycopy(g, k).wait_recv()
            add((0, 3, lone_z(g, y))[k], y, g, lambda r: yin[b, k, r, :])
        pl.when(g + Y_RING < R_STAGES)(
            lambda: pl.semaphore_signal(y_free, inc=1, device_id=y_side, device_id_type=MESH))

    def take(g, way, k):
        zcopy(g, way, k).wait_recv()
        zz = (3 - 3 * way) if k == 0 else lone_z(g, y)
        add(zz, y, g, lambda r: zin[lax.rem(g, Z_RING), way * 2 + k, r, :])

    def z_stage(g, way):
        further = z < 3 if way == 0 else z > 0
        first = z == 0 if way == 0 else z == 3

        @pl.when(further)
        def _():
            pl.when(g >= Z_RING)(lambda: pl.semaphore_wait(z_free.at[way], 1))
            pl.when(jnp.logical_not(first))(lambda: take(g, way, 0))
            zcopy(g, way, 0).start()

        lone = lone_z(g, y)

        @pl.when(z < lone if way == 0 else z > lone)
        def _():
            pl.when(jnp.logical_not(first))(lambda: take(g, way, 1))
            zcopy(g, way, 1).start()

    def own_stage(g):
        pl.when(z == 3)(lambda: take(g, 0, 0))
        pl.when(z == 0)(lambda: take(g, 1, 0))

        @pl.when(z == lone_z(g, y))
        def _():
            take(g, 0, 1)
            take(g, 1, 1)
            finished(g).start()

        pl.when(jnp.logical_or(z == 0, z == 3))(lambda: plane_sum(g).start())

        @pl.when(g + Z_RING < R_STAGES)
        def _():
            pl.when(z > 0)(
                lambda: pl.semaphore_signal(z_free.at[0], inc=1, device_id=down, device_id_type=MESH))
            pl.when(z < 3)(
                lambda: pl.semaphore_signal(z_free.at[1], inc=1, device_id=up, device_id_type=MESH))

    def f_stage(g):
        ends = jnp.logical_or(z == 0, z == 3)
        here = z == lone_z(g, y)

        @pl.when(ends)
        def _():
            plane_sum(g).wait()
            add(z, y, g, lambda r: fin[rows_at(first_of(g) + r.start, 16), :])

        @pl.when(jnp.logical_or(ends, here))
        def _():
            own_copy(g).start()
            core_copy(g, True).start()

        @pl.when(z == 3 - lone_z(g, y))
        def _():
            finished(g).wait_recv()
            core_copy(g, False).start()

    def service(i, ready):
        def on(g, act):
            pl.when(jnp.logical_and(g >= 0, g < R_STAGES))(lambda: act(g))

        on(i, x_stage)
        on(i - 1, y_stage)
        on(i - 1 - z, lambda g: z_stage(g, 0))
        on(i - 4 + z, lambda g: z_stage(g, 1))
        on(i - 4, own_stage)
        on(i - 5, f_stage)

        @pl.when(i + AHEAD < ready)
        def _():
            send(i + AHEAD, 0)
            send(i + AHEAD, 1)

    def send_stages(first, last):
        @pl.loop(first, last)
        def _(g):
            send(g, 0)
            send(g, 1)

    def shard(k):
        return lax.rem(k, 4), jnp.where(k < 4, 1 - y, y)

    def slot(k):
        zz, yy = shard(k)
        return zz * 2 + yy

    def stream(pairs):
        def fetch(k):
            b = lax.rem(k, 2)
            return [pltpu.make_async_copy(src(slot(k)), buf.at[b], lw.at[n, b]) for src, buf, n in pairs]

        def begin(k):
            for cp in fetch(k):
                cp.start()

        def turn_to(k):
            for cp in fetch(k):
                cp.wait()
            pl.when(k < 7)(lambda: begin(k + 1))

        return begin, turn_to

    def mod_row(image, k):
        return mod[pl.ds(image * 8 + k, 1), :]

    def by_rows(act):
        for image in range(2):
            @pl.loop(0, PATCH // CHUNK)
            def _(i):
                act(image, rows_at(image * PATCH + i * CHUNK, CHUNK))

    def count(image, k, v):
        payf[pl.ds(image * 8 + k, 1), :] += jnp.sum(v, axis=0, keepdims=True)

    def clear(ref):
        @pl.loop(0, ref.shape[0] // 16)
        def _(i):
            ref[rows_at(i * 16, 16), :] = jnp.zeros((16, D), jnp.float32)

    def gather_sum(h, left, right):
        for image in range(2):
            cut = slice(image * PATCH, (image + 1) * PATCH)
            rows = slice(h * 512 + image * PATCH, h * 512 + (image + 1) * PATCH)
            acc[rows, :] += tn(left[:, cut], right)

    def share_half(number, landing):
        @pl.loop(0, 512 // CHUNK)
        def _(i):
            sent[rows_at(i * CHUNK, CHUNK), :] = low(acc[rows_at(512 + i * CHUNK, CHUNK), :])

        cp = remote(sent, landing, es.at[number], er.at[number], core)
        cp.start()
        return cp

    load_dd.wait()
    send_stages(0, AHEAD)
    payf[...] = jnp.zeros_like(payf)
    gain_sum[...] = jnp.zeros_like(gain_sum)
    clear(acc)
    begin_g, turn_g = stream([
        (lambda s: full.at[s, pl.ds(C_FIRST, C_ROWS)], wd, 1),
        (lambda s: full.at[s, pl.ds(B_FIRST, B_ROWS)], wb, 2),
        (lambda s: gu_in.at[s], gu, 3),
    ])
    begin_a, turn_a = stream([
        (lambda s: full.at[s, pl.ds(0, A_ROWS)], wa, 4),
        (lambda s: qkv_in.at[s], qkv, 5),
        (lambda s: norm_in.at[s], norm, 6),
        (lambda s: stat_in.at[s], stat, 7),
        (lambda s: mixed_in.at[:, rows_at(s * HEAD, HEAD)], mixed, 8),
    ])
    begin_f, turn_f = stream([
        (lambda s: hid_in.at[s], hid, 0),
        (lambda s: full.at[s, pl.ds(C_FIRST, C_ROWS)], wd, 1),
    ])
    begin_g(0)
    loads[0].wait()
    loads[1].wait()

    @pl.loop(0, 8)
    def _(k):
        b = lax.rem(k, 2)
        zz, yy = shard(k)
        turn_g(k)
        grads_here = []
        for h in range(2):
            hg = nt(wd[b], buf_a[h])
            both = []
            for half in range(2):
                g, u = wide(gu[b, half, h, :HALF_FF]), wide(gu[b, half, h, HALF_FF:])
                sig = 1.0 / (1.0 + jnp.exp(-g))
                act = g * sig
                this = hg[half * HALF_FF : (half + 1) * HALF_FF]
                both += [low(this * u * (sig + act * (1.0 - sig))), low(this * act)]
            both = jnp.concatenate(both, axis=0)
            grads_here.append(both)
            gather_sum(h, both, wb[b])
        part[zz, yy, B_FIRST:C_FIRST, :] = low(nn(grads_here[0], buf_b[0]) + nn(grads_here[1], buf_b[1]))

        pl.when(lax.rem(k, 2) == 1)(lambda: service(k // 2, D_STAGES))

    load_fi = pltpu.make_async_copy(fi_in, buf_a, ls.at[0])
    load_fi.start()
    share_second = share_half(0, came)
    send_stages(D_STAGES, D_STAGES + AHEAD)
    begin_a(0)
    service(D_STAGES, GU_STAGES)
    for cp in loads[2:]:
        cp.wait()
    share_second.wait_recv()

    def after_rows(image, rows):
        a = att[rows, :]
        v = wide(tokens[rows, :]) + mod_row(image, 2) * a
        inv = lax.rsqrt(jnp.mean(v * v, axis=-1, keepdims=True) + epsilon)
        n = v * inv
        sg = acc[rows, :] + wide(came[rows, :])
        dn = sg * (1.0 + mod_row(image, 4))
        ag = wide(out_grad[rows, :]) + inv * (dn - n * jnp.mean(dn * n, axis=-1, keepdims=True))
        after[rows, :] = ag
        buf_b[0, rows, :] = low(ag * mod_row(image, 2))
        count(image, 2, ag * a)
        count(image, 3, sg)
        count(image, 4, sg * n)

    by_rows(after_rows)
    share_ag = remote(buf_b.at[0], buf_b.at[1], es.at[1], er.at[1], core)
    share_ag.start()
    service(D_STAGES + 1, GU_STAGES)
    clear(acc)
    load_fi.wait()
    share_ag.wait_recv()

    gain_cols = columns(wide(gains[...]))

    @pl.loop(0, 8)
    def _(k):
        b = lax.rem(k, 2)
        zz, yy = shard(k)
        turn_a(k)
        cos, sin = table[:HD, :PATCH], table[HD:, :PATCH]
        out_part = nn(mixed[b, 0], buf_b[0]) + nn(mixed[b, 1], buf_b[1])
        for h in range(2):
            mg_all = nt(wa[b, O_FIRST:], buf_b[h])
            mg_all = low(fill(mg_all[HEAD - HD :]))
            dqkv[h, 3 * HD :, :] = jnp.zeros((QKV_ROWS - 3 * HD, 512), jnp.float32)
            for image in range(2):
                cut = slice(image * PATCH, (image + 1) * PATCH)
                q, kk, v = [qkv[b, h, i * HEAD : (i + 1) * HEAD, cut] for i in range(3)]
                mg = mg_all[:, cut]
                p = jnp.exp(tn(kk, q) * FACTOR - stat[b, h, 2:3, cut])
                dqkv[h, 2 * HD : 3 * HD, cut] = nt(mg, low(p))[:HD]
                pg = tn(v, mg)
                sg = low(p * (pg - jnp.sum(p * pg, axis=0, keepdims=True)))
                backs = (nn(kk, sg), nt(q, sg))
                for i in range(2):
                    rows = slice(i * HD, (i + 1) * HD)
                    back = turn(backs[i][:HD] * FACTOR, cos, -sin)
                    n = wide(norm[b, h, i * HEAD : (i + 1) * HEAD, cut])[:HD]
                    gain_sum[rows, :] += back * n
                    dn = back * gain_cols[:HD, i : i + 1]
                    mean = jnp.sum(dn * n, axis=0, keepdims=True) * (1.0 / HD)
                    dqkv[h, rows, cut] = stat[b, h, i : i + 1, cut] * (dn - n * mean)
            dlow[h] = low(dqkv[h])
            gather_sum(h, dlow[h], wa[b, :QKV_ROWS])
        qkv_part = nn(dlow[0], buf_a[0]) + nn(dlow[1], buf_a[1])
        part[zz, yy, :A_ROWS, :] = low(jnp.concatenate([qkv_part[:QKV], out_part[HEAD - HD :]], axis=0))
        ones = jnp.ones((8, 512), jnp.bfloat16)
        sums = nt(ones, dlow[0]) + nt(ones, dlow[1])
        s = slot(k)
        payf[pl.ds(6 + s // 4, 1), pl.ds(pl.multiple_of(lax.rem(s, 4) * 256, 128), QKV)] = sums[:1, :QKV]

        pl.when(lax.rem(k, 3) != 0)(lambda: service(D_STAGES + 1 + k - k // 3, GU_STAGES))

    send_stages(GU_STAGES, GU_STAGES - 1 + AHEAD)
    share_second.wait_send()
    begin_f(0)
    share_first = share_half(2, came)
    service(GU_STAGES - 1, R_STAGES)
    share_first.wait_recv()

    def first_rows(image, rows):
        v = wide(tokens[rows, :])
        inv = lax.rsqrt(jnp.mean(v * v, axis=-1, keepdims=True) + epsilon)
        n = v * inv
        fgd = acc[rows, :] + wide(came[rows, :])
        dn = fgd * (1.0 + mod_row(image, 1))
        count(image, 0, fgd)
        count(image, 1, fgd * n)
        acc[rows, :] = after[rows, :] + inv * (dn - n * jnp.mean(dn * n, axis=-1, keepdims=True))

    by_rows(first_rows)
    save_tokens = pltpu.make_async_copy(acc.at[pl.ds(0, 512)], tokens_out, ls.at[3])
    save_tokens.start()
    service(GU_STAGES, R_STAGES)
    save_tokens.wait()
    clear(acc)

    @pl.loop(0, 8)
    def _(k):
        b = lax.rem(k, 2)
        turn_f(k)
        for h in range(2):
            gather_sum(h, jnp.concatenate([hid[b, 0, h], hid[b, 1, h]], axis=0), wd[b])

    share_first.wait_send()
    share_feed = share_half(3, came_feed)
    service(GU_STAGES + 1, R_STAGES)
    share_feed.wait_recv()

    def result_rows(image, rows):
        feed = acc[rows, :] + wide(came_feed[rows, :])
        v = wide(tokens[rows, :]) + mod_row(image, 2) * att[rows, :]
        result[rows, :] = low(v + mod_row(image, 5) * feed)
        count(image, 5, wide(out_grad[rows, :]) * feed)

    by_rows(result_rows)
    save_result = pltpu.make_async_copy(result, result_out, ls.at[4])
    save_result.start()
    lanes = gain_sum[:, :128] + gain_sum[:, 128:]
    lanes = jnp.concatenate([lanes, jnp.zeros((256 - 2 * HD, 128), jnp.float32)], axis=0)
    payf[14:15, :256] = jnp.sum(jnp.transpose(lanes), axis=0, keepdims=True)
    for image in range(2):
        real = jnp.where(t * 2 + image < counts[0], 1.0, 0.0)
        for k in (2, 5):
            row = slice(image * 8 + k, image * 8 + k + 1)
            payf[row, :] = payf[row, :] * real
    pay[...] = low(payf[...])
    keep_pay = pltpu.make_async_copy(pay, pay_all.at[x, c, z, y], ls.at[5])
    keep_pay.start()
    pay_x = remote(pay, pay_all.at[x, c, z, y], ps.at[0], pr.at[0], x_side)
    pay_x.start()
    service(GU_STAGES + 2, R_STAGES)
    keep_pay.wait()
    pay_x.wait_recv()
    line = pay_all.at[:, c, z, y]
    pay_y = remote(line, line, ps.at[1], pr.at[1], y_side)
    pay_y.start()
    service(GU_STAGES + 3, R_STAGES)
    pay_y.wait_recv()
    square = pay_all.at[:, c, z]
    pays = [remote(square, square, ps.at[1 + k], pr.at[1 + k], at(x, c, lax.rem(z + k, 4), y)) for k in (1, 2, 3)]
    for cp in pays:
        cp.start()

    @pl.loop(GU_STAGES + 4, GU_STAGES + 6)
    def _(i):
        service(i, R_STAGES)

    for cp in pays:
        cp.wait()
    layer = pay_all.at[:, c]
    swap = remote(layer, layer, ps.at[5], pr.at[5], core)
    swap.start()

    service(GU_STAGES + 6, R_STAGES)
    share_feed.wait_send()
    swap.wait()
    load_pay = pltpu.make_async_copy(pay_all.reshape(32 * PAY, D), sent, ls.at[5])
    load_pay.start()
    service(GU_STAGES + 7, R_STAGES)
    load_pay.wait()

    def picked(count, which):
        row = lax.broadcasted_iota(jnp.int32, (count, 32 * PAY), 0)
        col = lax.broadcasted_iota(jnp.int32, (count, 32 * PAY), 1)
        return nn(jnp.where(which(row, col), 1.0, 0.0).astype(jnp.bfloat16), sent[...])

    act = jnp.zeros((64, 144), jnp.float32)
    for k in range(6):
        mg = picked(64, lambda row, col: col == row * 8 + k)
        sums_out[k : k + 1, :] = jnp.sum(mg, axis=0, keepdims=True)
        act = act + nt(low(mg), ada_w[k])
    payf[:8, :] = picked(8, lambda row, col: jnp.logical_or(
        jnp.logical_and(row == 0, lax.rem(col, PAY) == 14),
        jnp.logical_and(row == 1 + lax.rem(col // (8 * PAY), 2), lax.rem(col, PAY) == 6 + t // 4)))
    sums_out[6:8, :] = payf[0:2, :]
    bias_out[...] = payf[:8, pl.ds(pl.multiple_of(lax.rem(t, 4) * 256, 128), 256)]
    for group in range(4):
        cond_all[group * 16 : (group + 1) * 16, :] = cond[group]
    v = cond_all[:, :144]
    sig = 1.0 / (1.0 + jnp.exp(-v))
    cond_all[:, :144] = act * sig * (1.0 + v * (1.0 - sig))
    cond_out[...] = cond_all[rows_at(d * 16, 16), :144]
    rest = cond_all[:, :144]
    classes = lax.broadcasted_iota(jnp.int32, (64, class_out.shape[1]), 1)
    chosen = jnp.where(classes == cond_all[:, 144:145].astype(jnp.int32), 1.0, 0.0).astype(jnp.bfloat16)
    total = jnp.zeros(class_out.shape, jnp.float32)
    for _ in range(3):
        piece = low(rest)
        rest = rest - wide(piece)
        total = total + tn(piece, chosen)
    class_out[...] = total

    @pl.loop(GU_STAGES + 8, R_STAGES + 5)
    def _(i):
        service(i, R_STAGES)

    @pl.loop(0, R_STAGES)
    def _(g):
        for side in (0, 1):
            xcopy(g, side).wait_send()
        for k in range(3):
            ycopy(g, k).wait_send()
        lone = lone_z(g, y)
        pl.when(z < 3)(lambda: zcopy(g, 0, 0).wait_send())
        pl.when(z > 0)(lambda: zcopy(g, 1, 0).wait_send())
        pl.when(z < lone)(lambda: zcopy(g, 0, 1).wait_send())
        pl.when(z > lone)(lambda: zcopy(g, 1, 1).wait_send())
        pl.when(z == lone)(lambda: finished(g).wait_send())
        pl.when(z != 3 - lone)(lambda: own_copy(g).wait())
        core_copy(g, True).wait()

    pay_x.wait_send()
    pay_y.wait_send()
    share_ag.wait_send()
    save_result.wait()


def backward(saved, counts, tokens, out_grad, ada_w, mod, gains, table, cond, classes):
    dma = pltpu.SemaphoreType.DMA
    regular = pltpu.SemaphoreType.REGULAR
    vm = pltpu.VMEM
    bf, f32 = jnp.bfloat16, jnp.float32
    anywhere = pl.BlockSpec(memory_space=pl.ANY)
    inside = pl.BlockSpec(memory_space=pltpu.VMEM)
    R = tokens.shape[0]
    outs = [((R, D), bf), ((R, D), f32), ((2, ROWS_ALL, D), bf), ((2, 2, 4, 2, PAY, D), bf)]
    small = [((8, D), f32), ((8, 256), f32), ((16, 144), f32), ((144, classes), f32)]
    return pl.pallas_call(
        backward_kernel,
        out_shape=tuple(jax.ShapeDtypeStruct(s, e) for s, e in outs + small),
        in_specs=[anywhere] * len(saved) + [pl.BlockSpec(memory_space=pltpu.SMEM)] + [anywhere] * 3 + [inside] * 4,
        out_specs=(anywhere,) * len(outs) + (inside,) * len(small),
        scratch_shapes=[
            vm((R, D), bf), vm((R, D), bf), vm((6, 144, D), bf), vm((64, 256), f32), vm((4, 2, ROWS_ALL, D), bf), vm((X_RING, 2, R_STAGE, D), bf), vm((Y_RING, 3, R_STAGE, D), bf),
            vm((Z_RING, 4, R_STAGE, D), bf), vm((ROWS_ALL, D), bf),
            vm((2, R, D), bf), vm((2, R, D), bf), vm((2 * R, D), f32), vm((R, D), f32), vm((R, D), f32),
            vm((R, D), bf), vm((R, D), bf), vm((R, D), bf), vm((R, D), bf),
            vm((2, C_ROWS, D), bf), vm((2, B_ROWS, D), bf), vm((2, A_ROWS, D), bf),
            vm((2, 2, 2, HALF_FF, R), bf), vm((2, 2, 2, SHARD_FF, R), bf), vm((2, 2, 3 * HEAD, R), bf),
            vm((2, 2, 2 * HEAD, R), bf), vm((2, 2, 8, R), f32), vm((2, 2, HEAD, R), bf),
            vm((2, QKV_ROWS, R), f32), vm((2, QKV_ROWS, R), bf), vm((2 * HD, PATCH), f32), vm((16, D), f32),
            vm((16, D), bf),
            dma((R_STAGES, 2)), dma((R_STAGES, 2)), dma((R_STAGES, 3)), dma((R_STAGES, 3)),
            dma((R_STAGES, 4)), dma((R_STAGES, 4)), dma((R_STAGES, 3)), dma((R_STAGES, 2)),
            dma((4,)), dma((4,)), dma((6,)), dma((6,)), dma((10,)), dma((9, 2)),
            regular, regular, regular((2,)),
        ],
        compiler_params=pltpu.CompilerParams(
            collective_id=1, has_side_effects=True, vmem_limit_bytes=62 * 2**20),
        name="backward",
    )(*saved, counts, tokens, out_grad, ada_w, mod, gains, table, cond)


def normalize(vectors, axis=-1, count=None):
    count = count or vectors.shape[axis]
    inverse = lax.rsqrt(jnp.sum(vectors * vectors, axis=axis, keepdims=True) / count + epsilon)
    return (vectors * inverse, inverse)


def normalize_back(grad, normed, inverse, axis=-1, count=None):
    count = count or grad.shape[axis]
    return inverse * (grad - normed * (jnp.sum(grad * normed, axis=axis, keepdims=True) / count))


def silu_slope(values):
    sigma = jax.nn.sigmoid(values)
    return sigma * (1.0 + values * (1.0 - sigma))


def pair_tables(count):
    pairs = HD // 4
    theta = np.exp(-math.log(100.0) * np.arange(pairs, dtype=np.float32) / pairs)
    spot = np.arange(count) % PATCH
    a, b = theta[:, None] * (spot // GRID)[None], theta[:, None] * (spot % GRID)[None]
    cos = np.concatenate([np.cos(a), np.cos(a), np.cos(b), np.cos(b)])
    sin = np.concatenate([-np.sin(a), np.sin(a), -np.sin(b), np.sin(b)])
    return np.concatenate([cos, sin]).astype(np.float32)


def unpack_grads(both):
    qkv = both[:, :QKV].reshape(2, 3, HD, D).swapaxes(0, 1).reshape(3, 2 * HD, D)
    o = both[:, QKV:A_ROWS].reshape(2 * HD, D)
    gu = both[:, B_FIRST:C_FIRST].reshape(2, 2, 2, HALF_FF, D)
    gu = gu.transpose(4, 2, 0, 1, 3).reshape(D, 2, 2 * SHARD_FF)
    dn = both[:, C_FIRST:].reshape(2 * SHARD_FF, D)
    return [wide(v) for v in (qkv.transpose(2, 0, 1), o, gu, dn)]


def fast(
    tokens, labels, timesteps, image_counts, class_table, ada_weight, ada_bias,
    qkv_weight, qkv_bias, qk_scale, out_weight, gate_up_weight, down_weight, out_grad,
):
    dot = lambda s, a, b: jnp.einsum(s, a, b, preferred_element_type=jnp.float32)
    t = lax.axis_index("tensor")
    c = lax.axis_index("dp") % 2
    images = labels.shape[0]
    columns_here = class_table.shape[1]
    column = t * columns_here + jnp.arange(columns_here)
    half_width = D // 2
    frequency = jnp.exp(-math.log(10000.0) * (column % half_width).astype(jnp.float32) / half_width)
    angles = timesteps.astype(jnp.float32)[:, None] * frequency[None, :]
    time_embed = jnp.where(column[None, :] < half_width, jnp.cos(angles), jnp.sin(angles))
    classes = jnp.arange(class_table.shape[0])
    condition = dot("in,nc->ic", low(labels[:, None] == classes[None, :]), class_table) + time_embed
    gu = lax.dynamic_slice_in_dim(gate_up_weight, c * SHARD_FF, SHARD_FF, 2)
    gu = gu.reshape(D, 2, 2, HALF_FF).transpose(2, 1, 3, 0).reshape(B_ROWS, D)
    table = pair_tables(tokens.shape[0])
    (weights, cond_all, mod, first_in, second_in, feed_grad, attention, qkv_t, norm_t, stat_t, mixed, gu_t, hidden,
     down_part) = forward(
        image_counts, qkv_weight.transpose(1, 2, 0), out_weight, gu, down_weight, condition, labels[:, None],
        ada_weight.transpose(1, 0, 2), ada_bias, qkv_bias, tokens, out_grad, qk_scale, table)
    saved = (weights, first_in, second_in, feed_grad, attention, qkv_t, norm_t, stat_t, mixed, gu_t, hidden,
             down_part.reshape(4, 2, C_ROWS, D))
    result, tokens_grad, summed, pay_all, sums, biases, cond_grad, table_grad = backward(
        saved, image_counts, tokens, out_grad, ada_weight.transpose(1, 0, 2), mod, qk_scale, table, cond_all,
        class_table.shape[0])
    qkv_weight_grad, out_weight_grad, gate_up_grad, down_grad = unpack_grads(summed)
    mod_grad = pay_all.reshape(-1, 8, D)[:, :6]
    cond_act = low(jax.nn.silu(cond_all.reshape(4 * images, -1)[:, :columns_here]))
    ada_weight_grad = dot("ic,ikd->ckd", cond_act, mod_grad)
    ada_bias_grad = sums[:6]
    qk_scale_grad = sums[6, : 2 * HD].reshape(2, HD)
    qkv_bias_grad = biases[1:3, :QKV].reshape(2, 3, HD).swapaxes(0, 1).reshape(3, 2 * HD)
    table_grad = table_grad.T
    return (
        result, tokens_grad, cond_grad, table_grad, ada_weight_grad, ada_bias_grad,
        qkv_weight_grad, qkv_bias_grad, qk_scale_grad, out_weight_grad, gate_up_grad, down_grad,
    )


def rope_tables(count):
    pairs = HD // 4
    theta = jnp.exp(-math.log(100.0) * jnp.arange(pairs, dtype=jnp.float32) / pairs)
    place = jnp.arange(count) % PATCH
    row_angle = (place // GRID).astype(jnp.float32)[:, None] * theta
    col_angle = (place % GRID).astype(jnp.float32)[:, None] * theta
    return ((jnp.cos(row_angle), jnp.sin(row_angle)), (jnp.cos(col_angle), jnp.sin(col_angle)))


def rotate_part(segment, cosine, sine, direction):
    half_len = segment.shape[-1] // 2
    first, second = (segment[..., :half_len], segment[..., half_len:])
    cosine = cosine[:, None, :]
    sine = direction * sine[:, None, :]
    return jnp.concatenate(
        [first * cosine - second * sine, second * cosine + first * sine], axis=-1
    )


def rotate(vectors, tables, direction):
    half_len = vectors.shape[-1] // 2
    return jnp.concatenate(
        [
            rotate_part(vectors[..., :half_len], tables[0][0], tables[0][1], direction),
            rotate_part(vectors[..., half_len:], tables[1][0], tables[1][1], direction),
        ],
        axis=-1,
    )


def general(
    tokens,
    labels,
    timesteps,
    image_counts,
    class_table,
    ada_weight,
    ada_bias,
    qkv_weight,
    qkv_bias,
    qk_scale,
    out_weight,
    gate_up_weight,
    down_weight,
    out_grad,
):
    width = tokens.shape[1]
    local_rows = tokens.shape[0]
    members = lax.axis_size("tensor")
    place = lax.axis_index("tensor")
    images = labels.shape[0]
    all_rows = local_rows * members
    columns_here = class_table.shape[1]
    heads_here = columns_here // HD
    column = place * columns_here + jnp.arange(columns_here)
    half_width = width // 2
    frequency = jnp.exp(-math.log(10000.0) * (column % half_width).astype(jnp.float32) / half_width)
    angles = timesteps.astype(jnp.float32)[:, None] * frequency[None, :]
    time_embed = jnp.where(column[None, :] < half_width, jnp.cos(angles), jnp.sin(angles))
    chosen = (labels[:, None] == jnp.arange(class_table.shape[0])[None, :]).astype(jnp.bfloat16)
    condition = jnp.dot(chosen, class_table, preferred_element_type=jnp.float32) + time_embed
    cond_act = jax.nn.silu(condition).astype(jnp.bfloat16)
    mod_part = jnp.einsum("ic,ckd->ikd", cond_act, ada_weight, preferred_element_type=jnp.float32)
    modulation = lax.psum(mod_part, "tensor") + ada_bias.astype(jnp.float32)
    row_index = place * local_rows + jnp.arange(local_rows)
    row_image = row_index // PATCH
    selector = (row_image[:, None] == jnp.arange(images)[None, :]).astype(jnp.float32)
    mod_rows = jnp.dot(selector, modulation.reshape(images, 6 * width), precision=HIGH).reshape(
        local_rows, 6, width
    )
    kept = (row_image < image_counts[0]).astype(jnp.float32)[:, None]
    shift_one, scale_one, gate_one, shift_two, scale_two, gate_two = [
        mod_rows[:, index] for index in range(6)
    ]
    tokens_f = tokens.astype(jnp.float32)
    first_norm, first_inverse = normalize(tokens_f)
    first_in = (first_norm * (1.0 + scale_one) + shift_one).astype(jnp.bfloat16)
    first_all = lax.all_gather(first_in, "tensor", axis=0, tiled=True)
    qkv = jnp.einsum(
        "nd,dkc->nkc", first_all, qkv_weight, preferred_element_type=jnp.float32
    ) + qkv_bias.astype(jnp.float32)
    head_view = qkv.reshape(all_rows, 3, heads_here, HD)
    tables = rope_tables(all_rows)
    qk_gains = qk_scale.astype(jnp.float32)
    query_normed, query_inverse = normalize(head_view[:, 0])
    key_normed, key_inverse = normalize(head_view[:, 1])
    block_shape = (all_rows // PATCH, PATCH, heads_here, HD)
    queries = (
        rotate(query_normed * qk_gains[0], tables, 1.0).astype(jnp.bfloat16).reshape(block_shape)
    )
    keys_rot = (
        rotate(key_normed * qk_gains[1], tables, 1.0).astype(jnp.bfloat16).reshape(block_shape)
    )
    values = head_view[:, 2].astype(jnp.bfloat16).reshape(block_shape)
    factor = HD ** (-0.5)
    scores = (
        jnp.einsum("iqhe,ikhe->ihqk", queries, keys_rot, preferred_element_type=jnp.float32)
        * factor
    )
    row_max = jnp.max(scores, axis=-1, keepdims=True)
    exponent = jnp.exp(scores - row_max)
    totals = jnp.sum(exponent, axis=-1, keepdims=True)
    logsum = row_max + jnp.log(totals)
    probability = (exponent / totals).astype(jnp.bfloat16)
    mixed_heads = (
        jnp.einsum("ihqk,ikhe->iqhe", probability, values, preferred_element_type=jnp.float32)
        .reshape(all_rows, columns_here)
        .astype(jnp.bfloat16)
    )
    attention = lax.psum_scatter(
        jnp.dot(mixed_heads, out_weight, preferred_element_type=jnp.float32).astype(jnp.bfloat16),
        "tensor",
        scatter_dimension=0,
        tiled=True,
    ).astype(jnp.float32)
    after_attn = tokens_f + kept * gate_one * attention
    second_norm, second_inverse = normalize(after_attn)
    second_in = (second_norm * (1.0 + scale_two) + shift_two).astype(jnp.bfloat16)
    second_all = lax.all_gather(second_in, "tensor", axis=0, tiled=True)
    gate_up = jnp.einsum(
        "nd,dkf->nkf", second_all, gate_up_weight, preferred_element_type=jnp.float32
    )
    gate_value, up_value = (gate_up[:, 0], gate_up[:, 1])
    activated = jax.nn.silu(gate_value)
    hidden = (activated * up_value).astype(jnp.bfloat16)
    feed = lax.psum_scatter(
        jnp.dot(hidden, down_weight, preferred_element_type=jnp.float32).astype(jnp.bfloat16),
        "tensor",
        scatter_dimension=0,
        tiled=True,
    ).astype(jnp.float32)
    result = (after_attn + kept * gate_two * feed).astype(jnp.bfloat16)
    grad_out = out_grad.astype(jnp.float32)
    feed_grad = (grad_out * kept * gate_two).astype(jnp.bfloat16)
    gate_two_grad = grad_out * kept * feed
    feed_grad_all = lax.all_gather(feed_grad, "tensor", axis=0, tiled=True)
    hidden_grad = jnp.einsum(
        "nd,fd->nf", feed_grad_all, down_weight, preferred_element_type=jnp.float32
    )
    down_grad = jnp.einsum("nf,nd->fd", hidden, feed_grad_all, preferred_element_type=jnp.float32)
    gate_grad = hidden_grad * up_value * silu_slope(gate_value)
    up_grad = hidden_grad * activated
    gu_grad = jnp.stack([gate_grad, up_grad], axis=1).astype(jnp.bfloat16)
    gate_up_grad = jnp.einsum(
        "nd,nkf->dkf", second_all, gu_grad, preferred_element_type=jnp.float32
    )
    second_grad = lax.psum_scatter(
        jnp.einsum(
            "nkf,dkf->nd", gu_grad, gate_up_weight, preferred_element_type=jnp.float32
        ).astype(jnp.bfloat16),
        "tensor",
        scatter_dimension=0,
        tiled=True,
    ).astype(jnp.float32)
    after_grad = grad_out + normalize_back(
        second_grad * (1.0 + scale_two), second_norm, second_inverse
    )
    attention_grad = (after_grad * kept * gate_one).astype(jnp.bfloat16)
    gate_one_grad = after_grad * kept * attention
    attention_grad_all = lax.all_gather(attention_grad, "tensor", axis=0, tiled=True)
    mixed_grad = jnp.einsum(
        "nd,cd->nc", attention_grad_all, out_weight, preferred_element_type=jnp.float32
    ).astype(jnp.bfloat16)
    out_weight_grad = jnp.einsum(
        "nc,nd->cd", mixed_heads, attention_grad_all, preferred_element_type=jnp.float32
    )
    scores_again = (
        jnp.einsum("iqhe,ikhe->ihqk", queries, keys_rot, preferred_element_type=jnp.float32)
        * factor
    )
    prob_again = jnp.exp(scores_again - logsum)
    mixed_blocks = mixed_grad.reshape(block_shape)
    values_grad = jnp.einsum(
        "ihqk,iqhe->ikhe",
        prob_again.astype(jnp.bfloat16),
        mixed_blocks,
        preferred_element_type=jnp.float32,
    )
    prob_grad = jnp.einsum(
        "iqhe,ikhe->ihqk", mixed_blocks, values, preferred_element_type=jnp.float32
    )
    score_grad = (
        prob_again * (prob_grad - jnp.sum(prob_again * prob_grad, axis=-1, keepdims=True))
    ).astype(jnp.bfloat16)
    queries_grad = (
        jnp.einsum("ihqk,ikhe->iqhe", score_grad, keys_rot, preferred_element_type=jnp.float32)
        * factor
    )
    keys_grad = (
        jnp.einsum("ihqk,iqhe->ikhe", score_grad, queries, preferred_element_type=jnp.float32)
        * factor
    )
    query_back = rotate(queries_grad.reshape(all_rows, heads_here, HD), tables, -1.0)
    key_back = rotate(keys_grad.reshape(all_rows, heads_here, HD), tables, -1.0)
    scale_part = jnp.stack(
        [
            jnp.sum(query_back * query_normed, axis=(0, 1)),
            jnp.sum(key_back * key_normed, axis=(0, 1)),
        ]
    )
    query_raw = normalize_back(query_back * qk_gains[0], query_normed, query_inverse)
    key_raw = normalize_back(key_back * qk_gains[1], key_normed, key_inverse)
    qkv_grad = (
        jnp.stack([query_raw, key_raw, values_grad.reshape(all_rows, heads_here, HD)], axis=1)
        .reshape(all_rows, 3, columns_here)
        .astype(jnp.bfloat16)
    )
    qkv_weight_grad = jnp.einsum(
        "nd,nkc->dkc", first_all, qkv_grad, preferred_element_type=jnp.float32
    )
    qkv_bias_grad = jnp.sum(qkv_grad.astype(jnp.float32), axis=0)
    first_grad = lax.psum_scatter(
        jnp.einsum("nkc,dkc->nd", qkv_grad, qkv_weight, preferred_element_type=jnp.float32).astype(
            jnp.bfloat16
        ),
        "tensor",
        scatter_dimension=0,
        tiled=True,
    ).astype(jnp.float32)
    tokens_grad = after_grad + normalize_back(
        first_grad * (1.0 + scale_one), first_norm, first_inverse
    )
    row_mod_grad = jnp.stack(
        [
            first_grad,
            first_grad * first_norm,
            gate_one_grad,
            second_grad,
            second_grad * second_norm,
            gate_two_grad,
        ],
        axis=1,
    ).reshape(local_rows, 6 * width)
    mod_grad_part = jnp.dot(selector.T, row_mod_grad, precision=HIGH).reshape(images, 6, width)
    mod_grad, scale_grad = (
        lax.psum(mod_grad_part.astype(jnp.bfloat16), "tensor").astype(jnp.float32),
        lax.psum(scale_part.astype(jnp.bfloat16), "tensor").astype(jnp.float32),
    )
    mod_grad_low = mod_grad.astype(jnp.bfloat16)
    ada_weight_grad = jnp.einsum(
        "ic,ikd->ckd", cond_act, mod_grad_low, preferred_element_type=jnp.float32
    )
    ada_bias_grad = jnp.sum(mod_grad_low.astype(jnp.float32), axis=0)
    act_grad = jnp.einsum(
        "ikd,ckd->ic", mod_grad_low, ada_weight, preferred_element_type=jnp.float32
    )
    cond_grad = act_grad * silu_slope(condition)
    table_grad = jnp.dot(chosen.astype(jnp.float32).T, cond_grad, precision=HIGH)
    summed = (
        lax.psum(table_grad.astype(jnp.bfloat16), "dp").astype(jnp.float32),
        lax.psum(ada_weight_grad.astype(jnp.bfloat16), "dp").astype(jnp.float32),
        lax.psum(ada_bias_grad.astype(jnp.bfloat16), "dp").astype(jnp.float32),
        lax.psum(qkv_weight_grad.astype(jnp.bfloat16), "dp").astype(jnp.float32),
        lax.psum(qkv_bias_grad.astype(jnp.bfloat16), "dp").astype(jnp.float32),
        lax.psum(scale_grad.astype(jnp.bfloat16), "dp").astype(jnp.float32),
        lax.psum(out_weight_grad.astype(jnp.bfloat16), "dp").astype(jnp.float32),
        lax.psum(gate_up_grad.astype(jnp.bfloat16), "dp").astype(jnp.float32),
        lax.psum(down_grad.astype(jnp.bfloat16), "dp").astype(jnp.float32),
    )
    return (result, tokens_grad, cond_grad) + tuple(summed)


def solution(mesh):
    placed = (
        P(("dp", "tensor"), None),
        P("dp"),
        P("dp"),
        P("dp"),
        P(None, "tensor"),
        P("tensor", None, None),
        P(),
        P(None, None, "tensor"),
        P(None, "tensor"),
        P(),
        P("tensor", None),
        P(None, None, "tensor"),
        P("tensor", None),
        P(("dp", "tensor"), None),
    )
    plain = mesh.shape["dp"] != 4 or mesh.shape["tensor"] != 8
    return jax.shard_map(
        general if plain else fast,
        mesh=mesh,
        in_specs=placed,
        out_specs=(
            P(("dp", "tensor"), None),
            P(("dp", "tensor"), None),
            P("dp", "tensor"),
            P(None, "tensor"),
            P("tensor", None, None),
            P(),
            P(None, None, "tensor"),
            P(None, "tensor"),
            P(),
            P("tensor", None),
            P(None, None, "tensor"),
            P("tensor", None),
        ),
        check_vma=False,
    )
```

```python
import math

import jax
import jax.numpy as jnp
import numpy as np
from jax import lax
from jax.experimental import pallas as pl
from jax.experimental.pallas import tpu as pltpu
from jax.sharding import PartitionSpec as P

HD = 72
GRID = 16
PATCH = 256
HIGH = lax.Precision.HIGHEST
MESH = pl.DeviceIdType.MESH
epsilon = 1e-06
D = 1152

QKV = 3 * HD
A_ROWS = 4 * HD
SHARD_FF = 192
HALF_FF = SHARD_FF // 2
B_ROWS = 2 * SHARD_FF
C_ROWS = SHARD_FF
ROWS_ALL = A_ROWS + B_ROWS + C_ROWS
B_FIRST = A_ROWS
C_FIRST = A_ROWS + B_ROWS
HEAD = 80
O_FIRST = A_ROWS - HEAD
QKV_ROWS = 224
CHUNK = 64
FACTOR = HD ** (-0.5)
PAY = 16

G_STAGE, G_LONE = 48, 16
G_STAGES = ROWS_ALL // G_STAGE
G_TURNED = (3, 9, 15)
A_STAGES = A_ROWS // G_STAGE
HALF_STAGES = (A_ROWS + SHARD_FF) // G_STAGE
AB_STAGES = C_FIRST // G_STAGE

R_STAGE = 48
R_STAGES = ROWS_ALL // R_STAGE
D_STAGES = C_ROWS // R_STAGE
GU_STAGES = (C_ROWS + B_ROWS) // R_STAGE
X_RING, Y_RING, Z_RING = 8, 6, 8
AHEAD = 2


def place():
    d = lax.axis_index("dp")
    t = lax.axis_index("tensor")
    return d // 2, d % 2, t // 2, t % 2


def at(x, c, z, y):
    return (x * 2 + c, z * 2 + y)


def greet(targets):
    barrier = pltpu.get_barrier_semaphore()
    for o in targets:
        pl.semaphore_signal(barrier, inc=1, device_id=o, device_id_type=MESH)
    pl.semaphore_wait(barrier, len(targets))


def rows_at(first, size):
    return pl.ds(pl.multiple_of(first, 16), size)


def nt(a, b):
    return lax.dot_general(a, b, (((1,), (1,)), ((), ())), preferred_element_type=jnp.float32)


def tn(a, b):
    return lax.dot_general(a, b, (((0,), (0,)), ((), ())), preferred_element_type=jnp.float32)


def nn(a, b):
    return lax.dot_general(a, b, (((1,), (0,)), ((), ())), preferred_element_type=jnp.float32)


def low(v):
    return v.astype(jnp.bfloat16)


def wide(v):
    return v.astype(jnp.float32)


def turn(v, cos, sin):
    other = jnp.concatenate([v[18:36], v[:18], v[54:72], v[36:54]], axis=0)
    return v * cos + other * sin


def fill(v):
    return jnp.concatenate([v, jnp.zeros((HEAD - HD, v.shape[1]), v.dtype)], axis=0)


def columns(rows):
    k, n = rows.shape
    rows = jnp.concatenate([rows, jnp.zeros((k, 128 - n), jnp.float32)], axis=1)
    rows = jnp.concatenate([rows, jnp.zeros((128 - k, 128), jnp.float32)], axis=0)
    return jnp.transpose(rows)


def remote(src, dst, ss, rs, to):
    return pltpu.make_async_remote_copy(
        src_ref=src, dst_ref=dst, send_sem=ss, recv_sem=rs, device_id=to, device_id_type=MESH)


def forward_kernel(
    counts, qkv_hbm, out_hbm, gu_w, down_w, condition, labels, ada_hbm, ada_b, bias_w, tokens_hbm, out_grad_hbm, gains, table,
    full, cond_out, mod_out, fi_out, si_out, fg_out, att_out, qkv_out, norm_out, stat_out, mixed_out, gu_out, hid_out,
    dd_out,
    qkv_w, out_w, ada_w, tokens, out_grad, own, mod_in, mod_send, cond_in, mod_all, mod, fi, si, fg, att, att_send, att_recv, wa, ow, mixed, qkv, norm, stat, wb, gu,
    hid, dd,
    send, recv, ms, mr, cs, cr, es, er, ls, qs, hs, ws, save, fs,
):
    x, c, z, y = place()
    t = z * 2 + y
    d = x * 2 + c
    peers = [lax.rem(t + k, 8) for k in range(1, 8)]
    groups = [lax.rem(d + k, 4) for k in range(1, 4)]
    fetch = [
        pltpu.make_async_copy(src, dst, fs.at[i])
        for i, (src, dst) in enumerate(
            [(qkv_hbm, qkv_w), (out_hbm, out_w), (ada_hbm, ada_w), (tokens_hbm, tokens), (out_grad_hbm, out_grad)])
    ]
    for cp in fetch:
        cp.start()
    load_gu = pltpu.make_async_copy(gu_w, own.at[pl.ds(B_FIRST, B_ROWS)], ls.at[4])
    load_gu.start()
    load_down = pltpu.make_async_copy(
        down_w.at[rows_at(c * C_ROWS, C_ROWS)], own.at[pl.ds(C_FIRST, C_ROWS)], ls.at[5])
    load_down.start()
    fetch[0].wait()
    fetch[1].wait()
    for head in range(2):
        @pl.when(c == head)
        def _():
            cut = slice(head * HD, (head + 1) * HD)
            own[:A_ROWS, :] = low(jnp.concatenate(
                [wide(qkv_w[0, cut]), wide(qkv_w[1, cut]), wide(qkv_w[2, cut]), wide(out_w[cut])], axis=0))

    greet([(d, p) for p in peers] + [(g, t) for g in groups])
    y_side, x_side, core = at(x, c, z, 1 - y), at(1 - x, c, z, y), at(x, 1 - c, z, y)
    up, down = at(x, c, z + 1, y), at(x, c, z - 1, y)

    def plane(g):
        return rows_at(g * G_STAGE + x * G_LONE, G_STAGE - G_LONE)

    def lone(g, side):
        return rows_at(g * G_STAGE + side * (G_STAGE - G_LONE), G_LONE)

    def copy(g, kind, src, slot, rows, path, to):
        return remote(src.at[rows], full.at[slot, rows], send.at[g, kind], recv.at[g, slot, path], to)

    def arrived(g, slot, rows, path):
        copy(g, 0, own, slot, rows, path, x_side).wait_recv()

    def turned(g):
        found = g == G_TURNED[0]
        for other in G_TURNED[1:]:
            found = jnp.logical_or(found, g == other)
        return found

    def straight(g):
        return jnp.logical_not(turned(g))

    def issue(g):
        copy(g, 2, own, t, plane(g), 0, y_side).start()
        pl.when(z < 3)(lambda: copy(g, 0, own, t, plane(g), 0, up).start())
        pl.when(z > 0)(lambda: copy(g, 1, own, t, plane(g), 0, down).start())

    def along_z(g, j):
        def below():
            slot = (z - j) * 2 + y
            arrived(g, slot, plane(g), 0)
            pl.when(z < 3)(lambda: copy(g, 1 + 2 * j, full.at[slot], slot, plane(g), 0, up).start())
            pl.when(straight(g))(lambda: copy(g, 8 + j, full.at[slot], slot, plane(g), 0, y_side).start())
            copy(g, 11 + j, full.at[slot], slot, lone(g, x), 1, x_side).start()

        def above():
            slot = (z + j) * 2 + y
            arrived(g, slot, plane(g), 0)
            pl.when(z > 0)(lambda: copy(g, 2 + 2 * j, full.at[slot], slot, plane(g), 0, down).start())
            pl.when(straight(g))(lambda: copy(g, 14 + j, full.at[slot], slot, plane(g), 0, y_side).start())
            copy(g, 17 + j, full.at[slot], slot, lone(g, x), 1, x_side).start()

        pl.when(z >= j)(below)
        pl.when(z + j <= 3)(above)

    def along_y(g, j, above):
        zz = z + j if above else z - j
        slot = zz * 2 + 1 - y
        arrived(g, slot, plane(g), 0)

        @pl.when(turned(g))
        def _():
            if j == 0 or not above:
                kind = 25 if j == 0 else 8 + j
                pl.when(z < 3)(lambda: copy(g, kind, full.at[slot], slot, plane(g), 0, up).start())
            if j == 0 or above:
                kind = 26 if j == 0 else 14 + j
                pl.when(z > 0)(lambda: copy(g, kind, full.at[slot], slot, plane(g), 0, down).start())

        copy(g, 21 + zz, full.at[slot], slot, lone(g, x), 1, x_side).start()

    def service(i):
        def on(g, act):
            pl.when(jnp.logical_and(g >= 0, g < G_STAGES))(lambda: act(g))

        on(i, issue)
        for j in (1, 2, 3):
            on(i - j, lambda g: along_z(g, j))
        on(i - 1, lambda g: along_y(g, 0, False))
        for j in (1, 2, 3):
            @pl.when(z >= j)
            def _():
                on(i - j - 1, lambda g: along_y(g, j, False))

            @pl.when(z + j <= 3)
            def _():
                on(i - j - 1, lambda g: along_y(g, j, True))

    def lone_in(first, last):
        @pl.loop(first, last)
        def _(g):
            for k in range(1, 8):
                arrived(g, lax.rem(t + k, 8), lone(g, 1 - x), 1)

    def mod_row(image, k):
        return mod[pl.ds(image * 8 + k, 1), :]

    def by_rows(act):
        for image in range(2):
            @pl.loop(0, PATCH // CHUNK)
            def _(i):
                act(image, rows_at(image * PATCH + i * CHUNK, CHUNK))

    service(0)

    cond_in[...] = jnp.zeros_like(cond_in)
    cond_in[:, :144] = condition[...]
    cond_in[:, 144:145] = columns(wide(labels[...]))[:16, :1]
    mod_in[...] = jnp.zeros_like(mod_in)
    for p in range(8):
        for k, row in enumerate((6, 7, 14)):
            mod_in[p, row : row + 1, :144] = wide(bias_w[k : k + 1, :])
    load_gu.wait()
    load_down.wait()
    kept = [pltpu.make_async_copy(own, full.at[t], ls.at[0])]
    kept[0].start()
    fetch[2].wait()
    service(1)
    v = condition[...]
    act = low(v * (1.0 / (1.0 + jnp.exp(-v))))
    for k in range(6):
        share = nn(act, ada_w[k])
        for image in range(16):
            mod_in[image // 2, image % 2 * 8 + k : image % 2 * 8 + k + 1, :] = share[image : image + 1]
    mod_send[...] = low(mod_in[...])
    small = []
    for k, p in enumerate(peers):
        small.append(remote(mod_send.at[p], mod_all.at[t], ms.at[k], mr.at[t], (d, p)))
    for k, g in enumerate(groups):
        small.append(remote(cond_in, cond_out.at[d], cs.at[k], cr.at[d], (g, t)))
    for cp in small:
        cp.start()
    kept += [
        pltpu.make_async_copy(mod_send.at[t], mod_all.at[t], ls.at[1]),
        pltpu.make_async_copy(cond_in, cond_out.at[d], ls.at[2]),
    ]
    kept[1].start()
    kept[2].start()
    service(2)
    fetch[3].wait()
    fetch[4].wait()
    service(3)
    for p in peers:
        remote(mod_send.at[p], mod_all.at[p], ms.at[0], mr.at[p], (d, p)).wait_recv()
    kept[1].wait()
    for image in range(2):
        total = jnp.concatenate([wide(ada_b[...]), jnp.zeros((2, D), jnp.float32)], axis=0)
        for s in range(8):
            total = total + wide(mod_all[s])[image * 8 : image * 8 + 8]
        real = jnp.where(t * 2 + image < counts[0], 1.0, 0.0)
        row = lax.broadcasted_iota(jnp.int32, (8, D), 0)
        gate = jnp.logical_or(row == 2, row == 5)
        mod[image * 8 : image * 8 + 8, :] = jnp.where(gate, total * real, total)
    service(4)

    def first_rows(image, rows):
        v = wide(tokens[rows, :])
        n = v * lax.rsqrt(jnp.mean(v * v, axis=-1, keepdims=True) + epsilon)
        fi[0, rows, :] = low(n * (1.0 + mod_row(image, 1)) + mod_row(image, 0))

    def feed_rows(image, rows):
        fg[0, rows, :] = low(wide(out_grad[rows, :]) * mod_row(image, 5))

    by_rows(first_rows)
    share_fi = remote(fi.at[0], fi.at[1], es.at[0], er.at[0], core)
    share_fi.start()
    service(5)
    by_rows(feed_rows)
    share_fg = remote(fg.at[0], fg.at[1], es.at[1], er.at[1], core)
    share_fg.start()

    @pl.loop(6, A_STAGES + 4)
    def _(i):
        service(i)

    kept[0].wait()
    lone_in(0, A_STAGES)
    share_fi.wait_recv()
    share_fg.wait_recv()
    saves = [
        pltpu.make_async_copy(fi, fi_out, save.at[0]),
        pltpu.make_async_copy(fg, fg_out, save.at[1]),
        pltpu.make_async_copy(mod, mod_out, save.at[2]),
    ]
    for cp in saves:
        cp.start()

    def load_a(s):
        return pltpu.make_async_copy(full.at[s, pl.ds(0, QKV_ROWS)], wa.at[lax.rem(s, 2)], ws.at[lax.rem(s, 2)])

    load_o = pltpu.make_async_copy(full.at[:, pl.ds(O_FIRST, HEAD)], ow, ls.at[3])
    load_o.start()
    load_a(0).start()
    gain_cols = columns(wide(gains[...]))

    def save_head(s):
        b = lax.rem(s, 2)
        return [
            pltpu.make_async_copy(qkv.at[b], qkv_out.at[s], qs.at[b, 0]),
            pltpu.make_async_copy(norm.at[b], norm_out.at[s], qs.at[b, 1]),
            pltpu.make_async_copy(stat.at[b], stat_out.at[s], qs.at[b, 2]),
        ]

    @pl.loop(0, 8)
    def _(s):
        b = lax.rem(s, 2)
        load_a(s).wait()
        pl.when(s < 7)(lambda: load_a(s + 1).start())

        @pl.when(s > 1)
        def _():
            for cp in save_head(s - 2):
                cp.wait()

        bias_rows = wide(mod_all[s, :, :256])
        bias_rows = jnp.concatenate([bias_rows[6:8, :144], bias_rows[14:15, :144]], axis=0)
        bias = columns(jnp.where(c == 0, bias_rows[:, :HD], bias_rows[:, HD:]))
        cos, sin = table[:HD, :], table[HD:, :]
        for h in range(2):
            raw = nt(wa[b], fi[h])
            for i in range(2):
                v = raw[i * HD : (i + 1) * HD] + bias[:HD, i : i + 1]
                inv = lax.rsqrt(jnp.sum(v * v, axis=0, keepdims=True) * (1.0 / HD) + epsilon)
                n = v * inv
                norm[b, h, i * HEAD : (i + 1) * HEAD, :] = low(fill(n))
                stat[b, h, i : i + 1, :] = inv
                qkv[b, h, i * HEAD : (i + 1) * HEAD, :] = low(fill(turn(n * gain_cols[:HD, i : i + 1], cos, sin)))
            v = low(fill(raw[2 * HD : 3 * HD] + bias[:HD, 2:3]))
            qkv[b, h, 2 * HEAD :, :] = v
            for image in range(2):
                cut = slice(image * PATCH, (image + 1) * PATCH)
                e = jnp.exp(tn(qkv[b, h, HEAD : 2 * HEAD, cut], qkv[b, h, :HEAD, cut]) * FACTOR)
                row_sum = jnp.sum(e, axis=0, keepdims=True)
                stat[b, h, 2:3, cut] = jnp.log(row_sum)
                p = low(e * (1.0 / row_sum))
                m = nn(v[:, cut], p)
                m = jnp.concatenate([m[HD:], m[:HD]], axis=0)
                mixed[h, pl.ds(pl.multiple_of(s * HEAD, 16), HEAD), cut] = low(m)
        for cp in save_head(s):
            cp.start()

        pl.when(jnp.logical_or(s == 0, lax.rem(s, 2) == 1))(lambda: service(A_STAGES + 4 + (s + 1) // 2))

    for s in (6, 7):
        for cp in save_head(s):
            cp.wait()
    load_o.wait()
    saves.append(pltpu.make_async_copy(mixed, mixed_out, save.at[3]))
    saves[-1].start()

    for image in range(2):
        cut = slice(image * PATCH, (image + 1) * PATCH)
        att_send[cut, :] = low(tn(mixed[1, :, cut], ow[...].reshape(8 * HEAD, D)))
    share_att = remote(att_send, att_recv, es.at[2], er.at[2], core)
    share_att.start()
    for image in range(2):
        cut = slice(image * PATCH, (image + 1) * PATCH)
        att[cut, :] = tn(mixed[0, :, cut], ow[...].reshape(8 * HEAD, D))
    service(A_STAGES + 9)
    share_att.wait_recv()

    def second_rows(image, rows):
        a = att[rows, :] + wide(att_recv[rows, :])
        att[rows, :] = a
        v = wide(tokens[rows, :]) + mod_row(image, 2) * a
        n = v * lax.rsqrt(jnp.mean(v * v, axis=-1, keepdims=True) + epsilon)
        si[0, rows, :] = low(n * (1.0 + mod_row(image, 4)) + mod_row(image, 3))

    by_rows(second_rows)
    share_si = remote(si.at[0], si.at[1], es.at[3], er.at[3], core)
    share_si.start()
    service(A_STAGES + 10)

    share_si.wait_recv()
    saves += [
        pltpu.make_async_copy(att, att_out, save.at[4]),
        pltpu.make_async_copy(si, si_out, save.at[5]),
    ]
    saves[-2].start()
    saves[-1].start()

    def load_b(half, p):
        b = lax.rem(p, 2)
        return pltpu.make_async_copy(
            full.at[pl.ds(p * 2, 2), pl.ds(B_FIRST + half * SHARD_FF, SHARD_FF)], wb.at[b], ws.at[2 + b])

    def save_pair(half, p):
        b = lax.rem(p, 2)
        both = pl.ds(p * 2, 2)
        return [
            pltpu.make_async_copy(gu.at[b], gu_out.at[both, half], hs.at[b, 0]),
            pltpu.make_async_copy(hid.at[b], hid_out.at[both, half], hs.at[b, 1]),
            pltpu.make_async_copy(dd.at[b], dd_out.at[both, half], hs.at[b, 2]),
        ]

    for half in range(2):
        lone_in(A_STAGES + half * (HALF_STAGES - A_STAGES), HALF_STAGES + half * (HALF_STAGES - A_STAGES))
        load_b(half, 0).start()

        @pl.loop(0, 4)
        def _(p):
            b = lax.rem(p, 2)
            load_b(half, p).wait()
            pl.when(p < 3)(lambda: load_b(half, p + 1).start())

            @pl.when(p > 1)
            def _():
                for cp in save_pair(half, p - 2):
                    cp.wait()

            for h in range(2):
                both = nt(wb[b].reshape(2 * SHARD_FF, D), si[h])
                for i in range(2):
                    g = both[i * SHARD_FF : i * SHARD_FF + HALF_FF]
                    u = both[i * SHARD_FF + HALF_FF : (i + 1) * SHARD_FF]
                    hid[b, i, h] = low(g * (1.0 / (1.0 + jnp.exp(-g))) * u)
                    gu[b, i, h] = low(both[i * SHARD_FF : (i + 1) * SHARD_FF])
            grad = sum(
                nn(jnp.concatenate([hid[b, 0, h], hid[b, 1, h]], axis=0), fg[h]) for h in range(2))
            dd[b] = low(grad).reshape(2, HALF_FF, D)
            for cp in save_pair(half, p):
                cp.start()

            if half == 0:
                pl.when(lax.rem(p, 2) == 1)(lambda: service(A_STAGES + 11 + p // 2))
            else:
                pl.when(p < 3)(lambda: service(A_STAGES + 13 + p))

        for p in (2, 3):
            for cp in save_pair(half, p):
                cp.wait()

    lone_in(AB_STAGES, G_STAGES)

    @pl.loop(0, G_STAGES)
    def _(g):
        def sent(kind, rows):
            copy(g, kind, own, t, rows, 0, x_side).wait_send()

        sent(2, plane(g))
        pl.when(z < 3)(lambda: sent(0, plane(g)))
        pl.when(z > 0)(lambda: sent(1, plane(g)))
        for k in range(4):
            sent(21 + k, lone(g, x))
        pl.when(jnp.logical_and(turned(g), z < 3))(lambda: sent(25, plane(g)))
        pl.when(jnp.logical_and(turned(g), z > 0))(lambda: sent(26, plane(g)))
        for j in (1, 2, 3):
            @pl.when(z >= j)
            def _():
                pl.when(z < 3)(lambda: sent(1 + 2 * j, plane(g)))
                pl.when(jnp.logical_or(straight(g), z < 3))(lambda: sent(8 + j, plane(g)))
                sent(11 + j, lone(g, x))

            @pl.when(z + j <= 3)
            def _():
                pl.when(z > 0)(lambda: sent(2 + 2 * j, plane(g)))
                pl.when(jnp.logical_or(straight(g), z > 0))(lambda: sent(14 + j, plane(g)))
                sent(17 + j, lone(g, x))

    for cp in small + [share_fi, share_fg, share_att, share_si]:
        cp.wait_send()
    for g in groups:
        remote(cond_in, cond_out.at[g], cs.at[0], cr.at[g], (g, t)).wait_recv()
    kept[2].wait()
    for cp in saves:
        cp.wait()


def forward(counts, qkv_w, out_w, gu_w, down_w, condition, labels, ada_w, ada_b, bias_w, tokens, out_grad, gains, table):
    dma = pltpu.SemaphoreType.DMA
    vm = pltpu.VMEM
    bf, f32 = jnp.bfloat16, jnp.float32
    anywhere = pl.BlockSpec(memory_space=pl.ANY)
    inside = pl.BlockSpec(memory_space=pltpu.VMEM)
    scalar = pl.BlockSpec(memory_space=pltpu.SMEM)
    R = tokens.shape[0]
    outs = [
        ((8, ROWS_ALL, D), bf), ((4, 16, 256), f32), ((16, D), f32),
        ((2, R, D), bf), ((2, R, D), bf), ((2, R, D), bf), ((R, D), f32),
        ((8, 2, 3 * HEAD, R), bf), ((8, 2, 2 * HEAD, R), bf), ((8, 2, 8, R), f32), ((2, 8 * HEAD, R), bf),
        ((8, 2, 2, SHARD_FF, R), bf), ((8, 2, 2, HALF_FF, R), bf), ((8, 2, HALF_FF, D), bf),
    ]
    return pl.pallas_call(
        forward_kernel,
        out_shape=tuple(jax.ShapeDtypeStruct(s, e) for s, e in outs),
        in_specs=[scalar] + [anywhere] * 4 + [inside] * 2 + [anywhere] + [inside] * 2 + [anywhere] * 2 + [inside] * 2,
        out_specs=(anywhere,) * len(outs),
        scratch_shapes=[
            vm((3, 144, D), bf), vm((144, D), bf), vm((6, 144, D), bf), vm((R, D), bf), vm((R, D), bf),
            vm((ROWS_ALL, D), bf), vm((8, 16, D), f32), vm((8, 16, D), bf), vm((16, 256), f32), vm((8, 16, D), bf),
            vm((16, D), f32),
            vm((2, R, D), bf), vm((2, R, D), bf), vm((2, R, D), bf), vm((R, D), f32), vm((R, D), bf), vm((R, D), bf),
            vm((2, QKV_ROWS, D), bf), vm((8, HEAD, D), bf), vm((2, 8 * HEAD, R), bf),
            vm((2, 2, 3 * HEAD, R), bf), vm((2, 2, 2 * HEAD, R), bf), vm((2, 2, 8, R), f32),
            vm((2, 2, SHARD_FF, D), bf), vm((2, 2, 2, SHARD_FF, R), bf), vm((2, 2, 2, HALF_FF, R), bf),
            vm((2, 2, HALF_FF, D), bf),
            dma((G_STAGES, 27)), dma((G_STAGES, 8, 2)), dma((7,)), dma((8,)), dma((3,)), dma((4,)),
            dma((4,)), dma((4,)), dma((6,)), dma((2, 3)), dma((2, 3)), dma((6,)), dma((6,)), dma((5,)),
        ],
        compiler_params=pltpu.CompilerParams(
            collective_id=0, has_side_effects=True, vmem_limit_bytes=60 * 2**20),
        name="forward",
    )(counts, qkv_w, out_w, gu_w, down_w, condition, labels, ada_w, ada_b, bias_w, tokens, out_grad, gains, table)


def backward_kernel(
    full, fi_in, si_in, fg_in, att_in, qkv_in, norm_in, stat_in, mixed_in, gu_in, hid_in, dd_in,
    counts, tokens_hbm, out_grad_hbm, ada_hbm, mod, gains, table, cond,
    result_out, tokens_out, grads, pay_all, sums_out, scale_out, bias_out, cond_out, class_out,
    tokens, out_grad, ada_w, cond_all, part, xin, yin, zin, fin, buf_a, buf_b, acc, after, att, sent, came, came_feed, result,
    wd, wb, wa, hid, gu, qkv, norm, stat, mixed, dqkv, dlow, gain_sum, payf, pay,
    xs, xr, ys, yr, zs, zr, fs, fr, es, er, ps, pr, ls, lw, x_free, y_free, z_free,
):
    x, c, z, y = place()
    t = z * 2 + y
    d = x * 2 + c
    y_side, x_side, core = at(x, c, z, 1 - y), at(1 - x, c, z, y), at(x, 1 - c, z, y)
    up, down = at(x, c, z + 1, y), at(x, c, z - 1, y)
    mates = [at(x, c, lax.rem(z + k, 4), y) for k in (1, 2, 3)] + [x_side, y_side]

    loads = [
        pltpu.make_async_copy(fg_in, buf_a, ls.at[0]),
        pltpu.make_async_copy(si_in, buf_b, ls.at[1]),
        pltpu.make_async_copy(att_in, att, ls.at[2]),
        pltpu.make_async_copy(tokens_hbm, tokens, ls.at[7]),
        pltpu.make_async_copy(out_grad_hbm, out_grad, ls.at[8]),
        pltpu.make_async_copy(ada_hbm, ada_w, ls.at[9]),
    ]
    load_dd = pltpu.make_async_copy(
        dd_in, part.at[:, :, pl.ds(C_FIRST, C_ROWS)], ls.at[6])
    load_dd.start()
    greet(mates + [core])
    for cp in loads:
        cp.start()

    def first_of(g):
        return ROWS_ALL - (g + 1) * R_STAGE

    def rows_of(g):
        return rows_at(first_of(g), R_STAGE)

    def side_y(side):
        return 1 - y if side == 0 else y

    def lone_z(g, yy):
        return jnp.where(yy == lax.rem(x + g, 2), 1, 2)

    def xcopy(g, side):
        yy = side_y(side)
        return remote(
            part.at[3 - lone_z(g, yy), yy, rows_of(g)], xin.at[lax.rem(g, X_RING), side],
            xs.at[g, side], xr.at[g, side], x_side)

    def ycopy(g, k):
        yy = 1 - y
        zz = (0, 3, lone_z(g, yy))[k]
        return remote(part.at[zz, yy, rows_of(g)], yin.at[lax.rem(g, Y_RING), k], ys.at[g, k], yr.at[g, k], y_side)

    def zcopy(g, way, k):
        zz = (3 - 3 * way) if k == 0 else lone_z(g, y)
        return remote(
            part.at[zz, y, rows_of(g)], zin.at[lax.rem(g, Z_RING), way * 2 + k],
            zs.at[g, way * 2 + k], zr.at[g, way * 2 + k], up if way == 0 else down)

    def plane_sum(g):
        return remote(part.at[z, y, rows_of(g)], fin.at[rows_of(g)], fs.at[g, 0], fr.at[g, 0], x_side)

    def finished(g):
        return remote(part.at[z, y, rows_of(g)], grads.at[c, rows_of(g)], fs.at[g, 0], fr.at[g, 0], x_side)

    def core_copy(g, here):
        src = part.at[z, y, rows_of(g)] if here else grads.at[c, rows_of(g)]
        return remote(src, grads.at[c, rows_of(g)], fs.at[g, 1], fr.at[g, 1], core)

    def own_copy(g):
        return pltpu.make_async_copy(part.at[z, y, rows_of(g)], grads.at[c, rows_of(g)], fs.at[g, 2])

    def add(zz, yy, g, piece):
        first = first_of(g)

        @pl.loop(0, R_STAGE // 16)
        def _(i):
            a = rows_at(first + i * 16, 16)
            part[zz, yy, a, :] = low(wide(part[zz, yy, a, :]) + wide(piece(rows_at(i * 16, 16))))

    def send(g, side):
        if side == 0:
            pl.when(g >= X_RING)(lambda: pl.semaphore_wait(x_free, 1))
            pl.when(g >= Y_RING)(lambda: pl.semaphore_wait(y_free, 1))
        xcopy(g, side).start()
        if side == 0:
            ycopy(g, 0).start()
            ycopy(g, 1).start()

    def x_stage(g):
        b = lax.rem(g, X_RING)
        for side in (0, 1):
            yy = side_y(side)
            xcopy(g, side).wait_recv()
            add(lone_z(g, yy), yy, g, lambda r: xin[b, side, r, :])
            if side == 0:
                ycopy(g, 2).start()
        pl.when(g + X_RING < R_STAGES)(
            lambda: pl.semaphore_signal(x_free, inc=1, device_id=x_side, device_id_type=MESH))

    def y_stage(g):
        b = lax.rem(g, Y_RING)
        for k in range(3):
            ycopy(g, k).wait_recv()
            add((0, 3, lone_z(g, y))[k], y, g, lambda r: yin[b, k, r, :])
        pl.when(g + Y_RING < R_STAGES)(
            lambda: pl.semaphore_signal(y_free, inc=1, device_id=y_side, device_id_type=MESH))

    def take(g, way, k):
        zcopy(g, way, k).wait_recv()
        zz = (3 - 3 * way) if k == 0 else lone_z(g, y)
        add(zz, y, g, lambda r: zin[lax.rem(g, Z_RING), way * 2 + k, r, :])

    def z_stage(g, way):
        further = z < 3 if way == 0 else z > 0
        first = z == 0 if way == 0 else z == 3

        @pl.when(further)
        def _():
            pl.when(g >= Z_RING)(lambda: pl.semaphore_wait(z_free.at[way], 1))
            pl.when(jnp.logical_not(first))(lambda: take(g, way, 0))
            zcopy(g, way, 0).start()

        lone = lone_z(g, y)

        @pl.when(z < lone if way == 0 else z > lone)
        def _():
            pl.when(jnp.logical_not(first))(lambda: take(g, way, 1))
            zcopy(g, way, 1).start()

    def own_stage(g):
        pl.when(z == 3)(lambda: take(g, 0, 0))
        pl.when(z == 0)(lambda: take(g, 1, 0))

        @pl.when(z == lone_z(g, y))
        def _():
            take(g, 0, 1)
            take(g, 1, 1)
            finished(g).start()

        pl.when(jnp.logical_or(z == 0, z == 3))(lambda: plane_sum(g).start())

        @pl.when(g + Z_RING < R_STAGES)
        def _():
            pl.when(z > 0)(
                lambda: pl.semaphore_signal(z_free.at[0], inc=1, device_id=down, device_id_type=MESH))
            pl.when(z < 3)(
                lambda: pl.semaphore_signal(z_free.at[1], inc=1, device_id=up, device_id_type=MESH))

    def f_stage(g):
        ends = jnp.logical_or(z == 0, z == 3)
        here = z == lone_z(g, y)

        @pl.when(ends)
        def _():
            plane_sum(g).wait()
            add(z, y, g, lambda r: fin[rows_at(first_of(g) + r.start, 16), :])

        @pl.when(jnp.logical_or(ends, here))
        def _():
            own_copy(g).start()
            core_copy(g, True).start()

        @pl.when(z == 3 - lone_z(g, y))
        def _():
            finished(g).wait_recv()
            core_copy(g, False).start()

    def service(i, ready):
        def on(g, act):
            pl.when(jnp.logical_and(g >= 0, g < R_STAGES))(lambda: act(g))

        on(i, x_stage)
        on(i - 1, y_stage)
        on(i - 1 - z, lambda g: z_stage(g, 0))
        on(i - 4 + z, lambda g: z_stage(g, 1))
        on(i - 4, own_stage)
        on(i - 5, f_stage)

        @pl.when(i + AHEAD < ready)
        def _():
            send(i + AHEAD, 0)
            send(i + AHEAD, 1)

    def send_stages(first, last):
        @pl.loop(first, last)
        def _(g):
            send(g, 0)
            send(g, 1)

    def shard(k):
        return lax.rem(k, 4), jnp.where(k < 4, 1 - y, y)

    def slot(k):
        zz, yy = shard(k)
        return zz * 2 + yy

    def stream(pairs):
        def fetch(k):
            b = lax.rem(k, 2)
            return [pltpu.make_async_copy(src(slot(k)), buf.at[b], lw.at[n, b]) for src, buf, n in pairs]

        def begin(k):
            for cp in fetch(k):
                cp.start()

        def turn_to(k):
            for cp in fetch(k):
                cp.wait()
            pl.when(k < 7)(lambda: begin(k + 1))

        return begin, turn_to

    def mod_row(image, k):
        return mod[pl.ds(image * 8 + k, 1), :]

    def by_rows(act):
        for image in range(2):
            @pl.loop(0, PATCH // CHUNK)
            def _(i):
                act(image, rows_at(image * PATCH + i * CHUNK, CHUNK))

    def count(image, k, v):
        payf[pl.ds(image * 8 + k, 1), :] += jnp.sum(v, axis=0, keepdims=True)

    def clear(ref):
        @pl.loop(0, ref.shape[0] // 16)
        def _(i):
            ref[rows_at(i * 16, 16), :] = jnp.zeros((16, D), jnp.float32)

    def gather_sum(h, left, right):
        for image in range(2):
            cut = slice(image * PATCH, (image + 1) * PATCH)
            rows = slice(h * 512 + image * PATCH, h * 512 + (image + 1) * PATCH)
            acc[rows, :] += tn(left[:, cut], right)

    def share_half(number, landing):
        @pl.loop(0, 512 // CHUNK)
        def _(i):
            sent[rows_at(i * CHUNK, CHUNK), :] = low(acc[rows_at(512 + i * CHUNK, CHUNK), :])

        cp = remote(sent, landing, es.at[number], er.at[number], core)
        cp.start()
        return cp

    load_dd.wait()
    send_stages(0, AHEAD)
    payf[...] = jnp.zeros_like(payf)
    gain_sum[...] = jnp.zeros_like(gain_sum)
    clear(acc)
    begin_g, turn_g = stream([
        (lambda s: full.at[s, pl.ds(C_FIRST, C_ROWS)], wd, 1),
        (lambda s: full.at[s, pl.ds(B_FIRST, B_ROWS)], wb, 2),
        (lambda s: gu_in.at[s], gu, 3),
    ])
    begin_a, turn_a = stream([
        (lambda s: full.at[s, pl.ds(0, A_ROWS)], wa, 4),
        (lambda s: qkv_in.at[s], qkv, 5),
        (lambda s: norm_in.at[s], norm, 6),
        (lambda s: stat_in.at[s], stat, 7),
        (lambda s: mixed_in.at[:, rows_at(s * HEAD, HEAD)], mixed, 8),
    ])
    begin_f, turn_f = stream([
        (lambda s: hid_in.at[s], hid, 0),
        (lambda s: full.at[s, pl.ds(C_FIRST, C_ROWS)], wd, 1),
    ])
    begin_g(0)
    loads[0].wait()
    loads[1].wait()

    @pl.loop(0, 8)
    def _(k):
        b = lax.rem(k, 2)
        zz, yy = shard(k)
        turn_g(k)
        grads_here = []
        for h in range(2):
            hg = nt(wd[b], buf_a[h])
            both = []
            for half in range(2):
                g, u = wide(gu[b, half, h, :HALF_FF]), wide(gu[b, half, h, HALF_FF:])
                sig = 1.0 / (1.0 + jnp.exp(-g))
                act = g * sig
                this = hg[half * HALF_FF : (half + 1) * HALF_FF]
                both += [low(this * u * (sig + act * (1.0 - sig))), low(this * act)]
            both = jnp.concatenate(both, axis=0)
            grads_here.append(both)
            gather_sum(h, both, wb[b])
        part[zz, yy, B_FIRST:C_FIRST, :] = low(nn(grads_here[0], buf_b[0]) + nn(grads_here[1], buf_b[1]))

        pl.when(lax.rem(k, 2) == 1)(lambda: service(k // 2, D_STAGES))

    load_fi = pltpu.make_async_copy(fi_in, buf_a, ls.at[0])
    load_fi.start()
    share_second = share_half(0, came)
    send_stages(D_STAGES, D_STAGES + AHEAD)
    begin_a(0)
    service(D_STAGES, GU_STAGES)
    for cp in loads[2:]:
        cp.wait()
    share_second.wait_recv()

    def after_rows(image, rows):
        a = att[rows, :]
        v = wide(tokens[rows, :]) + mod_row(image, 2) * a
        inv = lax.rsqrt(jnp.mean(v * v, axis=-1, keepdims=True) + epsilon)
        n = v * inv
        sg = acc[rows, :] + wide(came[rows, :])
        dn = sg * (1.0 + mod_row(image, 4))
        ag = wide(out_grad[rows, :]) + inv * (dn - n * jnp.mean(dn * n, axis=-1, keepdims=True))
        after[rows, :] = ag
        buf_b[0, rows, :] = low(ag * mod_row(image, 2))
        count(image, 2, ag * a)
        count(image, 3, sg)
        count(image, 4, sg * n)

    by_rows(after_rows)
    share_ag = remote(buf_b.at[0], buf_b.at[1], es.at[1], er.at[1], core)
    share_ag.start()
    service(D_STAGES + 1, GU_STAGES)
    clear(acc)
    load_fi.wait()
    share_ag.wait_recv()

    gain_cols = columns(wide(gains[...]))

    @pl.loop(0, 8)
    def _(k):
        b = lax.rem(k, 2)
        zz, yy = shard(k)
        turn_a(k)
        cos, sin = table[:HD, :PATCH], table[HD:, :PATCH]
        out_part = nn(mixed[b, 0], buf_b[0]) + nn(mixed[b, 1], buf_b[1])
        for h in range(2):
            mg_all = nt(wa[b, O_FIRST:], buf_b[h])
            mg_all = low(fill(mg_all[HEAD - HD :]))
            dqkv[h, 3 * HD :, :] = jnp.zeros((QKV_ROWS - 3 * HD, 512), jnp.float32)
            for image in range(2):
                cut = slice(image * PATCH, (image + 1) * PATCH)
                q, kk, v = [qkv[b, h, i * HEAD : (i + 1) * HEAD, cut] for i in range(3)]
                mg = mg_all[:, cut]
                p = jnp.exp(tn(kk, q) * FACTOR - stat[b, h, 2:3, cut])
                dqkv[h, 2 * HD : 3 * HD, cut] = nt(mg, low(p))[:HD]
                pg = tn(v, mg)
                sg = low(p * (pg - jnp.sum(p * pg, axis=0, keepdims=True)))
                backs = (nn(kk, sg), nt(q, sg))
                for i in range(2):
                    rows = slice(i * HD, (i + 1) * HD)
                    back = turn(backs[i][:HD] * FACTOR, cos, -sin)
                    n = wide(norm[b, h, i * HEAD : (i + 1) * HEAD, cut])[:HD]
                    gain_sum[rows, :] += back * n
                    dn = back * gain_cols[:HD, i : i + 1]
                    mean = jnp.sum(dn * n, axis=0, keepdims=True) * (1.0 / HD)
                    dqkv[h, rows, cut] = stat[b, h, i : i + 1, cut] * (dn - n * mean)
            dlow[h] = low(dqkv[h])
            gather_sum(h, dlow[h], wa[b, :QKV_ROWS])
        qkv_part = nn(dlow[0], buf_a[0]) + nn(dlow[1], buf_a[1])
        part[zz, yy, :A_ROWS, :] = low(jnp.concatenate([qkv_part[:QKV], out_part[HEAD - HD :]], axis=0))
        ones = jnp.ones((8, 512), jnp.bfloat16)
        sums = nt(ones, dlow[0]) + nt(ones, dlow[1])
        s = slot(k)
        payf[pl.ds(6 + s // 4, 1), pl.ds(pl.multiple_of(lax.rem(s, 4) * 256, 128), QKV)] = sums[:1, :QKV]

        pl.when(lax.rem(k, 3) != 0)(lambda: service(D_STAGES + 1 + k - k // 3, GU_STAGES))

    send_stages(GU_STAGES, GU_STAGES - 1 + AHEAD)
    share_second.wait_send()
    begin_f(0)
    share_first = share_half(2, came)
    service(GU_STAGES - 1, R_STAGES)
    share_first.wait_recv()

    def first_rows(image, rows):
        v = wide(tokens[rows, :])
        inv = lax.rsqrt(jnp.mean(v * v, axis=-1, keepdims=True) + epsilon)
        n = v * inv
        fgd = acc[rows, :] + wide(came[rows, :])
        dn = fgd * (1.0 + mod_row(image, 1))
        count(image, 0, fgd)
        count(image, 1, fgd * n)
        acc[rows, :] = after[rows, :] + inv * (dn - n * jnp.mean(dn * n, axis=-1, keepdims=True))

    by_rows(first_rows)
    save_tokens = pltpu.make_async_copy(acc.at[pl.ds(0, 512)], tokens_out, ls.at[3])
    save_tokens.start()
    service(GU_STAGES, R_STAGES)
    save_tokens.wait()
    clear(acc)

    @pl.loop(0, 8)
    def _(k):
        b = lax.rem(k, 2)
        turn_f(k)
        for h in range(2):
            gather_sum(h, jnp.concatenate([hid[b, 0, h], hid[b, 1, h]], axis=0), wd[b])

    share_first.wait_send()
    share_feed = share_half(3, came_feed)
    service(GU_STAGES + 1, R_STAGES)
    share_feed.wait_recv()

    def result_rows(image, rows):
        feed = acc[rows, :] + wide(came_feed[rows, :])
        v = wide(tokens[rows, :]) + mod_row(image, 2) * att[rows, :]
        result[rows, :] = low(v + mod_row(image, 5) * feed)
        count(image, 5, wide(out_grad[rows, :]) * feed)

    by_rows(result_rows)
    save_result = pltpu.make_async_copy(result, result_out, ls.at[4])
    save_result.start()
    lanes = gain_sum[:, :128] + gain_sum[:, 128:]
    lanes = jnp.concatenate([lanes, jnp.zeros((256 - 2 * HD, 128), jnp.float32)], axis=0)
    payf[14:15, :256] = jnp.sum(jnp.transpose(lanes), axis=0, keepdims=True)
    for image in range(2):
        real = jnp.where(t * 2 + image < counts[0], 1.0, 0.0)
        for k in (2, 5):
            row = slice(image * 8 + k, image * 8 + k + 1)
            payf[row, :] = payf[row, :] * real
    pay[...] = low(payf[...])
    keep_pay = pltpu.make_async_copy(pay, pay_all.at[x, c, z, y], ls.at[5])
    keep_pay.start()
    pay_x = remote(pay, pay_all.at[x, c, z, y], ps.at[0], pr.at[0], x_side)
    pay_x.start()
    service(GU_STAGES + 2, R_STAGES)
    keep_pay.wait()
    pay_x.wait_recv()
    line = pay_all.at[:, c, z, y]
    pay_y = remote(line, line, ps.at[1], pr.at[1], y_side)
    pay_y.start()
    service(GU_STAGES + 3, R_STAGES)
    pay_y.wait_recv()
    square = pay_all.at[:, c, z]
    pays = [remote(square, square, ps.at[1 + k], pr.at[1 + k], at(x, c, lax.rem(z + k, 4), y)) for k in (1, 2, 3)]
    for cp in pays:
        cp.start()

    @pl.loop(GU_STAGES + 4, GU_STAGES + 6)
    def _(i):
        service(i, R_STAGES)

    for cp in pays:
        cp.wait()
    layer = pay_all.at[:, c]
    swap = remote(layer, layer, ps.at[5], pr.at[5], core)
    swap.start()

    service(GU_STAGES + 6, R_STAGES)
    share_feed.wait_send()
    swap.wait()
    load_pay = pltpu.make_async_copy(pay_all.reshape(32 * PAY, D), sent, ls.at[5])
    load_pay.start()
    service(GU_STAGES + 7, R_STAGES)
    load_pay.wait()

    def picked(count, which):
        row = lax.broadcasted_iota(jnp.int32, (count, 32 * PAY), 0)
        col = lax.broadcasted_iota(jnp.int32, (count, 32 * PAY), 1)
        return nn(jnp.where(which(row, col), 1.0, 0.0).astype(jnp.bfloat16), sent[...])

    act = jnp.zeros((64, 144), jnp.float32)
    for k in range(6):
        mg = picked(64, lambda row, col: col == row * 8 + k)
        sums_out[k : k + 1, :] = jnp.sum(mg, axis=0, keepdims=True)
        act = act + nt(low(mg), ada_w[k])
    payf[:8, :] = picked(8, lambda row, col: jnp.logical_or(
        jnp.logical_and(row == 0, lax.rem(col, PAY) == 14),
        jnp.logical_and(row == 1 + lax.rem(col // (8 * PAY), 2), lax.rem(col, PAY) == 6 + t // 4)))
    found = payf[:8, :256]
    scale_out[0:1, :] = found[:1, :HD]
    scale_out[1:2, :] = found[:1, HD : 2 * HD]
    found = payf[:8, pl.ds(pl.multiple_of(lax.rem(t, 4) * 256, 128), 256)]
    for k in range(3):
        cut = slice(k * HD, (k + 1) * HD)
        bias_out[k : k + 1, :] = jnp.concatenate([found[1:2, cut], found[2:3, cut]], axis=1)
    for group in range(4):
        cond_all[group * 16 : (group + 1) * 16, :] = cond[group]
    v = cond_all[:, :144]
    sig = 1.0 / (1.0 + jnp.exp(-v))
    cond_all[:, :144] = act * sig * (1.0 + v * (1.0 - sig))
    cond_out[...] = cond_all[rows_at(d * 16, 16), :144]
    rest = cond_all[:, :144]
    classes = lax.broadcasted_iota(jnp.int32, (64, class_out.shape[1]), 1)
    chosen = jnp.where(classes == cond_all[:, 144:145].astype(jnp.int32), 1.0, 0.0).astype(jnp.bfloat16)
    total = jnp.zeros(class_out.shape, jnp.float32)
    for _ in range(3):
        piece = low(rest)
        rest = rest - wide(piece)
        total = total + tn(piece, chosen)
    class_out[...] = total

    @pl.loop(GU_STAGES + 8, R_STAGES + 5)
    def _(i):
        service(i, R_STAGES)

    @pl.loop(0, R_STAGES)
    def _(g):
        for side in (0, 1):
            xcopy(g, side).wait_send()
        for k in range(3):
            ycopy(g, k).wait_send()
        lone = lone_z(g, y)
        pl.when(z < 3)(lambda: zcopy(g, 0, 0).wait_send())
        pl.when(z > 0)(lambda: zcopy(g, 1, 0).wait_send())
        pl.when(z < lone)(lambda: zcopy(g, 0, 1).wait_send())
        pl.when(z > lone)(lambda: zcopy(g, 1, 1).wait_send())
        pl.when(z == lone)(lambda: finished(g).wait_send())
        pl.when(z != 3 - lone)(lambda: own_copy(g).wait())
        core_copy(g, True).wait()

    pay_x.wait_send()
    pay_y.wait_send()
    share_ag.wait_send()
    save_result.wait()


def backward(saved, counts, tokens, out_grad, ada_w, mod, gains, table, cond, classes):
    dma = pltpu.SemaphoreType.DMA
    regular = pltpu.SemaphoreType.REGULAR
    vm = pltpu.VMEM
    bf, f32 = jnp.bfloat16, jnp.float32
    anywhere = pl.BlockSpec(memory_space=pl.ANY)
    inside = pl.BlockSpec(memory_space=pltpu.VMEM)
    R = tokens.shape[0]
    outs = [((R, D), bf), ((R, D), f32), ((2, ROWS_ALL, D), bf), ((2, 2, 4, 2, PAY, D), bf)]
    small = [((6, D), f32), ((2, HD), f32), ((3, 2 * HD), f32), ((16, 144), f32), ((144, classes), f32)]
    return pl.pallas_call(
        backward_kernel,
        out_shape=tuple(jax.ShapeDtypeStruct(s, e) for s, e in outs + small),
        in_specs=[anywhere] * len(saved) + [pl.BlockSpec(memory_space=pltpu.SMEM)] + [anywhere] * 3 + [inside] * 4,
        out_specs=(anywhere,) * len(outs) + (inside,) * len(small),
        scratch_shapes=[
            vm((R, D), bf), vm((R, D), bf), vm((6, 144, D), bf), vm((64, 256), f32), vm((4, 2, ROWS_ALL, D), bf), vm((X_RING, 2, R_STAGE, D), bf), vm((Y_RING, 3, R_STAGE, D), bf),
            vm((Z_RING, 4, R_STAGE, D), bf), vm((ROWS_ALL, D), bf),
            vm((2, R, D), bf), vm((2, R, D), bf), vm((2 * R, D), f32), vm((R, D), f32), vm((R, D), f32),
            vm((R, D), bf), vm((R, D), bf), vm((R, D), bf), vm((R, D), bf),
            vm((2, C_ROWS, D), bf), vm((2, B_ROWS, D), bf), vm((2, A_ROWS, D), bf),
            vm((2, 2, 2, HALF_FF, R), bf), vm((2, 2, 2, SHARD_FF, R), bf), vm((2, 2, 3 * HEAD, R), bf),
            vm((2, 2, 2 * HEAD, R), bf), vm((2, 2, 8, R), f32), vm((2, 2, HEAD, R), bf),
            vm((2, QKV_ROWS, R), f32), vm((2, QKV_ROWS, R), bf), vm((2 * HD, PATCH), f32), vm((16, D), f32),
            vm((16, D), bf),
            dma((R_STAGES, 2)), dma((R_STAGES, 2)), dma((R_STAGES, 3)), dma((R_STAGES, 3)),
            dma((R_STAGES, 4)), dma((R_STAGES, 4)), dma((R_STAGES, 3)), dma((R_STAGES, 2)),
            dma((4,)), dma((4,)), dma((6,)), dma((6,)), dma((10,)), dma((9, 2)),
            regular, regular, regular((2,)),
        ],
        compiler_params=pltpu.CompilerParams(
            collective_id=1, has_side_effects=True, vmem_limit_bytes=62 * 2**20),
        name="backward",
    )(*saved, counts, tokens, out_grad, ada_w, mod, gains, table, cond)


def normalize(vectors, axis=-1, count=None):
    count = count or vectors.shape[axis]
    inverse = lax.rsqrt(jnp.sum(vectors * vectors, axis=axis, keepdims=True) / count + epsilon)
    return (vectors * inverse, inverse)


def normalize_back(grad, normed, inverse, axis=-1, count=None):
    count = count or grad.shape[axis]
    return inverse * (grad - normed * (jnp.sum(grad * normed, axis=axis, keepdims=True) / count))


def silu_slope(values):
    sigma = jax.nn.sigmoid(values)
    return sigma * (1.0 + values * (1.0 - sigma))


def pair_tables(count):
    pairs = HD // 4
    theta = np.exp(-math.log(100.0) * np.arange(pairs, dtype=np.float32) / pairs)
    spot = np.arange(count) % PATCH
    a, b = theta[:, None] * (spot // GRID)[None], theta[:, None] * (spot % GRID)[None]
    cos = np.concatenate([np.cos(a), np.cos(a), np.cos(b), np.cos(b)])
    sin = np.concatenate([-np.sin(a), np.sin(a), -np.sin(b), np.sin(b)])
    return np.concatenate([cos, sin]).astype(np.float32)


def unpack_grads(both):
    qkv = both[:, :QKV].reshape(2, 3, HD, D).swapaxes(0, 1).reshape(3, 2 * HD, D)
    o = both[:, QKV:A_ROWS].reshape(2 * HD, D)
    gu = both[:, B_FIRST:C_FIRST].reshape(2, 2, 2, HALF_FF, D)
    gu = gu.transpose(4, 2, 0, 1, 3).reshape(D, 2, 2 * SHARD_FF)
    dn = both[:, C_FIRST:].reshape(2 * SHARD_FF, D)
    return [wide(v) for v in (qkv.transpose(2, 0, 1), o, gu, dn)]


def fast(
    tokens, labels, timesteps, image_counts, class_table, ada_weight, ada_bias,
    qkv_weight, qkv_bias, qk_scale, out_weight, gate_up_weight, down_weight, out_grad,
):
    dot = lambda s, a, b: jnp.einsum(s, a, b, preferred_element_type=jnp.float32)
    t = lax.axis_index("tensor")
    c = lax.axis_index("dp") % 2
    images = labels.shape[0]
    columns_here = class_table.shape[1]
    column = t * columns_here + jnp.arange(columns_here)
    half_width = D // 2
    frequency = jnp.exp(-math.log(10000.0) * (column % half_width).astype(jnp.float32) / half_width)
    angles = timesteps.astype(jnp.float32)[:, None] * frequency[None, :]
    time_embed = jnp.where(column[None, :] < half_width, jnp.cos(angles), jnp.sin(angles))
    classes = jnp.arange(class_table.shape[0])
    condition = dot("in,nc->ic", low(labels[:, None] == classes[None, :]), class_table) + time_embed
    gu = lax.dynamic_slice_in_dim(gate_up_weight, c * SHARD_FF, SHARD_FF, 2)
    gu = gu.reshape(D, 2, 2, HALF_FF).transpose(2, 1, 3, 0).reshape(B_ROWS, D)
    table = pair_tables(tokens.shape[0])
    (weights, cond_all, mod, first_in, second_in, feed_grad, attention, qkv_t, norm_t, stat_t, mixed, gu_t, hidden,
     down_part) = forward(
        image_counts, qkv_weight.transpose(1, 2, 0), out_weight, gu, down_weight, condition, labels[None, :],
        ada_weight.transpose(1, 0, 2), ada_bias, qkv_bias, tokens, out_grad, qk_scale, table)
    saved = (weights, first_in, second_in, feed_grad, attention, qkv_t, norm_t, stat_t, mixed, gu_t, hidden,
             down_part.reshape(4, 2, C_ROWS, D))
    (result, tokens_grad, summed, pay_all, ada_bias_grad, qk_scale_grad, qkv_bias_grad, cond_grad,
     table_grad) = backward(
        saved, image_counts, tokens, out_grad, ada_weight.transpose(1, 0, 2), mod, qk_scale, table, cond_all,
        class_table.shape[0])
    qkv_weight_grad, out_weight_grad, gate_up_grad, down_grad = unpack_grads(summed)
    mod_grad = pay_all.reshape(-1, 8, D)[:, :6]
    cond_act = low(jax.nn.silu(cond_all.reshape(4 * images, -1)[:, :columns_here]))
    ada_weight_grad = dot("ic,ikd->ckd", cond_act, mod_grad)
    table_grad = table_grad.T
    return (
        result, tokens_grad, cond_grad, table_grad, ada_weight_grad, ada_bias_grad,
        qkv_weight_grad, qkv_bias_grad, qk_scale_grad, out_weight_grad, gate_up_grad, down_grad,
    )


def rope_tables(count):
    pairs = HD // 4
    theta = jnp.exp(-math.log(100.0) * jnp.arange(pairs, dtype=jnp.float32) / pairs)
    place = jnp.arange(count) % PATCH
    row_angle = (place // GRID).astype(jnp.float32)[:, None] * theta
    col_angle = (place % GRID).astype(jnp.float32)[:, None] * theta
    return ((jnp.cos(row_angle), jnp.sin(row_angle)), (jnp.cos(col_angle), jnp.sin(col_angle)))


def rotate_part(segment, cosine, sine, direction):
    half_len = segment.shape[-1] // 2
    first, second = (segment[..., :half_len], segment[..., half_len:])
    cosine = cosine[:, None, :]
    sine = direction * sine[:, None, :]
    return jnp.concatenate(
        [first * cosine - second * sine, second * cosine + first * sine], axis=-1
    )


def rotate(vectors, tables, direction):
    half_len = vectors.shape[-1] // 2
    return jnp.concatenate(
        [
            rotate_part(vectors[..., :half_len], tables[0][0], tables[0][1], direction),
            rotate_part(vectors[..., half_len:], tables[1][0], tables[1][1], direction),
        ],
        axis=-1,
    )


def general(
    tokens,
    labels,
    timesteps,
    image_counts,
    class_table,
    ada_weight,
    ada_bias,
    qkv_weight,
    qkv_bias,
    qk_scale,
    out_weight,
    gate_up_weight,
    down_weight,
    out_grad,
):
    width = tokens.shape[1]
    local_rows = tokens.shape[0]
    members = lax.axis_size("tensor")
    place = lax.axis_index("tensor")
    images = labels.shape[0]
    all_rows = local_rows * members
    columns_here = class_table.shape[1]
    heads_here = columns_here // HD
    column = place * columns_here + jnp.arange(columns_here)
    half_width = width // 2
    frequency = jnp.exp(-math.log(10000.0) * (column % half_width).astype(jnp.float32) / half_width)
    angles = timesteps.astype(jnp.float32)[:, None] * frequency[None, :]
    time_embed = jnp.where(column[None, :] < half_width, jnp.cos(angles), jnp.sin(angles))
    chosen = (labels[:, None] == jnp.arange(class_table.shape[0])[None, :]).astype(jnp.bfloat16)
    condition = jnp.dot(chosen, class_table, preferred_element_type=jnp.float32) + time_embed
    cond_act = jax.nn.silu(condition).astype(jnp.bfloat16)
    mod_part = jnp.einsum("ic,ckd->ikd", cond_act, ada_weight, preferred_element_type=jnp.float32)
    modulation = lax.psum(mod_part, "tensor") + ada_bias.astype(jnp.float32)
    row_index = place * local_rows + jnp.arange(local_rows)
    row_image = row_index // PATCH
    selector = (row_image[:, None] == jnp.arange(images)[None, :]).astype(jnp.float32)
    mod_rows = jnp.dot(selector, modulation.reshape(images, 6 * width), precision=HIGH).reshape(
        local_rows, 6, width
    )
    kept = (row_image < image_counts[0]).astype(jnp.float32)[:, None]
    shift_one, scale_one, gate_one, shift_two, scale_two, gate_two = [
        mod_rows[:, index] for index in range(6)
    ]
    tokens_f = tokens.astype(jnp.float32)
    first_norm, first_inverse = normalize(tokens_f)
    first_in = (first_norm * (1.0 + scale_one) + shift_one).astype(jnp.bfloat16)
    first_all = lax.all_gather(first_in, "tensor", axis=0, tiled=True)
    qkv = jnp.einsum(
        "nd,dkc->nkc", first_all, qkv_weight, preferred_element_type=jnp.float32
    ) + qkv_bias.astype(jnp.float32)
    head_view = qkv.reshape(all_rows, 3, heads_here, HD)
    tables = rope_tables(all_rows)
    qk_gains = qk_scale.astype(jnp.float32)
    query_normed, query_inverse = normalize(head_view[:, 0])
    key_normed, key_inverse = normalize(head_view[:, 1])
    block_shape = (all_rows // PATCH, PATCH, heads_here, HD)
    queries = (
        rotate(query_normed * qk_gains[0], tables, 1.0).astype(jnp.bfloat16).reshape(block_shape)
    )
    keys_rot = (
        rotate(key_normed * qk_gains[1], tables, 1.0).astype(jnp.bfloat16).reshape(block_shape)
    )
    values = head_view[:, 2].astype(jnp.bfloat16).reshape(block_shape)
    factor = HD ** (-0.5)
    scores = (
        jnp.einsum("iqhe,ikhe->ihqk", queries, keys_rot, preferred_element_type=jnp.float32)
        * factor
    )
    row_max = jnp.max(scores, axis=-1, keepdims=True)
    exponent = jnp.exp(scores - row_max)
    totals = jnp.sum(exponent, axis=-1, keepdims=True)
    logsum = row_max + jnp.log(totals)
    probability = (exponent / totals).astype(jnp.bfloat16)
    mixed_heads = (
        jnp.einsum("ihqk,ikhe->iqhe", probability, values, preferred_element_type=jnp.float32)
        .reshape(all_rows, columns_here)
        .astype(jnp.bfloat16)
    )
    attention = lax.psum_scatter(
        jnp.dot(mixed_heads, out_weight, preferred_element_type=jnp.float32).astype(jnp.bfloat16),
        "tensor",
        scatter_dimension=0,
        tiled=True,
    ).astype(jnp.float32)
    after_attn = tokens_f + kept * gate_one * attention
    second_norm, second_inverse = normalize(after_attn)
    second_in = (second_norm * (1.0 + scale_two) + shift_two).astype(jnp.bfloat16)
    second_all = lax.all_gather(second_in, "tensor", axis=0, tiled=True)
    gate_up = jnp.einsum(
        "nd,dkf->nkf", second_all, gate_up_weight, preferred_element_type=jnp.float32
    )
    gate_value, up_value = (gate_up[:, 0], gate_up[:, 1])
    activated = jax.nn.silu(gate_value)
    hidden = (activated * up_value).astype(jnp.bfloat16)
    feed = lax.psum_scatter(
        jnp.dot(hidden, down_weight, preferred_element_type=jnp.float32).astype(jnp.bfloat16),
        "tensor",
        scatter_dimension=0,
        tiled=True,
    ).astype(jnp.float32)
    result = (after_attn + kept * gate_two * feed).astype(jnp.bfloat16)
    grad_out = out_grad.astype(jnp.float32)
    feed_grad = (grad_out * kept * gate_two).astype(jnp.bfloat16)
    gate_two_grad = grad_out * kept * feed
    feed_grad_all = lax.all_gather(feed_grad, "tensor", axis=0, tiled=True)
    hidden_grad = jnp.einsum(
        "nd,fd->nf", feed_grad_all, down_weight, preferred_element_type=jnp.float32
    )
    down_grad = jnp.einsum("nf,nd->fd", hidden, feed_grad_all, preferred_element_type=jnp.float32)
    gate_grad = hidden_grad * up_value * silu_slope(gate_value)
    up_grad = hidden_grad * activated
    gu_grad = jnp.stack([gate_grad, up_grad], axis=1).astype(jnp.bfloat16)
    gate_up_grad = jnp.einsum(
        "nd,nkf->dkf", second_all, gu_grad, preferred_element_type=jnp.float32
    )
    second_grad = lax.psum_scatter(
        jnp.einsum(
            "nkf,dkf->nd", gu_grad, gate_up_weight, preferred_element_type=jnp.float32
        ).astype(jnp.bfloat16),
        "tensor",
        scatter_dimension=0,
        tiled=True,
    ).astype(jnp.float32)
    after_grad = grad_out + normalize_back(
        second_grad * (1.0 + scale_two), second_norm, second_inverse
    )
    attention_grad = (after_grad * kept * gate_one).astype(jnp.bfloat16)
    gate_one_grad = after_grad * kept * attention
    attention_grad_all = lax.all_gather(attention_grad, "tensor", axis=0, tiled=True)
    mixed_grad = jnp.einsum(
        "nd,cd->nc", attention_grad_all, out_weight, preferred_element_type=jnp.float32
    ).astype(jnp.bfloat16)
    out_weight_grad = jnp.einsum(
        "nc,nd->cd", mixed_heads, attention_grad_all, preferred_element_type=jnp.float32
    )
    scores_again = (
        jnp.einsum("iqhe,ikhe->ihqk", queries, keys_rot, preferred_element_type=jnp.float32)
        * factor
    )
    prob_again = jnp.exp(scores_again - logsum)
    mixed_blocks = mixed_grad.reshape(block_shape)
    values_grad = jnp.einsum(
        "ihqk,iqhe->ikhe",
        prob_again.astype(jnp.bfloat16),
        mixed_blocks,
        preferred_element_type=jnp.float32,
    )
    prob_grad = jnp.einsum(
        "iqhe,ikhe->ihqk", mixed_blocks, values, preferred_element_type=jnp.float32
    )
    score_grad = (
        prob_again * (prob_grad - jnp.sum(prob_again * prob_grad, axis=-1, keepdims=True))
    ).astype(jnp.bfloat16)
    queries_grad = (
        jnp.einsum("ihqk,ikhe->iqhe", score_grad, keys_rot, preferred_element_type=jnp.float32)
        * factor
    )
    keys_grad = (
        jnp.einsum("ihqk,iqhe->ikhe", score_grad, queries, preferred_element_type=jnp.float32)
        * factor
    )
    query_back = rotate(queries_grad.reshape(all_rows, heads_here, HD), tables, -1.0)
    key_back = rotate(keys_grad.reshape(all_rows, heads_here, HD), tables, -1.0)
    scale_part = jnp.stack(
        [
            jnp.sum(query_back * query_normed, axis=(0, 1)),
            jnp.sum(key_back * key_normed, axis=(0, 1)),
        ]
    )
    query_raw = normalize_back(query_back * qk_gains[0], query_normed, query_inverse)
    key_raw = normalize_back(key_back * qk_gains[1], key_normed, key_inverse)
    qkv_grad = (
        jnp.stack([query_raw, key_raw, values_grad.reshape(all_rows, heads_here, HD)], axis=1)
        .reshape(all_rows, 3, columns_here)
        .astype(jnp.bfloat16)
    )
    qkv_weight_grad = jnp.einsum(
        "nd,nkc->dkc", first_all, qkv_grad, preferred_element_type=jnp.float32
    )
    qkv_bias_grad = jnp.sum(qkv_grad.astype(jnp.float32), axis=0)
    first_grad = lax.psum_scatter(
        jnp.einsum("nkc,dkc->nd", qkv_grad, qkv_weight, preferred_element_type=jnp.float32).astype(
            jnp.bfloat16
        ),
        "tensor",
        scatter_dimension=0,
        tiled=True,
    ).astype(jnp.float32)
    tokens_grad = after_grad + normalize_back(
        first_grad * (1.0 + scale_one), first_norm, first_inverse
    )
    row_mod_grad = jnp.stack(
        [
            first_grad,
            first_grad * first_norm,
            gate_one_grad,
            second_grad,
            second_grad * second_norm,
            gate_two_grad,
        ],
        axis=1,
    ).reshape(local_rows, 6 * width)
    mod_grad_part = jnp.dot(selector.T, row_mod_grad, precision=HIGH).reshape(images, 6, width)
    mod_grad, scale_grad = (
        lax.psum(mod_grad_part.astype(jnp.bfloat16), "tensor").astype(jnp.float32),
        lax.psum(scale_part.astype(jnp.bfloat16), "tensor").astype(jnp.float32),
    )
    mod_grad_low = mod_grad.astype(jnp.bfloat16)
    ada_weight_grad = jnp.einsum(
        "ic,ikd->ckd", cond_act, mod_grad_low, preferred_element_type=jnp.float32
    )
    ada_bias_grad = jnp.sum(mod_grad_low.astype(jnp.float32), axis=0)
    act_grad = jnp.einsum(
        "ikd,ckd->ic", mod_grad_low, ada_weight, preferred_element_type=jnp.float32
    )
    cond_grad = act_grad * silu_slope(condition)
    table_grad = jnp.dot(chosen.astype(jnp.float32).T, cond_grad, precision=HIGH)
    summed = (
        lax.psum(table_grad.astype(jnp.bfloat16), "dp").astype(jnp.float32),
        lax.psum(ada_weight_grad.astype(jnp.bfloat16), "dp").astype(jnp.float32),
        lax.psum(ada_bias_grad.astype(jnp.bfloat16), "dp").astype(jnp.float32),
        lax.psum(qkv_weight_grad.astype(jnp.bfloat16), "dp").astype(jnp.float32),
        lax.psum(qkv_bias_grad.astype(jnp.bfloat16), "dp").astype(jnp.float32),
        lax.psum(scale_grad.astype(jnp.bfloat16), "dp").astype(jnp.float32),
        lax.psum(out_weight_grad.astype(jnp.bfloat16), "dp").astype(jnp.float32),
        lax.psum(gate_up_grad.astype(jnp.bfloat16), "dp").astype(jnp.float32),
        lax.psum(down_grad.astype(jnp.bfloat16), "dp").astype(jnp.float32),
    )
    return (result, tokens_grad, cond_grad) + tuple(summed)


def solution(mesh):
    placed = (
        P(("dp", "tensor"), None),
        P("dp"),
        P("dp"),
        P("dp"),
        P(None, "tensor"),
        P("tensor", None, None),
        P(),
        P(None, None, "tensor"),
        P(None, "tensor"),
        P(),
        P("tensor", None),
        P(None, None, "tensor"),
        P("tensor", None),
        P(("dp", "tensor"), None),
    )
    plain = mesh.shape["dp"] != 4 or mesh.shape["tensor"] != 8
    return jax.shard_map(
        general if plain else fast,
        mesh=mesh,
        in_specs=placed,
        out_specs=(
            P(("dp", "tensor"), None),
            P(("dp", "tensor"), None),
            P("dp", "tensor"),
            P(None, "tensor"),
            P("tensor", None, None),
            P(),
            P(None, None, "tensor"),
            P(None, "tensor"),
            P(),
            P("tensor", None),
            P(None, None, "tensor"),
            P("tensor", None),
        ),
        check_vma=False,
    )
```

```python
import math

import jax
import jax.numpy as jnp
import numpy as np
from jax import lax
from jax.experimental import pallas as pl
from jax.experimental.pallas import tpu as pltpu
from jax.sharding import PartitionSpec as P

HD = 72
GRID = 16
PATCH = 256
HIGH = lax.Precision.HIGHEST
MESH = pl.DeviceIdType.MESH
epsilon = 1e-06
D = 1152

QKV = 3 * HD
A_ROWS = 4 * HD
SHARD_FF = 192
HALF_FF = SHARD_FF // 2
B_ROWS = 2 * SHARD_FF
C_ROWS = SHARD_FF
ROWS_ALL = A_ROWS + B_ROWS + C_ROWS
B_FIRST = A_ROWS
C_FIRST = A_ROWS + B_ROWS
HEAD = 80
O_FIRST = A_ROWS - HEAD
QKV_ROWS = 224
CHUNK = 64
FACTOR = HD ** (-0.5)
PAY = 16

G_STAGE, G_LONE = 48, 16
G_STAGES = ROWS_ALL // G_STAGE
G_TURNED = (3, 9, 15)
A_STAGES = A_ROWS // G_STAGE
HALF_STAGES = (A_ROWS + SHARD_FF) // G_STAGE
AB_STAGES = C_FIRST // G_STAGE

R_STAGE = 48
R_STAGES = ROWS_ALL // R_STAGE
D_STAGES = C_ROWS // R_STAGE
GU_STAGES = (C_ROWS + B_ROWS) // R_STAGE
X_RING, Y_RING, Z_RING = 8, 6, 8
AHEAD = 2


def place():
    d = lax.axis_index("dp")
    t = lax.axis_index("tensor")
    return d // 2, d % 2, t // 2, t % 2


def at(x, c, z, y):
    return (x * 2 + c, z * 2 + y)


def greet(targets):
    barrier = pltpu.get_barrier_semaphore()
    for o in targets:
        pl.semaphore_signal(barrier, inc=1, device_id=o, device_id_type=MESH)
    pl.semaphore_wait(barrier, len(targets))


def rows_at(first, size):
    return pl.ds(pl.multiple_of(first, 16), size)


def nt(a, b):
    return lax.dot_general(a, b, (((1,), (1,)), ((), ())), preferred_element_type=jnp.float32)


def tn(a, b):
    return lax.dot_general(a, b, (((0,), (0,)), ((), ())), preferred_element_type=jnp.float32)


def nn(a, b):
    return lax.dot_general(a, b, (((1,), (0,)), ((), ())), preferred_element_type=jnp.float32)


def low(v):
    return v.astype(jnp.bfloat16)


def wide(v):
    return v.astype(jnp.float32)


def turn(v, cos, sin):
    other = jnp.concatenate([v[18:36], v[:18], v[54:72], v[36:54]], axis=0)
    return v * cos + other * sin


def fill(v):
    return jnp.concatenate([v, jnp.zeros((HEAD - HD, v.shape[1]), v.dtype)], axis=0)


def columns(rows):
    k, n = rows.shape
    rows = jnp.concatenate([rows, jnp.zeros((k, 128 - n), jnp.float32)], axis=1)
    rows = jnp.concatenate([rows, jnp.zeros((128 - k, 128), jnp.float32)], axis=0)
    return jnp.transpose(rows)


def remote(src, dst, ss, rs, to):
    return pltpu.make_async_remote_copy(
        src_ref=src, dst_ref=dst, send_sem=ss, recv_sem=rs, device_id=to, device_id_type=MESH)


def forward_kernel(
    counts, qkv_hbm, out_hbm, gu_w, down_w, condition, labels, ada_hbm, ada_b, bias_w, tokens_hbm, out_grad_hbm, gains, table,
    full, cond_out, mod_out, fi_out, si_out, fg_out, att_out, qkv_out, norm_out, stat_out, mixed_out, gu_out, hid_out,
    dd_out,
    qkv_w, out_w, ada_w, tokens, out_grad, own, mod_in, mod_send, cond_in, mod_all, mod, fi, si, fg, att, att_send, att_recv, wa, ow, mixed, qkv, norm, stat, wb, gu,
    hid, dd,
    send, recv, ms, mr, cs, cr, es, er, ls, qs, hs, ws, save, fs,
):
    x, c, z, y = place()
    t = z * 2 + y
    d = x * 2 + c
    peers = [lax.rem(t + k, 8) for k in range(1, 8)]
    groups = [lax.rem(d + k, 4) for k in range(1, 4)]
    fetch = [
        pltpu.make_async_copy(src, dst, fs.at[i])
        for i, (src, dst) in enumerate(
            [(qkv_hbm, qkv_w), (out_hbm, out_w), (ada_hbm, ada_w), (tokens_hbm, tokens), (out_grad_hbm, out_grad)])
    ]
    for cp in fetch:
        cp.start()
    load_gu = pltpu.make_async_copy(gu_w, own.at[pl.ds(B_FIRST, B_ROWS)], ls.at[4])
    load_gu.start()
    load_down = pltpu.make_async_copy(
        down_w.at[rows_at(c * C_ROWS, C_ROWS)], own.at[pl.ds(C_FIRST, C_ROWS)], ls.at[5])
    load_down.start()
    fetch[0].wait()
    fetch[1].wait()
    for head in range(2):
        @pl.when(c == head)
        def _():
            cut = slice(head * HD, (head + 1) * HD)
            own[:A_ROWS, :] = low(jnp.concatenate(
                [wide(qkv_w[0, cut]), wide(qkv_w[1, cut]), wide(qkv_w[2, cut]), wide(out_w[cut])], axis=0))

    greet([(d, p) for p in peers] + [(g, t) for g in groups])
    y_side, x_side, core = at(x, c, z, 1 - y), at(1 - x, c, z, y), at(x, 1 - c, z, y)
    up, down = at(x, c, z + 1, y), at(x, c, z - 1, y)

    def plane(g):
        return rows_at(g * G_STAGE + x * G_LONE, G_STAGE - G_LONE)

    def lone(g, side):
        return rows_at(g * G_STAGE + side * (G_STAGE - G_LONE), G_LONE)

    def copy(g, kind, src, slot, rows, path, to):
        return remote(src.at[rows], full.at[slot, rows], send.at[g, kind], recv.at[g, slot, path], to)

    def arrived(g, slot, rows, path):
        copy(g, 0, own, slot, rows, path, x_side).wait_recv()

    def turned(g):
        found = g == G_TURNED[0]
        for other in G_TURNED[1:]:
            found = jnp.logical_or(found, g == other)
        return found

    def straight(g):
        return jnp.logical_not(turned(g))

    def issue(g):
        copy(g, 2, own, t, plane(g), 0, y_side).start()
        pl.when(z < 3)(lambda: copy(g, 0, own, t, plane(g), 0, up).start())
        pl.when(z > 0)(lambda: copy(g, 1, own, t, plane(g), 0, down).start())

    def along_z(g, j):
        def below():
            slot = (z - j) * 2 + y
            arrived(g, slot, plane(g), 0)
            pl.when(z < 3)(lambda: copy(g, 1 + 2 * j, full.at[slot], slot, plane(g), 0, up).start())
            pl.when(straight(g))(lambda: copy(g, 8 + j, full.at[slot], slot, plane(g), 0, y_side).start())
            copy(g, 11 + j, full.at[slot], slot, lone(g, x), 1, x_side).start()

        def above():
            slot = (z + j) * 2 + y
            arrived(g, slot, plane(g), 0)
            pl.when(z > 0)(lambda: copy(g, 2 + 2 * j, full.at[slot], slot, plane(g), 0, down).start())
            pl.when(straight(g))(lambda: copy(g, 14 + j, full.at[slot], slot, plane(g), 0, y_side).start())
            copy(g, 17 + j, full.at[slot], slot, lone(g, x), 1, x_side).start()

        pl.when(z >= j)(below)
        pl.when(z + j <= 3)(above)

    def along_y(g, j, above):
        zz = z + j if above else z - j
        slot = zz * 2 + 1 - y
        arrived(g, slot, plane(g), 0)

        @pl.when(turned(g))
        def _():
            if j == 0 or not above:
                kind = 25 if j == 0 else 8 + j
                pl.when(z < 3)(lambda: copy(g, kind, full.at[slot], slot, plane(g), 0, up).start())
            if j == 0 or above:
                kind = 26 if j == 0 else 14 + j
                pl.when(z > 0)(lambda: copy(g, kind, full.at[slot], slot, plane(g), 0, down).start())

        copy(g, 21 + zz, full.at[slot], slot, lone(g, x), 1, x_side).start()

    def service(i):
        def on(g, act):
            pl.when(jnp.logical_and(g >= 0, g < G_STAGES))(lambda: act(g))

        on(i, issue)
        for j in (1, 2, 3):
            on(i - j, lambda g: along_z(g, j))
        on(i - 1, lambda g: along_y(g, 0, False))
        for j in (1, 2, 3):
            @pl.when(z >= j)
            def _():
                on(i - j - 1, lambda g: along_y(g, j, False))

            @pl.when(z + j <= 3)
            def _():
                on(i - j - 1, lambda g: along_y(g, j, True))

    def lone_in(first, last):
        @pl.loop(first, last)
        def _(g):
            for k in range(1, 8):
                arrived(g, lax.rem(t + k, 8), lone(g, 1 - x), 1)

    def mod_row(image, k):
        return mod[pl.ds(image * 8 + k, 1), :]

    def by_rows(act):
        for image in range(2):
            @pl.loop(0, PATCH // CHUNK)
            def _(i):
                act(image, rows_at(image * PATCH + i * CHUNK, CHUNK))

    service(0)

    cond_in[...] = jnp.zeros_like(cond_in)
    cond_in[:, :144] = condition[...]
    cond_in[:, 144:145] = columns(wide(labels[...]))[:16, :1]
    mod_in[...] = jnp.zeros_like(mod_in)
    for p in range(8):
        for k, row in enumerate((6, 7, 14)):
            mod_in[p, row : row + 1, :144] = wide(bias_w[k : k + 1, :])
    load_gu.wait()
    load_down.wait()
    kept = [pltpu.make_async_copy(own, full.at[t], ls.at[0])]
    kept[0].start()
    fetch[2].wait()
    service(1)
    v = condition[...]
    act = low(v * (1.0 / (1.0 + jnp.exp(-v))))
    for k in range(6):
        share = nn(act, ada_w[k])
        for image in range(16):
            mod_in[image // 2, image % 2 * 8 + k : image % 2 * 8 + k + 1, :] = share[image : image + 1]
    mod_send[...] = low(mod_in[...])
    small = []
    for k, p in enumerate(peers):
        small.append(remote(mod_send.at[p], mod_all.at[t], ms.at[k], mr.at[t], (d, p)))
    for k, g in enumerate(groups):
        small.append(remote(cond_in, cond_out.at[d], cs.at[k], cr.at[d], (g, t)))
    for cp in small:
        cp.start()
    kept += [
        pltpu.make_async_copy(mod_send.at[t], mod_all.at[t], ls.at[1]),
        pltpu.make_async_copy(cond_in, cond_out.at[d], ls.at[2]),
    ]
    kept[1].start()
    kept[2].start()
    service(2)
    fetch[3].wait()
    fetch[4].wait()
    service(3)
    for p in peers:
        remote(mod_send.at[p], mod_all.at[p], ms.at[0], mr.at[p], (d, p)).wait_recv()
    kept[1].wait()
    for image in range(2):
        total = jnp.concatenate([wide(ada_b[...]), jnp.zeros((2, D), jnp.float32)], axis=0)
        for s in range(8):
            total = total + wide(mod_all[s])[image * 8 : image * 8 + 8]
        real = jnp.where(t * 2 + image < counts[0], 1.0, 0.0)
        row = lax.broadcasted_iota(jnp.int32, (8, D), 0)
        gate = jnp.logical_or(row == 2, row == 5)
        mod[image * 8 : image * 8 + 8, :] = jnp.where(gate, total * real, total)
    service(4)

    def first_rows(image, rows):
        v = wide(tokens[rows, :])
        n = v * lax.rsqrt(jnp.mean(v * v, axis=-1, keepdims=True) + epsilon)
        fi[0, rows, :] = low(n * (1.0 + mod_row(image, 1)) + mod_row(image, 0))

    def feed_rows(image, rows):
        fg[0, rows, :] = low(wide(out_grad[rows, :]) * mod_row(image, 5))

    by_rows(first_rows)
    share_fi = remote(fi.at[0], fi.at[1], es.at[0], er.at[0], core)
    share_fi.start()
    service(5)
    by_rows(feed_rows)
    share_fg = remote(fg.at[0], fg.at[1], es.at[1], er.at[1], core)
    share_fg.start()

    @pl.loop(6, A_STAGES + 4)
    def _(i):
        service(i)

    kept[0].wait()
    lone_in(0, A_STAGES)
    share_fi.wait_recv()
    share_fg.wait_recv()
    saves = [
        pltpu.make_async_copy(fi, fi_out, save.at[0]),
        pltpu.make_async_copy(fg, fg_out, save.at[1]),
        pltpu.make_async_copy(mod, mod_out, save.at[2]),
    ]
    for cp in saves:
        cp.start()

    def load_a(s):
        return pltpu.make_async_copy(full.at[s, pl.ds(0, QKV_ROWS)], wa.at[lax.rem(s, 2)], ws.at[lax.rem(s, 2)])

    load_o = pltpu.make_async_copy(full.at[:, pl.ds(O_FIRST, HEAD)], ow, ls.at[3])
    load_o.start()
    load_a(0).start()
    gain_cols = columns(wide(gains[...]))

    def save_head(s):
        b = lax.rem(s, 2)
        return [
            pltpu.make_async_copy(qkv.at[b], qkv_out.at[s], qs.at[b, 0]),
            pltpu.make_async_copy(norm.at[b], norm_out.at[s], qs.at[b, 1]),
            pltpu.make_async_copy(stat.at[b], stat_out.at[s], qs.at[b, 2]),
        ]

    @pl.loop(0, 8)
    def _(s):
        b = lax.rem(s, 2)
        load_a(s).wait()
        pl.when(s < 7)(lambda: load_a(s + 1).start())

        @pl.when(s > 1)
        def _():
            for cp in save_head(s - 2):
                cp.wait()

        bias_rows = wide(mod_all[s, :, :256])
        bias_rows = jnp.concatenate([bias_rows[6:8, :144], bias_rows[14:15, :144]], axis=0)
        bias = columns(jnp.where(c == 0, bias_rows[:, :HD], bias_rows[:, HD:]))
        cos, sin = table[:HD, :], table[HD:, :]
        for h in range(2):
            raw = nt(wa[b], fi[h])
            for i in range(2):
                v = raw[i * HD : (i + 1) * HD] + bias[:HD, i : i + 1]
                inv = lax.rsqrt(jnp.sum(v * v, axis=0, keepdims=True) * (1.0 / HD) + epsilon)
                n = v * inv
                norm[b, h, i * HEAD : (i + 1) * HEAD, :] = low(fill(n))
                stat[b, h, i : i + 1, :] = inv
                qkv[b, h, i * HEAD : (i + 1) * HEAD, :] = low(fill(turn(n * gain_cols[:HD, i : i + 1], cos, sin)))
            v = low(fill(raw[2 * HD : 3 * HD] + bias[:HD, 2:3]))
            qkv[b, h, 2 * HEAD :, :] = v
            for image in range(2):
                cut = slice(image * PATCH, (image + 1) * PATCH)
                e = jnp.exp(tn(qkv[b, h, HEAD : 2 * HEAD, cut], qkv[b, h, :HEAD, cut]) * FACTOR)
                row_sum = jnp.sum(e, axis=0, keepdims=True)
                stat[b, h, 2:3, cut] = jnp.log(row_sum)
                p = low(e * (1.0 / row_sum))
                m = nn(v[:, cut], p)
                m = jnp.concatenate([m[HD:], m[:HD]], axis=0)
                mixed[h, pl.ds(pl.multiple_of(s * HEAD, 16), HEAD), cut] = low(m)
        for cp in save_head(s):
            cp.start()

        pl.when(jnp.logical_or(s == 0, lax.rem(s, 2) == 1))(lambda: service(A_STAGES + 4 + (s + 1) // 2))

    for s in (6, 7):
        for cp in save_head(s):
            cp.wait()
    load_o.wait()
    saves.append(pltpu.make_async_copy(mixed, mixed_out, save.at[3]))
    saves[-1].start()

    for image in range(2):
        cut = slice(image * PATCH, (image + 1) * PATCH)
        att_send[cut, :] = low(tn(mixed[1, :, cut], ow[...].reshape(8 * HEAD, D)))
    share_att = remote(att_send, att_recv, es.at[2], er.at[2], core)
    share_att.start()
    for image in range(2):
        cut = slice(image * PATCH, (image + 1) * PATCH)
        att[cut, :] = tn(mixed[0, :, cut], ow[...].reshape(8 * HEAD, D))
    service(A_STAGES + 9)
    share_att.wait_recv()

    def second_rows(image, rows):
        a = att[rows, :] + wide(att_recv[rows, :])
        att[rows, :] = a
        v = wide(tokens[rows, :]) + mod_row(image, 2) * a
        n = v * lax.rsqrt(jnp.mean(v * v, axis=-1, keepdims=True) + epsilon)
        si[0, rows, :] = low(n * (1.0 + mod_row(image, 4)) + mod_row(image, 3))

    by_rows(second_rows)
    share_si = remote(si.at[0], si.at[1], es.at[3], er.at[3], core)
    share_si.start()
    service(A_STAGES + 10)

    share_si.wait_recv()
    saves += [
        pltpu.make_async_copy(att, att_out, save.at[4]),
        pltpu.make_async_copy(si, si_out, save.at[5]),
    ]
    saves[-2].start()
    saves[-1].start()

    def load_b(half, p):
        b = lax.rem(p, 2)
        return pltpu.make_async_copy(
            full.at[pl.ds(p * 2, 2), pl.ds(B_FIRST + half * SHARD_FF, SHARD_FF)], wb.at[b], ws.at[2 + b])

    def save_pair(half, p):
        b = lax.rem(p, 2)
        both = pl.ds(p * 2, 2)
        return [
            pltpu.make_async_copy(gu.at[b], gu_out.at[both, half], hs.at[b, 0]),
            pltpu.make_async_copy(hid.at[b], hid_out.at[both, half], hs.at[b, 1]),
            pltpu.make_async_copy(dd.at[b], dd_out.at[both, half], hs.at[b, 2]),
        ]

    for half in range(2):
        lone_in(A_STAGES + half * (HALF_STAGES - A_STAGES), HALF_STAGES + half * (HALF_STAGES - A_STAGES))
        load_b(half, 0).start()

        @pl.loop(0, 4)
        def _(p):
            b = lax.rem(p, 2)
            load_b(half, p).wait()
            pl.when(p < 3)(lambda: load_b(half, p + 1).start())

            @pl.when(p > 1)
            def _():
                for cp in save_pair(half, p - 2):
                    cp.wait()

            for h in range(2):
                both = nt(wb[b].reshape(2 * SHARD_FF, D), si[h])
                for i in range(2):
                    g = both[i * SHARD_FF : i * SHARD_FF + HALF_FF]
                    u = both[i * SHARD_FF + HALF_FF : (i + 1) * SHARD_FF]
                    hid[b, i, h] = low(g * (1.0 / (1.0 + jnp.exp(-g))) * u)
                    gu[b, i, h] = low(both[i * SHARD_FF : (i + 1) * SHARD_FF])
            grad = sum(
                nn(jnp.concatenate([hid[b, 0, h], hid[b, 1, h]], axis=0), fg[h]) for h in range(2))
            dd[b] = low(grad).reshape(2, HALF_FF, D)
            for cp in save_pair(half, p):
                cp.start()

            if half == 0:
                pl.when(lax.rem(p, 2) == 1)(lambda: service(A_STAGES + 11 + p // 2))
            else:
                pl.when(p < 3)(lambda: service(A_STAGES + 13 + p))

        for p in (2, 3):
            for cp in save_pair(half, p):
                cp.wait()

    lone_in(AB_STAGES, G_STAGES)

    @pl.loop(0, G_STAGES)
    def _(g):
        def sent(kind, rows):
            copy(g, kind, own, t, rows, 0, x_side).wait_send()

        sent(2, plane(g))
        pl.when(z < 3)(lambda: sent(0, plane(g)))
        pl.when(z > 0)(lambda: sent(1, plane(g)))
        for k in range(4):
            sent(21 + k, lone(g, x))
        pl.when(jnp.logical_and(turned(g), z < 3))(lambda: sent(25, plane(g)))
        pl.when(jnp.logical_and(turned(g), z > 0))(lambda: sent(26, plane(g)))
        for j in (1, 2, 3):
            @pl.when(z >= j)
            def _():
                pl.when(z < 3)(lambda: sent(1 + 2 * j, plane(g)))
                pl.when(jnp.logical_or(straight(g), z < 3))(lambda: sent(8 + j, plane(g)))
                sent(11 + j, lone(g, x))

            @pl.when(z + j <= 3)
            def _():
                pl.when(z > 0)(lambda: sent(2 + 2 * j, plane(g)))
                pl.when(jnp.logical_or(straight(g), z > 0))(lambda: sent(14 + j, plane(g)))
                sent(17 + j, lone(g, x))

    for cp in small + [share_fi, share_fg, share_att, share_si]:
        cp.wait_send()
    for g in groups:
        remote(cond_in, cond_out.at[g], cs.at[0], cr.at[g], (g, t)).wait_recv()
    kept[2].wait()
    for cp in saves:
        cp.wait()


def forward(counts, qkv_w, out_w, gu_w, down_w, condition, labels, ada_w, ada_b, bias_w, tokens, out_grad, gains, table):
    dma = pltpu.SemaphoreType.DMA
    vm = pltpu.VMEM
    bf, f32 = jnp.bfloat16, jnp.float32
    anywhere = pl.BlockSpec(memory_space=pl.ANY)
    inside = pl.BlockSpec(memory_space=pltpu.VMEM)
    scalar = pl.BlockSpec(memory_space=pltpu.SMEM)
    R = tokens.shape[0]
    outs = [
        ((8, ROWS_ALL, D), bf), ((4, 16, 256), f32), ((16, D), f32),
        ((2, R, D), bf), ((2, R, D), bf), ((2, R, D), bf), ((R, D), f32),
        ((8, 2, 3 * HEAD, R), bf), ((8, 2, 2 * HEAD, R), bf), ((8, 2, 8, R), f32), ((2, 8 * HEAD, R), bf),
        ((8, 2, 2, SHARD_FF, R), bf), ((8, 2, 2, HALF_FF, R), bf), ((8, 2, HALF_FF, D), bf),
    ]
    return pl.pallas_call(
        forward_kernel,
        out_shape=tuple(jax.ShapeDtypeStruct(s, e) for s, e in outs),
        in_specs=[scalar] + [anywhere] * 4 + [inside] * 2 + [anywhere] + [inside] * 2 + [anywhere] * 2 + [inside] * 2,
        out_specs=(anywhere,) * len(outs),
        scratch_shapes=[
            vm((3, 144, D), bf), vm((144, D), bf), vm((6, 144, D), bf), vm((R, D), bf), vm((R, D), bf),
            vm((ROWS_ALL, D), bf), vm((8, 16, D), f32), vm((8, 16, D), bf), vm((16, 256), f32), vm((8, 16, D), bf),
            vm((16, D), f32),
            vm((2, R, D), bf), vm((2, R, D), bf), vm((2, R, D), bf), vm((R, D), f32), vm((R, D), bf), vm((R, D), bf),
            vm((2, QKV_ROWS, D), bf), vm((8, HEAD, D), bf), vm((2, 8 * HEAD, R), bf),
            vm((2, 2, 3 * HEAD, R), bf), vm((2, 2, 2 * HEAD, R), bf), vm((2, 2, 8, R), f32),
            vm((2, 2, SHARD_FF, D), bf), vm((2, 2, 2, SHARD_FF, R), bf), vm((2, 2, 2, HALF_FF, R), bf),
            vm((2, 2, HALF_FF, D), bf),
            dma((G_STAGES, 27)), dma((G_STAGES, 8, 2)), dma((7,)), dma((8,)), dma((3,)), dma((4,)),
            dma((4,)), dma((4,)), dma((6,)), dma((2, 3)), dma((2, 3)), dma((6,)), dma((6,)), dma((5,)),
        ],
        compiler_params=pltpu.CompilerParams(
            collective_id=0, has_side_effects=True, vmem_limit_bytes=60 * 2**20),
        name="forward",
    )(counts, qkv_w, out_w, gu_w, down_w, condition, labels, ada_w, ada_b, bias_w, tokens, out_grad, gains, table)


def backward_kernel(
    full, fi_in, si_in, fg_in, att_in, qkv_in, norm_in, stat_in, mixed_in, gu_in, hid_in, dd_in,
    counts, tokens_hbm, out_grad_hbm, ada_hbm, mod, gains, table, cond,
    result_out, tokens_out, grads, pay_all, sums_out, scale_out, bias_out, cond_out, class_out,
    tokens, out_grad, ada_w, cond_all, part, xin, yin, zin, fin, buf_a, buf_b, acc, after, att, sent, came, came_feed, result,
    wd, wb, wa, hid, gu, qkv, norm, stat, mixed, dqkv, dlow, gain_sum, payf, pay,
    xs, xr, ys, yr, zs, zr, fs, fr, es, er, ps, pr, ls, lw, x_free, y_free, z_free,
):
    x, c, z, y = place()
    t = z * 2 + y
    d = x * 2 + c
    y_side, x_side, core = at(x, c, z, 1 - y), at(1 - x, c, z, y), at(x, 1 - c, z, y)
    up, down = at(x, c, z + 1, y), at(x, c, z - 1, y)
    mates = [at(x, c, lax.rem(z + k, 4), y) for k in (1, 2, 3)] + [x_side, y_side]

    loads = [
        pltpu.make_async_copy(fg_in, buf_a, ls.at[0]),
        pltpu.make_async_copy(si_in, buf_b, ls.at[1]),
        pltpu.make_async_copy(att_in, att, ls.at[2]),
        pltpu.make_async_copy(tokens_hbm, tokens, ls.at[7]),
        pltpu.make_async_copy(out_grad_hbm, out_grad, ls.at[8]),
        pltpu.make_async_copy(ada_hbm, ada_w, ls.at[9]),
    ]
    load_dd = pltpu.make_async_copy(
        dd_in, part.at[:, :, pl.ds(C_FIRST, C_ROWS)], ls.at[6])
    load_dd.start()
    greet(mates + [core])
    for cp in loads:
        cp.start()

    def first_of(g):
        return ROWS_ALL - (g + 1) * R_STAGE

    def rows_of(g):
        return rows_at(first_of(g), R_STAGE)

    def side_y(side):
        return 1 - y if side == 0 else y

    def lone_z(g, yy):
        return jnp.where(yy == lax.rem(x + g, 2), 1, 2)

    def xcopy(g, side):
        yy = side_y(side)
        return remote(
            part.at[3 - lone_z(g, yy), yy, rows_of(g)], xin.at[lax.rem(g, X_RING), side],
            xs.at[g, side], xr.at[g, side], x_side)

    def ycopy(g, k):
        yy = 1 - y
        zz = (0, 3, lone_z(g, yy))[k]
        return remote(part.at[zz, yy, rows_of(g)], yin.at[lax.rem(g, Y_RING), k], ys.at[g, k], yr.at[g, k], y_side)

    def zcopy(g, way, k):
        zz = (3 - 3 * way) if k == 0 else lone_z(g, y)
        return remote(
            part.at[zz, y, rows_of(g)], zin.at[lax.rem(g, Z_RING), way * 2 + k],
            zs.at[g, way * 2 + k], zr.at[g, way * 2 + k], up if way == 0 else down)

    def plane_sum(g):
        return remote(part.at[z, y, rows_of(g)], fin.at[rows_of(g)], fs.at[g, 0], fr.at[g, 0], x_side)

    def finished(g):
        return remote(part.at[z, y, rows_of(g)], grads.at[c, rows_of(g)], fs.at[g, 0], fr.at[g, 0], x_side)

    def core_copy(g, here):
        src = part.at[z, y, rows_of(g)] if here else grads.at[c, rows_of(g)]
        return remote(src, grads.at[c, rows_of(g)], fs.at[g, 1], fr.at[g, 1], core)

    def own_copy(g):
        return pltpu.make_async_copy(part.at[z, y, rows_of(g)], grads.at[c, rows_of(g)], fs.at[g, 2])

    def add(zz, yy, g, piece):
        first = first_of(g)

        @pl.loop(0, R_STAGE // 16)
        def _(i):
            a = rows_at(first + i * 16, 16)
            part[zz, yy, a, :] = low(wide(part[zz, yy, a, :]) + wide(piece(rows_at(i * 16, 16))))

    def send(g, side):
        if side == 0:
            pl.when(g >= X_RING)(lambda: pl.semaphore_wait(x_free, 1))
            pl.when(g >= Y_RING)(lambda: pl.semaphore_wait(y_free, 1))
        xcopy(g, side).start()
        if side == 0:
            ycopy(g, 0).start()
            ycopy(g, 1).start()

    def x_stage(g):
        b = lax.rem(g, X_RING)
        for side in (0, 1):
            yy = side_y(side)
            xcopy(g, side).wait_recv()
            add(lone_z(g, yy), yy, g, lambda r: xin[b, side, r, :])
            if side == 0:
                ycopy(g, 2).start()
        pl.when(g + X_RING < R_STAGES)(
            lambda: pl.semaphore_signal(x_free, inc=1, device_id=x_side, device_id_type=MESH))

    def y_stage(g):
        b = lax.rem(g, Y_RING)
        for k in range(3):
            ycopy(g, k).wait_recv()
            add((0, 3, lone_z(g, y))[k], y, g, lambda r: yin[b, k, r, :])
        pl.when(g + Y_RING < R_STAGES)(
            lambda: pl.semaphore_signal(y_free, inc=1, device_id=y_side, device_id_type=MESH))

    def take(g, way, k):
        zcopy(g, way, k).wait_recv()
        zz = (3 - 3 * way) if k == 0 else lone_z(g, y)
        add(zz, y, g, lambda r: zin[lax.rem(g, Z_RING), way * 2 + k, r, :])

    def z_stage(g, way):
        further = z < 3 if way == 0 else z > 0
        first = z == 0 if way == 0 else z == 3

        @pl.when(further)
        def _():
            pl.when(g >= Z_RING)(lambda: pl.semaphore_wait(z_free.at[way], 1))
            pl.when(jnp.logical_not(first))(lambda: take(g, way, 0))
            zcopy(g, way, 0).start()

        lone = lone_z(g, y)

        @pl.when(z < lone if way == 0 else z > lone)
        def _():
            pl.when(jnp.logical_not(first))(lambda: take(g, way, 1))
            zcopy(g, way, 1).start()

    def own_stage(g):
        pl.when(z == 3)(lambda: take(g, 0, 0))
        pl.when(z == 0)(lambda: take(g, 1, 0))

        @pl.when(z == lone_z(g, y))
        def _():
            take(g, 0, 1)
            take(g, 1, 1)
            finished(g).start()

        pl.when(jnp.logical_or(z == 0, z == 3))(lambda: plane_sum(g).start())

        @pl.when(g + Z_RING < R_STAGES)
        def _():
            pl.when(z > 0)(
                lambda: pl.semaphore_signal(z_free.at[0], inc=1, device_id=down, device_id_type=MESH))
            pl.when(z < 3)(
                lambda: pl.semaphore_signal(z_free.at[1], inc=1, device_id=up, device_id_type=MESH))

    def f_stage(g):
        ends = jnp.logical_or(z == 0, z == 3)
        here = z == lone_z(g, y)

        @pl.when(ends)
        def _():
            plane_sum(g).wait()
            add(z, y, g, lambda r: fin[rows_at(first_of(g) + r.start, 16), :])

        @pl.when(jnp.logical_or(ends, here))
        def _():
            own_copy(g).start()
            core_copy(g, True).start()

        @pl.when(z == 3 - lone_z(g, y))
        def _():
            finished(g).wait_recv()
            core_copy(g, False).start()

    def service(i, ready):
        def on(g, act):
            pl.when(jnp.logical_and(g >= 0, g < R_STAGES))(lambda: act(g))

        on(i, x_stage)
        on(i - 1, y_stage)
        on(i - 1 - z, lambda g: z_stage(g, 0))
        on(i - 4 + z, lambda g: z_stage(g, 1))
        on(i - 4, own_stage)
        on(i - 5, f_stage)

        @pl.when(i + AHEAD < ready)
        def _():
            send(i + AHEAD, 0)
            send(i + AHEAD, 1)

    def send_stages(first, last):
        @pl.loop(first, last)
        def _(g):
            send(g, 0)
            send(g, 1)

    def shard(k):
        return lax.rem(k, 4), jnp.where(k < 4, 1 - y, y)

    def slot(k):
        zz, yy = shard(k)
        return zz * 2 + yy

    def stream(pairs):
        def fetch(k):
            b = lax.rem(k, 2)
            return [pltpu.make_async_copy(src(slot(k)), buf.at[b], lw.at[n, b]) for src, buf, n in pairs]

        def begin(k):
            for cp in fetch(k):
                cp.start()

        def turn_to(k):
            for cp in fetch(k):
                cp.wait()
            pl.when(k < 7)(lambda: begin(k + 1))

        return begin, turn_to

    def mod_row(image, k):
        return mod[pl.ds(image * 8 + k, 1), :]

    def by_rows(act):
        for image in range(2):
            @pl.loop(0, PATCH // CHUNK)
            def _(i):
                act(image, rows_at(image * PATCH + i * CHUNK, CHUNK))

    def count(image, k, v):
        payf[pl.ds(image * 8 + k, 1), :] += jnp.sum(v, axis=0, keepdims=True)

    def clear(ref):
        @pl.loop(0, ref.shape[0] // 16)
        def _(i):
            ref[rows_at(i * 16, 16), :] = jnp.zeros((16, D), jnp.float32)

    def gather_sum(h, left, right):
        for image in range(2):
            cut = slice(image * PATCH, (image + 1) * PATCH)
            rows = slice(h * 512 + image * PATCH, h * 512 + (image + 1) * PATCH)
            acc[rows, :] += tn(left[:, cut], right)

    def share_half(number, landing):
        @pl.loop(0, 512 // CHUNK)
        def _(i):
            sent[rows_at(i * CHUNK, CHUNK), :] = low(acc[rows_at(512 + i * CHUNK, CHUNK), :])

        cp = remote(sent, landing, es.at[number], er.at[number], core)
        cp.start()
        return cp

    load_dd.wait()
    send_stages(0, AHEAD)
    payf[...] = jnp.zeros_like(payf)
    gain_sum[...] = jnp.zeros_like(gain_sum)
    clear(acc)
    begin_g, turn_g = stream([
        (lambda s: full.at[s, pl.ds(C_FIRST, C_ROWS)], wd, 1),
        (lambda s: full.at[s, pl.ds(B_FIRST, B_ROWS)], wb, 2),
        (lambda s: gu_in.at[s], gu, 3),
    ])
    begin_a, turn_a = stream([
        (lambda s: full.at[s, pl.ds(0, A_ROWS)], wa, 4),
        (lambda s: qkv_in.at[s], qkv, 5),
        (lambda s: norm_in.at[s], norm, 6),
        (lambda s: stat_in.at[s], stat, 7),
        (lambda s: mixed_in.at[:, rows_at(s * HEAD, HEAD)], mixed, 8),
    ])
    begin_f, turn_f = stream([
        (lambda s: hid_in.at[s], hid, 0),
        (lambda s: full.at[s, pl.ds(C_FIRST, C_ROWS)], wd, 1),
    ])
    begin_g(0)
    loads[0].wait()
    loads[1].wait()

    @pl.loop(0, 8)
    def _(k):
        b = lax.rem(k, 2)
        zz, yy = shard(k)
        turn_g(k)
        grads_here = []
        for h in range(2):
            hg = nt(wd[b], buf_a[h])
            both = []
            for half in range(2):
                g, u = wide(gu[b, half, h, :HALF_FF]), wide(gu[b, half, h, HALF_FF:])
                sig = 1.0 / (1.0 + jnp.exp(-g))
                act = g * sig
                this = hg[half * HALF_FF : (half + 1) * HALF_FF]
                both += [low(this * u * (sig + act * (1.0 - sig))), low(this * act)]
            both = jnp.concatenate(both, axis=0)
            grads_here.append(both)
            gather_sum(h, both, wb[b])
        part[zz, yy, B_FIRST:C_FIRST, :] = low(nn(grads_here[0], buf_b[0]) + nn(grads_here[1], buf_b[1]))

        pl.when(lax.rem(k, 2) == 1)(lambda: service(k // 2, D_STAGES))

    load_fi = pltpu.make_async_copy(fi_in, buf_a, ls.at[0])
    load_fi.start()
    share_second = share_half(0, came)
    send_stages(D_STAGES, D_STAGES + AHEAD)
    begin_a(0)
    service(D_STAGES, GU_STAGES)
    for cp in loads[2:]:
        cp.wait()
    share_second.wait_recv()

    def after_rows(image, rows):
        a = att[rows, :]
        v = wide(tokens[rows, :]) + mod_row(image, 2) * a
        inv = lax.rsqrt(jnp.mean(v * v, axis=-1, keepdims=True) + epsilon)
        n = v * inv
        sg = acc[rows, :] + wide(came[rows, :])
        dn = sg * (1.0 + mod_row(image, 4))
        ag = wide(out_grad[rows, :]) + inv * (dn - n * jnp.mean(dn * n, axis=-1, keepdims=True))
        after[rows, :] = ag
        buf_b[0, rows, :] = low(ag * mod_row(image, 2))
        count(image, 2, ag * a)
        count(image, 3, sg)
        count(image, 4, sg * n)

    by_rows(after_rows)
    share_ag = remote(buf_b.at[0], buf_b.at[1], es.at[1], er.at[1], core)
    share_ag.start()
    service(D_STAGES + 1, GU_STAGES)
    clear(acc)
    load_fi.wait()
    share_ag.wait_recv()

    gain_cols = columns(wide(gains[...]))

    @pl.loop(0, 8)
    def _(k):
        b = lax.rem(k, 2)
        zz, yy = shard(k)
        turn_a(k)
        cos, sin = table[:HD, :PATCH], table[HD:, :PATCH]
        out_part = nn(mixed[b, 0], buf_b[0]) + nn(mixed[b, 1], buf_b[1])
        for h in range(2):
            mg_all = nt(wa[b, O_FIRST:], buf_b[h])
            mg_all = low(fill(mg_all[HEAD - HD :]))
            dqkv[h, 3 * HD :, :] = jnp.zeros((QKV_ROWS - 3 * HD, 512), jnp.float32)
            for image in range(2):
                cut = slice(image * PATCH, (image + 1) * PATCH)
                q, kk, v = [qkv[b, h, i * HEAD : (i + 1) * HEAD, cut] for i in range(3)]
                mg = mg_all[:, cut]
                p = jnp.exp(tn(kk, q) * FACTOR - stat[b, h, 2:3, cut])
                dqkv[h, 2 * HD : 3 * HD, cut] = nt(mg, low(p))[:HD]
                pg = tn(v, mg)
                sg = low(p * (pg - jnp.sum(p * pg, axis=0, keepdims=True)))
                backs = (nn(kk, sg), nt(q, sg))
                for i in range(2):
                    rows = slice(i * HD, (i + 1) * HD)
                    back = turn(backs[i][:HD] * FACTOR, cos, -sin)
                    n = wide(norm[b, h, i * HEAD : (i + 1) * HEAD, cut])[:HD]
                    gain_sum[rows, :] += back * n
                    dn = back * gain_cols[:HD, i : i + 1]
                    mean = jnp.sum(dn * n, axis=0, keepdims=True) * (1.0 / HD)
                    dqkv[h, rows, cut] = stat[b, h, i : i + 1, cut] * (dn - n * mean)
            dlow[h] = low(dqkv[h])
            gather_sum(h, dlow[h], wa[b, :QKV_ROWS])
        qkv_part = nn(dlow[0], buf_a[0]) + nn(dlow[1], buf_a[1])
        part[zz, yy, :A_ROWS, :] = low(jnp.concatenate([qkv_part[:QKV], out_part[HEAD - HD :]], axis=0))
        ones = jnp.ones((8, 512), jnp.bfloat16)
        sums = nt(ones, dlow[0]) + nt(ones, dlow[1])
        s = slot(k)
        payf[pl.ds(6 + s // 4, 1), pl.ds(pl.multiple_of(lax.rem(s, 4) * 256, 128), QKV)] = sums[:1, :QKV]

        pl.when(lax.rem(k, 3) != 0)(lambda: service(D_STAGES + 1 + k - k // 3, GU_STAGES))

    send_stages(GU_STAGES, GU_STAGES - 1 + AHEAD)
    share_second.wait_send()
    begin_f(0)
    share_first = share_half(2, came)
    service(GU_STAGES - 1, R_STAGES)
    share_first.wait_recv()

    def first_rows(image, rows):
        v = wide(tokens[rows, :])
        inv = lax.rsqrt(jnp.mean(v * v, axis=-1, keepdims=True) + epsilon)
        n = v * inv
        fgd = acc[rows, :] + wide(came[rows, :])
        dn = fgd * (1.0 + mod_row(image, 1))
        count(image, 0, fgd)
        count(image, 1, fgd * n)
        acc[rows, :] = after[rows, :] + inv * (dn - n * jnp.mean(dn * n, axis=-1, keepdims=True))

    by_rows(first_rows)
    save_tokens = pltpu.make_async_copy(acc.at[pl.ds(0, 512)], tokens_out, ls.at[3])
    save_tokens.start()
    service(GU_STAGES, R_STAGES)
    save_tokens.wait()
    clear(acc)

    @pl.loop(0, 8)
    def _(k):
        b = lax.rem(k, 2)
        turn_f(k)
        for h in range(2):
            gather_sum(h, jnp.concatenate([hid[b, 0, h], hid[b, 1, h]], axis=0), wd[b])

    share_first.wait_send()
    share_feed = share_half(3, came_feed)
    service(GU_STAGES + 1, R_STAGES)
    share_feed.wait_recv()

    def result_rows(image, rows):
        feed = acc[rows, :] + wide(came_feed[rows, :])
        v = wide(tokens[rows, :]) + mod_row(image, 2) * att[rows, :]
        result[rows, :] = low(v + mod_row(image, 5) * feed)
        count(image, 5, wide(out_grad[rows, :]) * feed)

    by_rows(result_rows)
    save_result = pltpu.make_async_copy(result, result_out, ls.at[4])
    save_result.start()
    lanes = gain_sum[:, :128] + gain_sum[:, 128:]
    lanes = jnp.concatenate([lanes, jnp.zeros((256 - 2 * HD, 128), jnp.float32)], axis=0)
    payf[14:15, :256] = jnp.sum(jnp.transpose(lanes), axis=0, keepdims=True)
    for image in range(2):
        real = jnp.where(t * 2 + image < counts[0], 1.0, 0.0)
        for k in (2, 5):
            row = slice(image * 8 + k, image * 8 + k + 1)
            payf[row, :] = payf[row, :] * real
    pay[...] = low(payf[...])
    keep_pay = pltpu.make_async_copy(pay, pay_all.at[x, c, z, y], ls.at[5])
    keep_pay.start()
    pay_x = remote(pay, pay_all.at[x, c, z, y], ps.at[0], pr.at[0], x_side)
    pay_x.start()
    service(GU_STAGES + 2, R_STAGES)
    keep_pay.wait()
    pay_x.wait_recv()
    line = pay_all.at[:, c, z, y]
    pay_y = remote(line, line, ps.at[1], pr.at[1], y_side)
    pay_y.start()
    service(GU_STAGES + 3, R_STAGES)
    pay_y.wait_recv()
    square = pay_all.at[:, c, z]
    pays = [remote(square, square, ps.at[1 + k], pr.at[1 + k], at(x, c, lax.rem(z + k, 4), y)) for k in (1, 2, 3)]
    for cp in pays:
        cp.start()

    @pl.loop(GU_STAGES + 4, GU_STAGES + 6)
    def _(i):
        service(i, R_STAGES)

    for cp in pays:
        cp.wait()
    layer = pay_all.at[:, c]
    swap = remote(layer, layer, ps.at[5], pr.at[5], core)
    swap.start()

    service(GU_STAGES + 6, R_STAGES)
    share_feed.wait_send()
    swap.wait()
    load_pay = pltpu.make_async_copy(pay_all.reshape(32 * PAY, D), sent, ls.at[5])
    load_pay.start()
    service(GU_STAGES + 7, R_STAGES)
    load_pay.wait()

    def picked(count, which):
        row = lax.broadcasted_iota(jnp.int32, (count, 32 * PAY), 0)
        col = lax.broadcasted_iota(jnp.int32, (count, 32 * PAY), 1)
        return nn(jnp.where(which(row, col), 1.0, 0.0).astype(jnp.bfloat16), sent[...])

    act = jnp.zeros((64, 144), jnp.float32)
    for k in range(6):
        mg = picked(64, lambda row, col: col == row * 8 + k)
        sums_out[k : k + 1, :] = jnp.sum(mg, axis=0, keepdims=True)
        act = act + nt(low(mg), ada_w[k])
    payf[:8, :] = picked(8, lambda row, col: jnp.logical_or(
        jnp.logical_and(row == 0, lax.rem(col, PAY) == 14),
        jnp.logical_and(row == 1 + lax.rem(col // (8 * PAY), 2), lax.rem(col, PAY) == 6 + t // 4)))
    found = payf[:8, :256]
    scale_out[0:1, :] = found[:1, :HD]
    scale_out[1:2, :] = found[:1, HD : 2 * HD]
    found = payf[:8, pl.ds(pl.multiple_of(lax.rem(t, 4) * 256, 128), 256)]
    for k in range(3):
        cut = slice(k * HD, (k + 1) * HD)
        bias_out[k : k + 1, :] = jnp.concatenate([found[1:2, cut], found[2:3, cut]], axis=1)
    for group in range(4):
        cond_all[group * 16 : (group + 1) * 16, :] = cond[group]
    v = cond_all[:, :144]
    sig = 1.0 / (1.0 + jnp.exp(-v))
    cond_all[:, :144] = act * sig * (1.0 + v * (1.0 - sig))
    cond_out[...] = cond_all[rows_at(d * 16, 16), :144]
    rest = cond_all[:, :144]
    classes = lax.broadcasted_iota(jnp.int32, (64, class_out.shape[1]), 1)
    chosen = jnp.where(classes == cond_all[:, 144:145].astype(jnp.int32), 1.0, 0.0).astype(jnp.bfloat16)
    total = jnp.zeros(class_out.shape, jnp.float32)
    for _ in range(3):
        piece = low(rest)
        rest = rest - wide(piece)
        total = total + tn(piece, chosen)
    class_out[...] = total

    @pl.loop(GU_STAGES + 8, R_STAGES + 5)
    def _(i):
        service(i, R_STAGES)

    @pl.loop(0, R_STAGES)
    def _(g):
        for side in (0, 1):
            xcopy(g, side).wait_send()
        for k in range(3):
            ycopy(g, k).wait_send()
        lone = lone_z(g, y)
        pl.when(z < 3)(lambda: zcopy(g, 0, 0).wait_send())
        pl.when(z > 0)(lambda: zcopy(g, 1, 0).wait_send())
        pl.when(z < lone)(lambda: zcopy(g, 0, 1).wait_send())
        pl.when(z > lone)(lambda: zcopy(g, 1, 1).wait_send())
        pl.when(z == lone)(lambda: finished(g).wait_send())
        pl.when(z != 3 - lone)(lambda: own_copy(g).wait())
        core_copy(g, True).wait()

    pay_x.wait_send()
    pay_y.wait_send()
    share_ag.wait_send()
    save_result.wait()


def backward(saved, counts, tokens, out_grad, ada_w, mod, gains, table, cond, classes):
    dma = pltpu.SemaphoreType.DMA
    regular = pltpu.SemaphoreType.REGULAR
    vm = pltpu.VMEM
    bf, f32 = jnp.bfloat16, jnp.float32
    anywhere = pl.BlockSpec(memory_space=pl.ANY)
    inside = pl.BlockSpec(memory_space=pltpu.VMEM)
    R = tokens.shape[0]
    outs = [((R, D), bf), ((R, D), f32), ((2, ROWS_ALL, D), bf), ((2, 2, 4, 2, PAY, D), bf)]
    small = [((6, D), f32), ((2, HD), f32), ((3, 2 * HD), f32), ((16, 144), f32), ((144, classes), f32)]
    return pl.pallas_call(
        backward_kernel,
        out_shape=tuple(jax.ShapeDtypeStruct(s, e) for s, e in outs + small),
        in_specs=[anywhere] * len(saved) + [pl.BlockSpec(memory_space=pltpu.SMEM)] + [anywhere] * 3 + [inside] * 4,
        out_specs=(anywhere,) * len(outs) + (inside,) * len(small),
        scratch_shapes=[
            vm((R, D), bf), vm((R, D), bf), vm((6, 144, D), bf), vm((64, 256), f32), vm((4, 2, ROWS_ALL, D), bf), vm((X_RING, 2, R_STAGE, D), bf), vm((Y_RING, 3, R_STAGE, D), bf),
            vm((Z_RING, 4, R_STAGE, D), bf), vm((ROWS_ALL, D), bf),
            vm((2, R, D), bf), vm((2, R, D), bf), vm((2 * R, D), f32), vm((R, D), f32), vm((R, D), f32),
            vm((R, D), bf), vm((R, D), bf), vm((R, D), bf), vm((R, D), bf),
            vm((2, C_ROWS, D), bf), vm((2, B_ROWS, D), bf), vm((2, A_ROWS, D), bf),
            vm((2, 2, 2, HALF_FF, R), bf), vm((2, 2, 2, SHARD_FF, R), bf), vm((2, 2, 3 * HEAD, R), bf),
            vm((2, 2, 2 * HEAD, R), bf), vm((2, 2, 8, R), f32), vm((2, 2, HEAD, R), bf),
            vm((2, QKV_ROWS, R), f32), vm((2, QKV_ROWS, R), bf), vm((2 * HD, PATCH), f32), vm((16, D), f32),
            vm((16, D), bf),
            dma((R_STAGES, 2)), dma((R_STAGES, 2)), dma((R_STAGES, 3)), dma((R_STAGES, 3)),
            dma((R_STAGES, 4)), dma((R_STAGES, 4)), dma((R_STAGES, 3)), dma((R_STAGES, 2)),
            dma((4,)), dma((4,)), dma((6,)), dma((6,)), dma((10,)), dma((9, 2)),
            regular, regular, regular((2,)),
        ],
        compiler_params=pltpu.CompilerParams(
            collective_id=1, has_side_effects=True, vmem_limit_bytes=62 * 2**20),
        name="backward",
    )(*saved, counts, tokens, out_grad, ada_w, mod, gains, table, cond)


def normalize(vectors, axis=-1, count=None):
    count = count or vectors.shape[axis]
    inverse = lax.rsqrt(jnp.sum(vectors * vectors, axis=axis, keepdims=True) / count + epsilon)
    return (vectors * inverse, inverse)


def normalize_back(grad, normed, inverse, axis=-1, count=None):
    count = count or grad.shape[axis]
    return inverse * (grad - normed * (jnp.sum(grad * normed, axis=axis, keepdims=True) / count))


def silu_slope(values):
    sigma = jax.nn.sigmoid(values)
    return sigma * (1.0 + values * (1.0 - sigma))


def pair_tables(count):
    pairs = HD // 4
    theta = np.exp(-math.log(100.0) * np.arange(pairs, dtype=np.float32) / pairs)
    spot = np.arange(count) % PATCH
    a, b = theta[:, None] * (spot // GRID)[None], theta[:, None] * (spot % GRID)[None]
    cos = np.concatenate([np.cos(a), np.cos(a), np.cos(b), np.cos(b)])
    sin = np.concatenate([-np.sin(a), np.sin(a), -np.sin(b), np.sin(b)])
    return np.concatenate([cos, sin]).astype(np.float32)


def unpack_grads(both):
    qkv = both[:, :QKV].reshape(2, 3, HD, D).swapaxes(0, 1).reshape(3, 2 * HD, D)
    o = both[:, QKV:A_ROWS].reshape(2 * HD, D)
    gu = both[:, B_FIRST:C_FIRST].reshape(2, 2, 2, HALF_FF, D)
    gu = lax.optimization_barrier(gu.transpose(4, 2, 0, 1, 3).reshape(D, 2, 2 * SHARD_FF))
    dn = both[:, C_FIRST:].reshape(2 * SHARD_FF, D)
    return [wide(v) for v in (qkv.transpose(2, 0, 1), o, gu, dn)]


def fast(
    tokens, labels, timesteps, image_counts, class_table, ada_weight, ada_bias,
    qkv_weight, qkv_bias, qk_scale, out_weight, gate_up_weight, down_weight, out_grad,
):
    dot = lambda s, a, b: jnp.einsum(s, a, b, preferred_element_type=jnp.float32)
    t = lax.axis_index("tensor")
    c = lax.axis_index("dp") % 2
    images = labels.shape[0]
    columns_here = class_table.shape[1]
    column = t * columns_here + jnp.arange(columns_here)
    half_width = D // 2
    frequency = jnp.exp(-math.log(10000.0) * (column % half_width).astype(jnp.float32) / half_width)
    angles = timesteps.astype(jnp.float32)[:, None] * frequency[None, :]
    time_embed = jnp.where(column[None, :] < half_width, jnp.cos(angles), jnp.sin(angles))
    classes = jnp.arange(class_table.shape[0])
    condition = dot("in,nc->ic", low(labels[:, None] == classes[None, :]), class_table) + time_embed
    gu = lax.dynamic_slice_in_dim(gate_up_weight, c * SHARD_FF, SHARD_FF, 2)
    gu = gu.reshape(D, 2, 2, HALF_FF).transpose(2, 1, 3, 0).reshape(B_ROWS, D)
    table = pair_tables(tokens.shape[0])
    (weights, cond_all, mod, first_in, second_in, feed_grad, attention, qkv_t, norm_t, stat_t, mixed, gu_t, hidden,
     down_part) = forward(
        image_counts, qkv_weight.transpose(1, 2, 0), out_weight, gu, down_weight, condition, labels[None, :],
        ada_weight.transpose(1, 0, 2), ada_bias, qkv_bias, tokens, out_grad, qk_scale, table)
    saved = (weights, first_in, second_in, feed_grad, attention, qkv_t, norm_t, stat_t, mixed, gu_t, hidden,
             down_part.reshape(4, 2, C_ROWS, D))
    (result, tokens_grad, summed, pay_all, ada_bias_grad, qk_scale_grad, qkv_bias_grad, cond_grad,
     table_grad) = backward(
        saved, image_counts, tokens, out_grad, ada_weight.transpose(1, 0, 2), mod, qk_scale, table, cond_all,
        class_table.shape[0])
    qkv_weight_grad, out_weight_grad, gate_up_grad, down_grad = unpack_grads(summed)
    mod_grad = pay_all.reshape(-1, 8, D)[:, :6]
    cond_act = low(jax.nn.silu(cond_all.reshape(4 * images, -1)[:, :columns_here]))
    ada_weight_grad = dot("ic,ikd->ckd", cond_act, mod_grad)
    table_grad = table_grad.T
    return (
        result, tokens_grad, cond_grad, table_grad, ada_weight_grad, ada_bias_grad,
        qkv_weight_grad, qkv_bias_grad, qk_scale_grad, out_weight_grad, gate_up_grad, down_grad,
    )


def rope_tables(count):
    pairs = HD // 4
    theta = jnp.exp(-math.log(100.0) * jnp.arange(pairs, dtype=jnp.float32) / pairs)
    place = jnp.arange(count) % PATCH
    row_angle = (place // GRID).astype(jnp.float32)[:, None] * theta
    col_angle = (place % GRID).astype(jnp.float32)[:, None] * theta
    return ((jnp.cos(row_angle), jnp.sin(row_angle)), (jnp.cos(col_angle), jnp.sin(col_angle)))


def rotate_part(segment, cosine, sine, direction):
    half_len = segment.shape[-1] // 2
    first, second = (segment[..., :half_len], segment[..., half_len:])
    cosine = cosine[:, None, :]
    sine = direction * sine[:, None, :]
    return jnp.concatenate(
        [first * cosine - second * sine, second * cosine + first * sine], axis=-1
    )


def rotate(vectors, tables, direction):
    half_len = vectors.shape[-1] // 2
    return jnp.concatenate(
        [
            rotate_part(vectors[..., :half_len], tables[0][0], tables[0][1], direction),
            rotate_part(vectors[..., half_len:], tables[1][0], tables[1][1], direction),
        ],
        axis=-1,
    )


def general(
    tokens,
    labels,
    timesteps,
    image_counts,
    class_table,
    ada_weight,
    ada_bias,
    qkv_weight,
    qkv_bias,
    qk_scale,
    out_weight,
    gate_up_weight,
    down_weight,
    out_grad,
):
    width = tokens.shape[1]
    local_rows = tokens.shape[0]
    members = lax.axis_size("tensor")
    place = lax.axis_index("tensor")
    images = labels.shape[0]
    all_rows = local_rows * members
    columns_here = class_table.shape[1]
    heads_here = columns_here // HD
    column = place * columns_here + jnp.arange(columns_here)
    half_width = width // 2
    frequency = jnp.exp(-math.log(10000.0) * (column % half_width).astype(jnp.float32) / half_width)
    angles = timesteps.astype(jnp.float32)[:, None] * frequency[None, :]
    time_embed = jnp.where(column[None, :] < half_width, jnp.cos(angles), jnp.sin(angles))
    chosen = (labels[:, None] == jnp.arange(class_table.shape[0])[None, :]).astype(jnp.bfloat16)
    condition = jnp.dot(chosen, class_table, preferred_element_type=jnp.float32) + time_embed
    cond_act = jax.nn.silu(condition).astype(jnp.bfloat16)
    mod_part = jnp.einsum("ic,ckd->ikd", cond_act, ada_weight, preferred_element_type=jnp.float32)
    modulation = lax.psum(mod_part, "tensor") + ada_bias.astype(jnp.float32)
    row_index = place * local_rows + jnp.arange(local_rows)
    row_image = row_index // PATCH
    selector = (row_image[:, None] == jnp.arange(images)[None, :]).astype(jnp.float32)
    mod_rows = jnp.dot(selector, modulation.reshape(images, 6 * width), precision=HIGH).reshape(
        local_rows, 6, width
    )
    kept = (row_image < image_counts[0]).astype(jnp.float32)[:, None]
    shift_one, scale_one, gate_one, shift_two, scale_two, gate_two = [
        mod_rows[:, index] for index in range(6)
    ]
    tokens_f = tokens.astype(jnp.float32)
    first_norm, first_inverse = normalize(tokens_f)
    first_in = (first_norm * (1.0 + scale_one) + shift_one).astype(jnp.bfloat16)
    first_all = lax.all_gather(first_in, "tensor", axis=0, tiled=True)
    qkv = jnp.einsum(
        "nd,dkc->nkc", first_all, qkv_weight, preferred_element_type=jnp.float32
    ) + qkv_bias.astype(jnp.float32)
    head_view = qkv.reshape(all_rows, 3, heads_here, HD)
    tables = rope_tables(all_rows)
    qk_gains = qk_scale.astype(jnp.float32)
    query_normed, query_inverse = normalize(head_view[:, 0])
    key_normed, key_inverse = normalize(head_view[:, 1])
    block_shape = (all_rows // PATCH, PATCH, heads_here, HD)
    queries = (
        rotate(query_normed * qk_gains[0], tables, 1.0).astype(jnp.bfloat16).reshape(block_shape)
    )
    keys_rot = (
        rotate(key_normed * qk_gains[1], tables, 1.0).astype(jnp.bfloat16).reshape(block_shape)
    )
    values = head_view[:, 2].astype(jnp.bfloat16).reshape(block_shape)
    factor = HD ** (-0.5)
    scores = (
        jnp.einsum("iqhe,ikhe->ihqk", queries, keys_rot, preferred_element_type=jnp.float32)
        * factor
    )
    row_max = jnp.max(scores, axis=-1, keepdims=True)
    exponent = jnp.exp(scores - row_max)
    totals = jnp.sum(exponent, axis=-1, keepdims=True)
    logsum = row_max + jnp.log(totals)
    probability = (exponent / totals).astype(jnp.bfloat16)
    mixed_heads = (
        jnp.einsum("ihqk,ikhe->iqhe", probability, values, preferred_element_type=jnp.float32)
        .reshape(all_rows, columns_here)
        .astype(jnp.bfloat16)
    )
    attention = lax.psum_scatter(
        jnp.dot(mixed_heads, out_weight, preferred_element_type=jnp.float32).astype(jnp.bfloat16),
        "tensor",
        scatter_dimension=0,
        tiled=True,
    ).astype(jnp.float32)
    after_attn = tokens_f + kept * gate_one * attention
    second_norm, second_inverse = normalize(after_attn)
    second_in = (second_norm * (1.0 + scale_two) + shift_two).astype(jnp.bfloat16)
    second_all = lax.all_gather(second_in, "tensor", axis=0, tiled=True)
    gate_up = jnp.einsum(
        "nd,dkf->nkf", second_all, gate_up_weight, preferred_element_type=jnp.float32
    )
    gate_value, up_value = (gate_up[:, 0], gate_up[:, 1])
    activated = jax.nn.silu(gate_value)
    hidden = (activated * up_value).astype(jnp.bfloat16)
    feed = lax.psum_scatter(
        jnp.dot(hidden, down_weight, preferred_element_type=jnp.float32).astype(jnp.bfloat16),
        "tensor",
        scatter_dimension=0,
        tiled=True,
    ).astype(jnp.float32)
    result = (after_attn + kept * gate_two * feed).astype(jnp.bfloat16)
    grad_out = out_grad.astype(jnp.float32)
    feed_grad = (grad_out * kept * gate_two).astype(jnp.bfloat16)
    gate_two_grad = grad_out * kept * feed
    feed_grad_all = lax.all_gather(feed_grad, "tensor", axis=0, tiled=True)
    hidden_grad = jnp.einsum(
        "nd,fd->nf", feed_grad_all, down_weight, preferred_element_type=jnp.float32
    )
    down_grad = jnp.einsum("nf,nd->fd", hidden, feed_grad_all, preferred_element_type=jnp.float32)
    gate_grad = hidden_grad * up_value * silu_slope(gate_value)
    up_grad = hidden_grad * activated
    gu_grad = jnp.stack([gate_grad, up_grad], axis=1).astype(jnp.bfloat16)
    gate_up_grad = jnp.einsum(
        "nd,nkf->dkf", second_all, gu_grad, preferred_element_type=jnp.float32
    )
    second_grad = lax.psum_scatter(
        jnp.einsum(
            "nkf,dkf->nd", gu_grad, gate_up_weight, preferred_element_type=jnp.float32
        ).astype(jnp.bfloat16),
        "tensor",
        scatter_dimension=0,
        tiled=True,
    ).astype(jnp.float32)
    after_grad = grad_out + normalize_back(
        second_grad * (1.0 + scale_two), second_norm, second_inverse
    )
    attention_grad = (after_grad * kept * gate_one).astype(jnp.bfloat16)
    gate_one_grad = after_grad * kept * attention
    attention_grad_all = lax.all_gather(attention_grad, "tensor", axis=0, tiled=True)
    mixed_grad = jnp.einsum(
        "nd,cd->nc", attention_grad_all, out_weight, preferred_element_type=jnp.float32
    ).astype(jnp.bfloat16)
    out_weight_grad = jnp.einsum(
        "nc,nd->cd", mixed_heads, attention_grad_all, preferred_element_type=jnp.float32
    )
    scores_again = (
        jnp.einsum("iqhe,ikhe->ihqk", queries, keys_rot, preferred_element_type=jnp.float32)
        * factor
    )
    prob_again = jnp.exp(scores_again - logsum)
    mixed_blocks = mixed_grad.reshape(block_shape)
    values_grad = jnp.einsum(
        "ihqk,iqhe->ikhe",
        prob_again.astype(jnp.bfloat16),
        mixed_blocks,
        preferred_element_type=jnp.float32,
    )
    prob_grad = jnp.einsum(
        "iqhe,ikhe->ihqk", mixed_blocks, values, preferred_element_type=jnp.float32
    )
    score_grad = (
        prob_again * (prob_grad - jnp.sum(prob_again * prob_grad, axis=-1, keepdims=True))
    ).astype(jnp.bfloat16)
    queries_grad = (
        jnp.einsum("ihqk,ikhe->iqhe", score_grad, keys_rot, preferred_element_type=jnp.float32)
        * factor
    )
    keys_grad = (
        jnp.einsum("ihqk,iqhe->ikhe", score_grad, queries, preferred_element_type=jnp.float32)
        * factor
    )
    query_back = rotate(queries_grad.reshape(all_rows, heads_here, HD), tables, -1.0)
    key_back = rotate(keys_grad.reshape(all_rows, heads_here, HD), tables, -1.0)
    scale_part = jnp.stack(
        [
            jnp.sum(query_back * query_normed, axis=(0, 1)),
            jnp.sum(key_back * key_normed, axis=(0, 1)),
        ]
    )
    query_raw = normalize_back(query_back * qk_gains[0], query_normed, query_inverse)
    key_raw = normalize_back(key_back * qk_gains[1], key_normed, key_inverse)
    qkv_grad = (
        jnp.stack([query_raw, key_raw, values_grad.reshape(all_rows, heads_here, HD)], axis=1)
        .reshape(all_rows, 3, columns_here)
        .astype(jnp.bfloat16)
    )
    qkv_weight_grad = jnp.einsum(
        "nd,nkc->dkc", first_all, qkv_grad, preferred_element_type=jnp.float32
    )
    qkv_bias_grad = jnp.sum(qkv_grad.astype(jnp.float32), axis=0)
    first_grad = lax.psum_scatter(
        jnp.einsum("nkc,dkc->nd", qkv_grad, qkv_weight, preferred_element_type=jnp.float32).astype(
            jnp.bfloat16
        ),
        "tensor",
        scatter_dimension=0,
        tiled=True,
    ).astype(jnp.float32)
    tokens_grad = after_grad + normalize_back(
        first_grad * (1.0 + scale_one), first_norm, first_inverse
    )
    row_mod_grad = jnp.stack(
        [
            first_grad,
            first_grad * first_norm,
            gate_one_grad,
            second_grad,
            second_grad * second_norm,
            gate_two_grad,
        ],
        axis=1,
    ).reshape(local_rows, 6 * width)
    mod_grad_part = jnp.dot(selector.T, row_mod_grad, precision=HIGH).reshape(images, 6, width)
    mod_grad, scale_grad = (
        lax.psum(mod_grad_part.astype(jnp.bfloat16), "tensor").astype(jnp.float32),
        lax.psum(scale_part.astype(jnp.bfloat16), "tensor").astype(jnp.float32),
    )
    mod_grad_low = mod_grad.astype(jnp.bfloat16)
    ada_weight_grad = jnp.einsum(
        "ic,ikd->ckd", cond_act, mod_grad_low, preferred_element_type=jnp.float32
    )
    ada_bias_grad = jnp.sum(mod_grad_low.astype(jnp.float32), axis=0)
    act_grad = jnp.einsum(
        "ikd,ckd->ic", mod_grad_low, ada_weight, preferred_element_type=jnp.float32
    )
    cond_grad = act_grad * silu_slope(condition)
    table_grad = jnp.dot(chosen.astype(jnp.float32).T, cond_grad, precision=HIGH)
    summed = (
        lax.psum(table_grad.astype(jnp.bfloat16), "dp").astype(jnp.float32),
        lax.psum(ada_weight_grad.astype(jnp.bfloat16), "dp").astype(jnp.float32),
        lax.psum(ada_bias_grad.astype(jnp.bfloat16), "dp").astype(jnp.float32),
        lax.psum(qkv_weight_grad.astype(jnp.bfloat16), "dp").astype(jnp.float32),
        lax.psum(qkv_bias_grad.astype(jnp.bfloat16), "dp").astype(jnp.float32),
        lax.psum(scale_grad.astype(jnp.bfloat16), "dp").astype(jnp.float32),
        lax.psum(out_weight_grad.astype(jnp.bfloat16), "dp").astype(jnp.float32),
        lax.psum(gate_up_grad.astype(jnp.bfloat16), "dp").astype(jnp.float32),
        lax.psum(down_grad.astype(jnp.bfloat16), "dp").astype(jnp.float32),
    )
    return (result, tokens_grad, cond_grad) + tuple(summed)


def solution(mesh):
    placed = (
        P(("dp", "tensor"), None),
        P("dp"),
        P("dp"),
        P("dp"),
        P(None, "tensor"),
        P("tensor", None, None),
        P(),
        P(None, None, "tensor"),
        P(None, "tensor"),
        P(),
        P("tensor", None),
        P(None, None, "tensor"),
        P("tensor", None),
        P(("dp", "tensor"), None),
    )
    plain = mesh.shape["dp"] != 4 or mesh.shape["tensor"] != 8
    return jax.shard_map(
        general if plain else fast,
        mesh=mesh,
        in_specs=placed,
        out_specs=(
            P(("dp", "tensor"), None),
            P(("dp", "tensor"), None),
            P("dp", "tensor"),
            P(None, "tensor"),
            P("tensor", None, None),
            P(),
            P(None, None, "tensor"),
            P(None, "tensor"),
            P(),
            P("tensor", None),
            P(None, None, "tensor"),
            P("tensor", None),
        ),
        check_vma=False,
    )
```
